32 devices in a mesh: row: 2 (over y), col: 8 (over z, x), leaf: 2 (over core).
Axes of the slice: x: 2, y: 2, z: 4, core: 2. Of those that a mesh axis runs over, the one named last changes fastest.
Arguments:
- front: float32 [4096, 8192], P('row', ('col', 'leaf')), may hold values from -6 to 6
- child: float32 [4096, 8192], P(('row', 'col', 'leaf')), may hold values from -6 to 6
- row_map: int32 [2, 8], P('row'), may hold values from 0 to 7, each once within a row
- col_map: int32 [32], replicated, may hold values from 0 to 31, each once
- x_fac: float32 [16, 16384], P('row', ('col', 'leaf')), may hold values from -0.75 to 0.75
- w_fac: float32 [16, 16384], P('row', ('col', 'leaf')), may hold values from -0.375 to 0.375
- v_fac: float32 [32, 16384], P(('col', 'leaf'), 'row'), may hold values from -6 to 6
- z_fac: float32 [32, 16384], P(('col', 'leaf'), 'row'), may hold values from -0.75 to 0.75
- dinv: float32 [256, 256], replicated, may hold values from -0.375 to 0.375
- pivots: int32 [256], replicated, may hold values from 0 to 255, each once
- rank_rows: int32 [16], P('row'), may hold values from 16 to 64
- rank_cols: int32 [32], P(('col', 'leaf')), may hold values from 16 to 64
- admissible: int32 [16, 32], P('row', ('col', 'leaf')), may hold values 0 or 1
Outputs:
- updated: float32 [4096, 8192], P('row', ('col', 'leaf'))
The draws below stay inside these ranges and needn't reach their ends.
Inputs may be any that keep to these rules, and one draw needn't show every extreme that they name: Each row of row_map orders the 8 tile rows of one group; col_map orders all 32 tile columns. `pivots`: A permutation of the panel's columns.
All inputs are finite; a program needn't handle non-finite values. No bound on the sum of `admissible` on one device may be relied on, other than what follows from the above.
Results may differ from the reference program's by a relative error of at most 0.0003.
Values sent between devices are 32-bit elements; how exact they have to be, the bound alone decides.
No kernel may reach another device: no remote copies, remote signals or barrier semaphores. Data moves between devices by JAX's collectives and lax.ppermute only.
A program may use at most 128 MiB of HBM per device.

```python
import jax
import jax.numpy as jnp
from jax import lax

B = 256
RMAX = 64
RT = 8
NRT = 16
NCT = 32
MROWS = 4096
MCOLS = 8192
N_ROW = 2


def set_ends(entries, stream_key, least, high):
    extent = entries.shape
    spot = [jax.random.randint(jax.random.fold_in(stream_key, axis), (), 0, extent[axis]) for axis in range(len(extent))]
    entries = entries.at[tuple(spot)].set(least)
    longest = extent.index(max(extent))
    spot[longest] = (spot[longest] + 1) % extent[longest]
    return entries.at[tuple(spot)].set(high)


def block_scale(rng, shape, shards, least, high):
    def one(axis_at, blocks):
        draws = jax.random.uniform(jax.random.fold_in(jax.random.fold_in(rng, 6), axis_at), (blocks,), jnp.float32, least / len(shards), high / len(shards))
        return jnp.repeat(jnp.exp(draws), shape[axis_at] // blocks).reshape((-1,) + (1,) * (len(shape) - axis_at - 1))

    gain = one(*shards[0])
    for cut in shards[1:]:
        gain = gain * one(*cut)
    return gain


def noise(stream_key, dims, scale, most, shards=(), kind=jnp.bfloat16):
    level = block_scale(stream_key, dims, shards, -0.22, 0.18) if shards else 1.0
    array = jax.random.normal(stream_key, dims, jnp.float32) * scale * level
    return jnp.minimum(jnp.maximum(array, -most), most).astype(kind)


def setup_inputs(seed: int = 0) -> dict:
    seeds = jax.random.split(jax.random.key(seed), 14)
    return {
        "front": noise(seeds[0], (MROWS, MCOLS), 1.0, 6.0, ((0, 2), (1, 16)), jnp.float32),
        "child": noise(seeds[1], (MROWS, MCOLS), 1.0, 6.0, ((0, 32),), jnp.float32),
        "row_map": jax.vmap(lambda own: jax.random.permutation(own, RT))(jax.random.split(seeds[2], N_ROW)).reshape((N_ROW, RT)).astype(jnp.int32),
        "col_map": jax.random.permutation(seeds[3], NCT).astype(jnp.int32),
        "x_fac": noise(seeds[4], (NRT, RMAX * B), RMAX ** -0.5, 0.75, ((0, 2), (1, 16)), jnp.float32),
        "w_fac": noise(seeds[5], (NRT, RMAX * B), B ** -0.5, 0.375, ((0, 2), (1, 16)), jnp.float32),
        "v_fac": noise(seeds[6], (NCT, RMAX * B), 1.0, 6.0, ((0, 16), (1, 2)), jnp.float32),
        "z_fac": noise(seeds[7], (NCT, RMAX * B), RMAX ** -0.5, 0.75, ((0, 16), (1, 2)), jnp.float32),
        "dinv": noise(seeds[8], (B, B), B ** -0.5, 0.375, (), jnp.float32),
        "pivots": jax.random.permutation(seeds[9], B).astype(jnp.int32),
        "rank_rows": set_ends(jax.random.randint(seeds[10], (NRT,), RMAX // 4, RMAX + 1), jax.random.fold_in(seeds[10], 1), RMAX // 4, RMAX).astype(jnp.int32),
        "rank_cols": set_ends(jax.random.randint(seeds[11], (NCT,), RMAX // 4, RMAX + 1), jax.random.fold_in(seeds[11], 1), RMAX // 4, RMAX).astype(jnp.int32),
        "admissible": set_ends((jax.random.randint(seeds[12], (NRT, NCT), 0, 2) < 1).astype(jnp.int32), jax.random.fold_in(seeds[12], 1), 0, 1),
    }


def inverse_order(order):
    count = order.shape[0]
    return jnp.zeros((count,), jnp.int32).at[order].set(jnp.arange(count, dtype=jnp.int32))


def reference(front, child, row_map, col_map, x_fac, w_fac, v_fac, z_fac, dinv, pivots, rank_rows, rank_cols, admissible):
    highest = lax.Precision.HIGHEST
    tile = dinv.shape[0]
    nrt = x_fac.shape[0]
    nct = v_fac.shape[0]
    rank_max = x_fac.shape[1] // tile
    x_three = x_fac.reshape(nrt, rank_max, tile)
    w_three = w_fac.reshape(nrt, rank_max, tile)
    v_three = v_fac.reshape(nct, rank_max, tile)
    z_three = z_fac.reshape(nct, rank_max, tile)
    groups = row_map.shape[0]
    per_group = row_map.shape[1]
    dest_rows = (jnp.arange(groups, dtype=jnp.int32)[:, None] * per_group + row_map).reshape(-1)
    blocks = child.reshape(nrt, tile, nct, tile)
    blocks = jnp.take(blocks, inverse_order(dest_rows), axis=0)
    blocks = jnp.take(blocks, inverse_order(col_map), axis=2)
    relaid = blocks.reshape(nrt * tile, nct * tile)
    dv = jnp.einsum('kb,jrb->jkr', dinv, v_three, precision=highest)
    permuted = jnp.take(w_three, pivots, axis=2)
    rank_index = jnp.arange(rank_max, dtype=jnp.int32)

    def one_row(items):
        x_row, w_row, rank_row, adm_row = items
        core = jnp.einsum('rk,jks->jrs', w_row, dv, precision=highest)
        dense_tile = (adm_row == 0)[:, None]
        keep_rows = (rank_index[None, :] < rank_row) | dense_tile
        keep_cols = (rank_index[None, :] < rank_cols[:, None]) | dense_tile
        core = jnp.where(keep_rows[:, :, None] & keep_cols[:, None, :], core, jnp.float32(0.0))
        left = jnp.einsum('rb,jrs->jbs', x_row, core, precision=highest)
        product = jnp.einsum('jbs,jsc->bjc', left, z_three, precision=highest)
        return product.reshape(tile, nct * tile)

    update = lax.map(one_row, (x_three, permuted, rank_rows, admissible)).reshape(nrt * tile, nct * tile)
    return front + relaid - update
```

```python
import functools

import jax
import jax.numpy as jnp
import numpy as np
from jax import lax
from jax.experimental import pallas as pl
from jax.experimental.pallas import tpu as pltpu
from jax.sharding import PartitionSpec as P

RMAX = 64
LANES = 128
GROUP = ("col", "leaf")
HIGHEST = lax.Precision.HIGHEST
MIB = 1 << 20


def place_kernel(tiles, tile, col_map, child, placed, held, in_sem, out_sem):
    def fetch(b):
        return pltpu.make_async_copy(child.at[:, pl.ds(b * tile, tile)], held.at[b], in_sem.at[b])

    def store(b):
        return pltpu.make_async_copy(held.at[b], placed.at[col_map[b]], out_sem.at[b])

    for b in range(tiles):
        fetch(b).start()
    for b in range(tiles):
        fetch(b).wait()
        store(b).start()
    for b in range(tiles):
        store(b).wait()


def place(child, col_map, tile):
    rows = child.shape[0]
    tiles = col_map.shape[0]
    return pl.pallas_call(
        functools.partial(place_kernel, tiles, tile),
        out_shape=jax.ShapeDtypeStruct((tiles, rows, tile), child.dtype),
        in_specs=[pl.BlockSpec(memory_space=pltpu.SMEM), pl.BlockSpec(memory_space=pl.ANY)],
        out_specs=pl.BlockSpec(memory_space=pl.ANY),
        scratch_shapes=[
            pltpu.VMEM((tiles, rows, tile), child.dtype),
            pltpu.SemaphoreType.DMA((tiles,)),
            pltpu.SemaphoreType.DMA((tiles,)),
        ],
        compiler_params=pltpu.CompilerParams(vmem_limit_bytes=16 * MIB),
        cost_estimate=pl.CostEstimate(flops=0, bytes_accessed=2 * child.size * 4, transcendentals=0),
        name="place_child",
    )(col_map, child)


def dot(a, b, contract=((1,), (0,))):
    return lax.dot_general(a, b, (contract, ((), ())), precision=HIGHEST, preferred_element_type=jnp.float32)


def update_kernel(
    parts, halves, per, row_tiles, col_tiles, tile,
    front, dinv, pivots, keep, *rest,
):
    xw = rest[:parts]
    vz = rest[parts : parts + halves]
    out, xs, ts, vs, zs = rest[parts + halves :]
    step = pl.program_id(0)
    chunk = vz[0].shape[1] // tile
    slots = xw[0].shape[0]
    rows = slots * row_tiles

    @pl.when(step == 0)
    def _():
        hot = (lax.broadcasted_iota(jnp.int32, (tile, tile), 0) == pivots[...]).astype(jnp.float32)
        turned = dot(hot, dinv[...])
        zs[...] = jnp.zeros_like(zs)
        for h in range(halves):
            for j in range(col_tiles):
                for p in range(chunk):
                    r = j * RMAX + h * chunk + p
                    span = pl.ds(p * tile, tile)
                    vs[pl.ds(r, 1), :] = vz[h][pl.ds(j, 1), span]
                    zs[pl.ds(r, 1), pl.ds(j * tile, tile)] = vz[h][pl.ds(col_tiles + j, 1), span]
        dv = dot(turned, vs[...], ((1,), (1,)))
        for q in range(per):
            span = pl.ds(q * tile, tile)
            for n in range(parts):
                at = pl.ds((q * parts + n) * rows, rows)
                left = xw[n][:, :row_tiles, span].reshape(rows, tile)
                for g in range(tile // LANES):
                    xs[g, at, :] = left[:, g * LANES : (g + 1) * LANES]
                core = dot(xw[n][:, row_tiles:, span].reshape(rows, tile), dv)
                kept = jnp.where(keep[at, :] > 0, core, 0.0)
                right = dot(kept, zs[...])
                for g in range(right.shape[1] // LANES):
                    ts[g, at, :] = right[:, g * LANES : (g + 1) * LANES]

    mine = pl.ds(step, RMAX, stride=row_tiles)
    left = jnp.concatenate([xs[g, mine, :] for g in range(xs.shape[0])], axis=1)
    right = jnp.concatenate([ts[g, mine, :] for g in range(ts.shape[0])], axis=1)
    out[...] = front[...] - dot(left, right, ((0,), (0,)))


def subtract_update(front, dinv, pivots, keep, xw, vz):
    tile = dinv.shape[0]
    row_tiles = front.shape[0] // tile
    width = front.shape[1]
    col_tiles = width // tile
    per = xw[0].shape[2] // tile
    total = RMAX * row_tiles

    def whole(array):
        return pl.BlockSpec(array.shape, lambda i: (0,) * array.ndim)

    block = pl.BlockSpec((tile, width), lambda i: (i, 0))
    pivots = pivots.reshape(1, tile)
    return pl.pallas_call(
        functools.partial(update_kernel, len(xw), len(vz), per, row_tiles, col_tiles, tile),
        grid=(row_tiles,),
        out_shape=jax.ShapeDtypeStruct(front.shape, front.dtype),
        in_specs=[block, whole(dinv), whole(pivots), whole(keep)] + [whole(a) for a in xw] + [whole(a) for a in vz],
        out_specs=block,
        scratch_shapes=[
            pltpu.VMEM((tile // LANES, total, LANES), jnp.float32),
            pltpu.VMEM((width // LANES, total, LANES), jnp.float32),
            pltpu.VMEM((col_tiles * RMAX, tile), jnp.float32),
            pltpu.VMEM((col_tiles * RMAX, width), jnp.float32),
        ],
        compiler_params=pltpu.CompilerParams(vmem_limit_bytes=24 * MIB),
        cost_estimate=pl.CostEstimate(flops=2 * front.size * 256, bytes_accessed=2 * front.size * 4, transcendentals=0),
        name="front_less_update",
    )(front, dinv, pivots, keep, *xw, *vz)


def add_kernel(row_tiles, pieces, col_tiles, rows, tile, row_map, base, arrived, out, held, got, base_sem, got_sem, out_sem):
    def at(a):
        return pl.ds(row_map[0, a] * tile, tile)

    def fetch_base(a):
        return pltpu.make_async_copy(base.at[at(a), :], held.at[a], base_sem.at[a])

    def fetch_got(a):
        return pltpu.make_async_copy(arrived.at[pl.ds(a * pieces, pieces)], got.at[a], got_sem.at[a])

    def store(a):
        return pltpu.make_async_copy(held.at[a], out.at[at(a), :], out_sem.at[a])

    for a in range(row_tiles):
        fetch_base(a).start()
        fetch_got(a).start()
    for a in range(row_tiles):
        fetch_base(a).wait()
        fetch_got(a).wait()
        for p in range(pieces):
            for j in range(col_tiles):
                low, left = pl.ds(p * rows, rows), pl.ds(j * tile, tile)
                held[a, low, left] = held[a, low, left] + got[a, p, j]
        store(a).start()
    for a in range(row_tiles):
        store(a).wait()


def add_child(base, arrived, row_map, tile):
    row_tiles = base.shape[0] // tile
    count, col_tiles, rows, _ = arrived.shape
    pieces = count // row_tiles
    return pl.pallas_call(
        functools.partial(add_kernel, row_tiles, pieces, col_tiles, rows, tile),
        out_shape=jax.ShapeDtypeStruct(base.shape, base.dtype),
        in_specs=[
            pl.BlockSpec(memory_space=pltpu.SMEM),
            pl.BlockSpec(memory_space=pl.ANY),
            pl.BlockSpec(memory_space=pl.ANY),
        ],
        out_specs=pl.BlockSpec(memory_space=pl.ANY),
        scratch_shapes=[
            pltpu.VMEM((row_tiles, tile, base.shape[1]), base.dtype),
            pltpu.VMEM((row_tiles, pieces, col_tiles, rows, tile), base.dtype),
            pltpu.SemaphoreType.DMA((row_tiles,)),
            pltpu.SemaphoreType.DMA((row_tiles,)),
            pltpu.SemaphoreType.DMA((row_tiles,)),
        ],
        compiler_params=pltpu.CompilerParams(vmem_limit_bytes=24 * MIB),
        cost_estimate=pl.CostEstimate(flops=base.size, bytes_accessed=3 * base.size * 4, transcendentals=0),
        name="add_child",
    )(row_map, base, arrived)


def gather_group(array):
    cols, leaves = lax.axis_size("col"), lax.axis_size("leaf")
    near = 2
    far = cols // near

    def index(a, x, l):
        return (a % far * near + x % near) * leaves + l % leaves

    every = [(a, x, l) for a in range(far) for x in range(near) for l in range(leaves)]
    line = [array]
    for s in range(1, far):
        line.append(lax.ppermute(array, GROUP, [(index(a, x, l), index(a + s, x, l)) for a, x, l in every]))
    line = jnp.stack(line)
    hops = [(dx, dl) for dx in range(near) for dl in range(leaves)]
    parts = [line]
    for dx, dl in hops[1:]:
        parts.append(lax.ppermute(line, GROUP, [(index(a, x, l), index(a, x + dx, l + dl)) for a, x, l in every]))
    sources = [[[index(a - s, x - dx, l - dl) for s in range(far)] for dx, dl in hops] for a, x, l in every]
    return parts, np.array(sources, np.int32)


def own(table, axes):
    return lax.dynamic_slice_in_dim(jnp.asarray(table), lax.axis_index(axes), 1)


def gather_row(array):
    size = lax.axis_size("row")
    parts = [array]
    for s in range(1, size):
        parts.append(lax.ppermute(array, "row", [(y, (y + s) % size) for y in range(size)]))
    return parts, np.array([[(y - s) % size for s in range(size)] for y in range(size)], np.int32)


def on_device(
    front,
    child,
    row_map,
    col_map,
    x_fac,
    w_fac,
    v_fac,
    z_fac,
    dinv,
    pivots,
    rank_rows,
    rank_cols,
    admissible,
):
    tile = dinv.shape[0]
    row_tiles = front.shape[0] // tile
    col_tiles = front.shape[1] // tile
    local_rows = child.shape[0]
    devices = lax.axis_size("col") * lax.axis_size("leaf")
    per = x_fac.shape[1] // tile
    chunk = v_fac.shape[1] // tile

    vz, row_from = gather_row(jnp.concatenate([v_fac, z_fac], axis=0))
    xw, group_from = gather_group(jnp.concatenate([x_fac, w_fac], axis=0))

    placed = place(child, col_map, tile).reshape(devices, col_tiles, local_rows, tile)
    arrived = lax.all_to_all(placed, GROUP, split_axis=0, concat_axis=0, tiled=True)

    r = group_from[:, None] * per + np.arange(per, dtype=np.int32)[:, None, None]
    s = row_from[:, :, None] * chunk + np.arange(chunk, dtype=np.int32)
    keep_rows = own(r.reshape(-1, RMAX), GROUP).reshape(RMAX, 1) < rank_rows[None, :]
    keep_cols = own(s.reshape(-1, RMAX), "row") < rank_cols[:, None]
    dense = (admissible == 0)[None, :, :, None]
    keep = (keep_rows[:, :, None, None] & keep_cols[None, None]) | dense
    keep = keep.astype(jnp.float32).reshape(RMAX * row_tiles, col_tiles * RMAX)

    base = subtract_update(front, dinv, pivots, keep, xw, vz)
    return add_child(base, arrived, row_map, tile)


def solution(mesh):
    return jax.shard_map(
        on_device,
        mesh=mesh,
        in_specs=(
            P("row", GROUP),
            P(("row", "col", "leaf"), None),
            P("row", None),
            P(),
            P("row", GROUP),
            P("row", GROUP),
            P(GROUP, "row"),
            P(GROUP, "row"),
            P(),
            P(),
            P("row"),
            P(GROUP),
            P("row", GROUP),
        ),
        out_specs=P("row", GROUP),
        check_vma=False,
    )
```

```python
import functools

import jax
import jax.numpy as jnp
import numpy as np
from jax import lax
from jax.experimental import pallas as pl
from jax.experimental.pallas import tpu as pltpu
from jax.sharding import PartitionSpec as P

RMAX = 64
LANES = 128
NEAR = 4
GROUP = ("col", "leaf")
HIGHEST = lax.Precision.HIGHEST
MIB = 1 << 20


def group_index():
    return lax.axis_index("col") * lax.axis_size("leaf") + lax.axis_index("leaf")


def place_kernel(tiles, tile, col_tiles, col_map, child, *rest):
    pieces = rest[: tiles // col_tiles]
    inverse, sem = rest[tiles // col_tiles :]
    me = group_index()
    for b in range(tiles):
        inverse[col_map[b]] = b

    def copy(m, j):
        b = inverse[(me ^ m) * col_tiles + j]
        span = pl.ds(pl.multiple_of(b * tile, tile), tile)
        return pltpu.make_async_copy(child.at[:, span], pieces[m].at[j], sem.at[m, j])

    order = [(m, j) for m in reversed(range(len(pieces))) for j in range(col_tiles)]
    for m, j in order:
        copy(m, j).start()
    for m, j in order:
        copy(m, j).wait()


def in_hbm(array):
    return pltpu.with_memory_space_constraint(array, pltpu.HBM)


def place(child, col_map, tile, devices):
    rows = child.shape[0]
    tiles = col_map.shape[0]
    col_tiles = tiles // devices
    return pl.pallas_call(
        functools.partial(place_kernel, tiles, tile, col_tiles),
        out_shape=[jax.ShapeDtypeStruct((col_tiles, rows, tile), child.dtype)] * devices,
        in_specs=[pl.BlockSpec(memory_space=pltpu.SMEM), pl.BlockSpec(memory_space=pltpu.HBM)],
        out_specs=[pl.BlockSpec(memory_space=pl.ANY)] * devices,
        scratch_shapes=[pltpu.SMEM((tiles,), jnp.int32), pltpu.SemaphoreType.DMA((devices, col_tiles))],
        cost_estimate=pl.CostEstimate(flops=0, bytes_accessed=2 * child.size * 4, transcendentals=0),
        name="place_child",
    )(col_map, in_hbm(child))


def dot(a, b, contract=((1,), (0,))):
    return lax.dot_general(a, b, (contract, ((), ())), precision=HIGHEST, preferred_element_type=jnp.float32)


def update_kernel(
    parts, halves, per, row_tiles, col_tiles, tile,
    front, dinv, pivots, keep, *rest,
):
    xw = rest[:parts]
    vz = rest[parts : parts + halves]
    out, xs, ts, vs, zs = rest[parts + halves :]
    step = pl.program_id(0)
    chunk = vz[0].shape[1] // tile
    slots = xw[0].shape[0]
    rows = slots * row_tiles

    @pl.when(step == 0)
    def _():
        hot = (lax.broadcasted_iota(jnp.int32, (tile, tile), 0) == pivots[...]).astype(jnp.float32)
        turned = dot(hot, dinv[...])
        zs[...] = jnp.zeros_like(zs)
        for h in range(halves):
            for j in range(col_tiles):
                for p in range(chunk):
                    r = j * RMAX + h * chunk + p
                    span = pl.ds(p * tile, tile)
                    vs[pl.ds(r, 1), :] = vz[h][pl.ds(j, 1), span]
                    zs[pl.ds(r, 1), pl.ds(j * tile, tile)] = vz[h][pl.ds(col_tiles + j, 1), span]
        dv = dot(turned, vs[...], ((1,), (1,)))
        for q in range(per):
            span = pl.ds(q * tile, tile)
            for n in range(parts):
                at = pl.ds((q * parts + n) * rows, rows)
                left = xw[n][:, :row_tiles, span].reshape(rows, tile)
                for g in range(tile // LANES):
                    xs[g, at, :] = left[:, g * LANES : (g + 1) * LANES]
                core = dot(xw[n][:, row_tiles:, span].reshape(rows, tile), dv)
                kept = jnp.where(keep[at, :] > 0, core, 0.0)
                right = dot(kept, zs[...])
                for g in range(right.shape[1] // LANES):
                    ts[g, at, :] = right[:, g * LANES : (g + 1) * LANES]

    mine = pl.ds(step, RMAX, stride=row_tiles)
    left = jnp.concatenate([xs[g, mine, :] for g in range(xs.shape[0])], axis=1)
    right = jnp.concatenate([ts[g, mine, :] for g in range(ts.shape[0])], axis=1)
    out[...] = front[...] - dot(left, right, ((0,), (0,)))


def subtract_update(front, dinv, pivots, keep, xw, vz):
    tile = dinv.shape[0]
    row_tiles = front.shape[0] // tile
    width = front.shape[1]
    col_tiles = width // tile
    per = xw[0].shape[2] // tile
    total = RMAX * row_tiles

    def whole(array):
        return pl.BlockSpec(array.shape, lambda i: (0,) * array.ndim)

    block = pl.BlockSpec((tile, width), lambda i: (i, 0))
    pivots = pivots.reshape(1, tile)
    return pl.pallas_call(
        functools.partial(update_kernel, len(xw), len(vz), per, row_tiles, col_tiles, tile),
        grid=(row_tiles,),
        out_shape=pltpu.HBM(front.shape, front.dtype),
        in_specs=[block, whole(dinv), whole(pivots), whole(keep)] + [whole(a) for a in xw] + [whole(a) for a in vz],
        out_specs=block,
        scratch_shapes=[
            pltpu.VMEM((tile // LANES, total, LANES), jnp.float32),
            pltpu.VMEM((width // LANES, total, LANES), jnp.float32),
            pltpu.VMEM((col_tiles * RMAX, tile), jnp.float32),
            pltpu.VMEM((col_tiles * RMAX, width), jnp.float32),
        ],
        compiler_params=pltpu.CompilerParams(vmem_limit_bytes=24 * MIB),
        cost_estimate=pl.CostEstimate(flops=2 * front.size * 256, bytes_accessed=2 * front.size * 4, transcendentals=0),
        name="front_less_update",
    )(in_hbm(front), dinv, pivots, keep, *xw, *vz)


def add_kernel(count, row_tiles, col_tiles, rows, tile, row_map, base, *rest):
    arrived = rest[:count]
    out, held, got, base_sem, got_sem, out_sem = rest[count:]
    me = group_index()
    per_tile = tile // rows

    def at(m):
        source = me ^ m
        low = row_map[0, source // per_tile] * tile + source % per_tile * rows
        return pl.ds(pl.multiple_of(low, rows), rows)

    def fetch_base(m):
        return pltpu.make_async_copy(base.at[at(m), :], held.at[m], base_sem.at[m])

    def fetch_got(m):
        return pltpu.make_async_copy(arrived[m], got.at[m], got_sem.at[m])

    def store(m):
        return pltpu.make_async_copy(held.at[m], out.at[at(m), :], out_sem.at[m])

    for m in range(count):
        fetch_base(m).start()
        fetch_got(m).start()
    for m in range(count):
        fetch_base(m).wait()
        fetch_got(m).wait()
        for j in range(col_tiles):
            span = pl.ds(j * tile, tile)
            held[m, :, span] = held[m, :, span] + got[m, j]
        store(m).start()
    for m in range(count):
        store(m).wait()


def add_child(base, arrived, row_map, tile):
    row_tiles = base.shape[0] // tile
    count = len(arrived)
    col_tiles, rows, _ = arrived[0].shape
    anywhere = pl.BlockSpec(memory_space=pl.ANY)
    return pl.pallas_call(
        functools.partial(add_kernel, count, row_tiles, col_tiles, rows, tile),
        out_shape=jax.ShapeDtypeStruct(base.shape, base.dtype),
        in_specs=[pl.BlockSpec(memory_space=pltpu.SMEM), pl.BlockSpec(memory_space=pltpu.HBM)] + [anywhere] * count,
        out_specs=pl.BlockSpec(memory_space=pltpu.HBM),
        scratch_shapes=[
            pltpu.VMEM((count, rows, base.shape[1]), base.dtype),
            pltpu.VMEM((count, col_tiles, rows, tile), base.dtype),
            pltpu.SemaphoreType.DMA((count,)),
            pltpu.SemaphoreType.DMA((count,)),
            pltpu.SemaphoreType.DMA((count,)),
        ],
        compiler_params=pltpu.CompilerParams(vmem_limit_bytes=16 * MIB),
        cost_estimate=pl.CostEstimate(flops=base.size, bytes_accessed=3 * base.size * 4, transcendentals=0),
        name="add_child",
    )(row_map, in_hbm(base), *arrived)


def swap(array, m):
    size = lax.axis_size("col") * lax.axis_size("leaf")
    return lax.ppermute(array, GROUP, [(d, d ^ m) for d in range(size)])


def gather_row(array):
    size = lax.axis_size("row")
    return [array] + [lax.ppermute(array, "row", [(y, y ^ m) for y in range(size)]) for m in range(1, size)]


def on_device(
    front,
    child,
    row_map,
    col_map,
    x_fac,
    w_fac,
    v_fac,
    z_fac,
    dinv,
    pivots,
    rank_rows,
    rank_cols,
    admissible,
):
    tile = dinv.shape[0]
    row_tiles = front.shape[0] // tile
    col_tiles = front.shape[1] // tile
    devices = lax.axis_size("col") * lax.axis_size("leaf")
    per = x_fac.shape[1] // tile
    chunk = v_fac.shape[1] // tile

    vz = gather_row(jnp.concatenate([v_fac, z_fac], axis=0))
    mine = jnp.concatenate([x_fac, w_fac], axis=0)
    line = [mine] + [swap(mine, m) for m in range(NEAR, devices, NEAR)]
    pieces = place(child, col_map, tile, devices)
    line, pieces = lax.optimization_barrier((line, pieces))
    line = jnp.stack(line)
    xw = [line] + [swap(line, m) for m in range(1, NEAR)]
    arrived = [swap(pieces[m], m) for m in reversed(range(1, devices))]
    arrived = [pieces[0]] + arrived[::-1]

    far = np.arange(0, devices, NEAR, dtype=np.int32)
    source = group_index() ^ (far + np.arange(NEAR, dtype=np.int32)[:, None])
    r = source * per + np.arange(per, dtype=np.int32)[:, None, None]
    source = lax.axis_index("row") ^ np.arange(lax.axis_size("row"), dtype=np.int32)
    s = source[:, None] * chunk + np.arange(chunk, dtype=np.int32)
    keep_rows = r.reshape(RMAX, 1) < rank_rows[None, :]
    keep_cols = s.reshape(1, RMAX) < rank_cols[:, None]
    dense = (admissible == 0)[None, :, :, None]
    keep = (keep_rows[:, :, None, None] & keep_cols[None, None]) | dense
    keep = keep.astype(jnp.float32).reshape(RMAX * row_tiles, col_tiles * RMAX)

    base = subtract_update(front, dinv, pivots, keep, xw, vz)
    return add_child(base, arrived, row_map, tile)


def solution(mesh):
    return jax.shard_map(
        on_device,
        mesh=mesh,
        in_specs=(
            P("row", GROUP),
            P(("row", "col", "leaf"), None),
            P("row", None),
            P(),
            P("row", GROUP),
            P("row", GROUP),
            P(GROUP, "row"),
            P(GROUP, "row"),
            P(),
            P(),
            P("row"),
            P(GROUP),
            P("row", GROUP),
        ),
        out_specs=P("row", GROUP),
        check_vma=False,
    )
```

```python
import functools

import jax
import jax.numpy as jnp
import numpy as np
from jax import lax
from jax.experimental import pallas as pl
from jax.experimental.pallas import tpu as pltpu
from jax.sharding import PartitionSpec as P

RMAX = 64
LANES = 128
NEAR = 4
GROUP = ("col", "leaf")
HIGHEST = lax.Precision.HIGHEST
MIB = 1 << 20


def group_index():
    return lax.axis_index("col") * lax.axis_size("leaf") + lax.axis_index("leaf")


def in_hbm(array):
    return pltpu.with_memory_space_constraint(array, pltpu.HBM)


def place_kernel(tiles, tile, col_map, child, placed, held, in_sem, out_sem):
    def fetch(b):
        return pltpu.make_async_copy(child.at[:, pl.ds(b * tile, tile)], held.at[b], in_sem.at[b])

    def store(b):
        return pltpu.make_async_copy(held.at[b], placed.at[col_map[b]], out_sem.at[b])

    for b in range(tiles):
        fetch(b).start()
    for b in range(tiles):
        fetch(b).wait()
        store(b).start()
    for b in range(tiles):
        store(b).wait()


def place(child, col_map, tile):
    rows = child.shape[0]
    tiles = col_map.shape[0]
    return pl.pallas_call(
        functools.partial(place_kernel, tiles, tile),
        out_shape=pltpu.HBM((tiles, rows, tile), child.dtype),
        in_specs=[pl.BlockSpec(memory_space=pltpu.SMEM), pl.BlockSpec(memory_space=pltpu.HBM)],
        out_specs=pl.BlockSpec(memory_space=pltpu.HBM),
        scratch_shapes=[
            pltpu.VMEM((tiles, rows, tile), child.dtype),
            pltpu.SemaphoreType.DMA((tiles,)),
            pltpu.SemaphoreType.DMA((tiles,)),
        ],
        compiler_params=pltpu.CompilerParams(vmem_limit_bytes=16 * MIB),
        cost_estimate=pl.CostEstimate(flops=0, bytes_accessed=2 * child.size * 4, transcendentals=0),
        name="place_child",
    )(col_map, in_hbm(child))


def dot(a, b, contract=((1,), (0,))):
    return lax.dot_general(a, b, (contract, ((), ())), precision=HIGHEST, preferred_element_type=jnp.float32)


def update_kernel(
    parts, halves, per, row_tiles, col_tiles, tile,
    front, dinv, pivots, keep, *rest,
):
    xw = rest[:parts]
    vz = rest[parts : parts + halves]
    out, xs, ts, vs, zs = rest[parts + halves :]
    step = pl.program_id(0)
    chunk = vz[0].shape[1] // tile
    slots = xw[0].shape[0]
    rows = slots * row_tiles

    @pl.when(step == 0)
    def _():
        hot = (lax.broadcasted_iota(jnp.int32, (tile, tile), 0) == pivots[...]).astype(jnp.float32)
        turned = dot(hot, dinv[...])
        zs[...] = jnp.zeros_like(zs)
        for h in range(halves):
            for j in range(col_tiles):
                for p in range(chunk):
                    r = j * RMAX + h * chunk + p
                    span = pl.ds(p * tile, tile)
                    vs[pl.ds(r, 1), :] = vz[h][pl.ds(j, 1), span]
                    zs[pl.ds(r, 1), pl.ds(j * tile, tile)] = vz[h][pl.ds(col_tiles + j, 1), span]
        dv = dot(turned, vs[...], ((1,), (1,)))
        for q in range(per):
            span = pl.ds(q * tile, tile)
            for n in range(parts):
                at = pl.ds((q * parts + n) * rows, rows)
                left = xw[n][:, :row_tiles, span].reshape(rows, tile)
                for g in range(tile // LANES):
                    xs[g, at, :] = left[:, g * LANES : (g + 1) * LANES]
                core = dot(xw[n][:, row_tiles:, span].reshape(rows, tile), dv)
                kept = jnp.where(keep[at, :] > 0, core, 0.0)
                right = dot(kept, zs[...])
                for g in range(right.shape[1] // LANES):
                    ts[g, at, :] = right[:, g * LANES : (g + 1) * LANES]

    mine = pl.ds(step, RMAX, stride=row_tiles)
    left = jnp.concatenate([xs[g, mine, :] for g in range(xs.shape[0])], axis=1)
    right = jnp.concatenate([ts[g, mine, :] for g in range(ts.shape[0])], axis=1)
    out[...] = front[...] - dot(left, right, ((0,), (0,)))


def subtract_update(front, dinv, pivots, keep, xw, vz):
    tile = dinv.shape[0]
    row_tiles = front.shape[0] // tile
    width = front.shape[1]
    col_tiles = width // tile
    per = xw[0].shape[2] // tile
    total = RMAX * row_tiles

    def whole(array):
        return pl.BlockSpec(array.shape, lambda i: (0,) * array.ndim)

    block = pl.BlockSpec((tile, width), lambda i: (i, 0))
    pivots = pivots.reshape(1, tile)
    return pl.pallas_call(
        functools.partial(update_kernel, len(xw), len(vz), per, row_tiles, col_tiles, tile),
        grid=(row_tiles,),
        out_shape=pltpu.HBM(front.shape, front.dtype),
        in_specs=[block, whole(dinv), whole(pivots), whole(keep)] + [whole(a) for a in xw] + [whole(a) for a in vz],
        out_specs=block,
        scratch_shapes=[
            pltpu.VMEM((tile // LANES, total, LANES), jnp.float32),
            pltpu.VMEM((width // LANES, total, LANES), jnp.float32),
            pltpu.VMEM((col_tiles * RMAX, tile), jnp.float32),
            pltpu.VMEM((col_tiles * RMAX, width), jnp.float32),
        ],
        compiler_params=pltpu.CompilerParams(vmem_limit_bytes=24 * MIB),
        cost_estimate=pl.CostEstimate(flops=2 * front.size * 256, bytes_accessed=2 * front.size * 4, transcendentals=0),
        name="front_less_update",
    )(in_hbm(front), dinv, pivots, keep, *xw, *vz)


def add_kernel(row_tiles, pieces, col_tiles, rows, tile, row_map, base, arrived, out, held, got, base_sem, got_sem, out_sem):
    def at(a):
        return pl.ds(row_map[0, a] * tile, tile)

    def fetch_base(a):
        return pltpu.make_async_copy(base.at[at(a), :], held.at[a], base_sem.at[a])

    def fetch_got(a):
        return pltpu.make_async_copy(arrived.at[pl.ds(a * pieces, pieces)], got.at[a], got_sem.at[a])

    def store(a):
        return pltpu.make_async_copy(held.at[a], out.at[at(a), :], out_sem.at[a])

    for a in range(row_tiles):
        fetch_base(a).start()
        fetch_got(a).start()
    for a in range(row_tiles):
        fetch_base(a).wait()
        fetch_got(a).wait()
        for p in range(pieces):
            for j in range(col_tiles):
                low, left = pl.ds(p * rows, rows), pl.ds(j * tile, tile)
                held[a, low, left] = held[a, low, left] + got[a, p, j]
        store(a).start()
    for a in range(row_tiles):
        store(a).wait()


def add_child(base, arrived, row_map, tile):
    row_tiles = base.shape[0] // tile
    count, col_tiles, rows, _ = arrived.shape
    pieces = count // row_tiles
    return pl.pallas_call(
        functools.partial(add_kernel, row_tiles, pieces, col_tiles, rows, tile),
        out_shape=pltpu.HBM(base.shape, base.dtype),
        in_specs=[
            pl.BlockSpec(memory_space=pltpu.SMEM),
            pl.BlockSpec(memory_space=pltpu.HBM),
            pl.BlockSpec(memory_space=pltpu.HBM),
        ],
        out_specs=pl.BlockSpec(memory_space=pltpu.HBM),
        scratch_shapes=[
            pltpu.VMEM((row_tiles, tile, base.shape[1]), base.dtype),
            pltpu.VMEM((row_tiles, pieces, col_tiles, rows, tile), base.dtype),
            pltpu.SemaphoreType.DMA((row_tiles,)),
            pltpu.SemaphoreType.DMA((row_tiles,)),
            pltpu.SemaphoreType.DMA((row_tiles,)),
        ],
        compiler_params=pltpu.CompilerParams(vmem_limit_bytes=24 * MIB),
        cost_estimate=pl.CostEstimate(flops=base.size, bytes_accessed=3 * base.size * 4, transcendentals=0),
        name="add_child",
    )(row_map, in_hbm(base), in_hbm(arrived))


def swap(array, m):
    size = lax.axis_size("col") * lax.axis_size("leaf")
    return lax.ppermute(array, GROUP, [(d, d ^ m) for d in range(size)])


def gather_row(array):
    size = lax.axis_size("row")
    return [array] + [lax.ppermute(array, "row", [(y, y ^ m) for y in range(size)]) for m in range(1, size)]


def on_device(
    front,
    child,
    row_map,
    col_map,
    x_fac,
    w_fac,
    v_fac,
    z_fac,
    dinv,
    pivots,
    rank_rows,
    rank_cols,
    admissible,
):
    tile = dinv.shape[0]
    row_tiles = front.shape[0] // tile
    col_tiles = front.shape[1] // tile
    devices = lax.axis_size("col") * lax.axis_size("leaf")
    per = x_fac.shape[1] // tile
    chunk = v_fac.shape[1] // tile

    vz = gather_row(jnp.concatenate([v_fac, z_fac], axis=0))
    mine = jnp.concatenate([x_fac, w_fac], axis=0)
    line = [mine] + [swap(mine, m) for m in range(NEAR, devices, NEAR)]
    placed = place(child, col_map, tile).reshape(devices, col_tiles, child.shape[0], tile)
    line, vz, placed = lax.optimization_barrier((line, vz, placed))
    line = jnp.stack(line)
    xw = [line] + [swap(line, m) for m in range(1, NEAR)]
    arrived = lax.all_to_all(placed, GROUP, split_axis=0, concat_axis=0, tiled=True)

    far = np.arange(0, devices, NEAR, dtype=np.int32)
    source = group_index() ^ (far + np.arange(NEAR, dtype=np.int32)[:, None])
    r = source * per + np.arange(per, dtype=np.int32)[:, None, None]
    source = lax.axis_index("row") ^ np.arange(lax.axis_size("row"), dtype=np.int32)
    s = source[:, None] * chunk + np.arange(chunk, dtype=np.int32)
    keep_rows = r.reshape(RMAX, 1) < rank_rows[None, :]
    keep_cols = s.reshape(1, RMAX) < rank_cols[:, None]
    dense = (admissible == 0)[None, :, :, None]
    keep = (keep_rows[:, :, None, None] & keep_cols[None, None]) | dense
    keep = keep.astype(jnp.float32).reshape(RMAX * row_tiles, col_tiles * RMAX)

    base = subtract_update(front, dinv, pivots, keep, xw, vz)
    return add_child(base, arrived, row_map, tile)


def solution(mesh):
    return jax.shard_map(
        on_device,
        mesh=mesh,
        in_specs=(
            P("row", GROUP),
            P(("row", "col", "leaf"), None),
            P("row", None),
            P(),
            P("row", GROUP),
            P("row", GROUP),
            P(GROUP, "row"),
            P(GROUP, "row"),
            P(),
            P(),
            P("row"),
            P(GROUP),
            P("row", GROUP),
        ),
        out_specs=P("row", GROUP),
        check_vma=False,
    )
```

```python
import functools

import jax
import jax.numpy as jnp
import numpy as np
from jax import lax
from jax.experimental import pallas as pl
from jax.experimental.pallas import tpu as pltpu
from jax.sharding import PartitionSpec as P

RMAX = 64
LANES = 128
NEAR = 4
GROUP = ("col", "leaf")
HIGHEST = lax.Precision.HIGHEST
MIB = 1 << 20


def group_index():
    return lax.axis_index("col") * lax.axis_size("leaf") + lax.axis_index("leaf")


def in_hbm(array):
    return pltpu.with_memory_space_constraint(array, pltpu.HBM)


def place_kernel(tiles, groups, tile, col_map, child, placed, held, in_sem, out_sem):
    width = tiles // groups * tile

    def fetch(g):
        span = pl.ds(g * width, width)
        return pltpu.make_async_copy(child.at[:, span], held.at[:, span], in_sem.at[g])

    def store(b):
        return pltpu.make_async_copy(held.at[:, pl.ds(b * tile, tile)], placed.at[col_map[b]], out_sem.at[b])

    for g in range(groups):
        fetch(g).start()
    for g in range(groups):
        fetch(g).wait()
        for b in range(g * tiles // groups, (g + 1) * tiles // groups):
            store(b).start()
    for b in range(tiles):
        store(b).wait()


def in_vmem(array):
    return pltpu.with_memory_space_constraint(array, pltpu.VMEM)


def place(child, col_map, tile):
    rows = child.shape[0]
    tiles = col_map.shape[0]
    groups = 8
    return pl.pallas_call(
        functools.partial(place_kernel, tiles, groups, tile),
        out_shape=pltpu.HBM((tiles, rows, tile), child.dtype),
        in_specs=[pl.BlockSpec(memory_space=pltpu.SMEM), pl.BlockSpec(memory_space=pltpu.HBM)],
        out_specs=pl.BlockSpec(memory_space=pltpu.HBM),
        scratch_shapes=[
            pltpu.VMEM(child.shape, child.dtype),
            pltpu.SemaphoreType.DMA((groups,)),
            pltpu.SemaphoreType.DMA((tiles,)),
        ],
        compiler_params=pltpu.CompilerParams(vmem_limit_bytes=16 * MIB),
        cost_estimate=pl.CostEstimate(flops=0, bytes_accessed=2 * child.size * 4, transcendentals=0),
        name="place_child",
    )(in_hbm(col_map), in_hbm(child))


def dot(a, b, contract=((1,), (0,))):
    return lax.dot_general(a, b, (contract, ((), ())), precision=HIGHEST, preferred_element_type=jnp.float32)


def update_kernel(
    parts, halves, per, row_tiles, col_tiles, tile,
    front, dinv, pivots, keep, *rest,
):
    xw = rest[:parts]
    vz = rest[parts : parts + halves]
    out, xs, ts, vs, zs = rest[parts + halves :]
    step = pl.program_id(0)
    chunk = vz[0].shape[1] // tile
    slots = xw[0].shape[0]
    rows = slots * row_tiles

    @pl.when(step == 0)
    def _():
        hot = (lax.broadcasted_iota(jnp.int32, (tile, tile), 0) == pivots[...]).astype(jnp.float32)
        turned = dot(hot, dinv[...])
        zs[...] = jnp.zeros_like(zs)
        for h in range(halves):
            for j in range(col_tiles):
                for p in range(chunk):
                    r = j * RMAX + h * chunk + p
                    span = pl.ds(p * tile, tile)
                    vs[pl.ds(r, 1), :] = vz[h][pl.ds(j, 1), span]
                    zs[pl.ds(r, 1), pl.ds(j * tile, tile)] = vz[h][pl.ds(col_tiles + j, 1), span]
        dv = dot(turned, vs[...], ((1,), (1,)))
        for q in range(per):
            span = pl.ds(q * tile, tile)
            for n in range(parts):
                at = pl.ds((q * parts + n) * rows, rows)
                left = xw[n][:, :row_tiles, span].reshape(rows, tile)
                for g in range(tile // LANES):
                    xs[g, at, :] = left[:, g * LANES : (g + 1) * LANES]
                core = dot(xw[n][:, row_tiles:, span].reshape(rows, tile), dv)
                kept = jnp.where(keep[at, :] > 0, core, 0.0)
                right = dot(kept, zs[...])
                for g in range(right.shape[1] // LANES):
                    ts[g, at, :] = right[:, g * LANES : (g + 1) * LANES]

    mine = pl.ds(step, RMAX, stride=row_tiles)
    left = jnp.concatenate([xs[g, mine, :] for g in range(xs.shape[0])], axis=1)
    right = jnp.concatenate([ts[g, mine, :] for g in range(ts.shape[0])], axis=1)
    out[...] = front[...] - dot(left, right, ((0,), (0,)))


def subtract_update(front, dinv, pivots, keep, xw, vz):
    tile = dinv.shape[0]
    row_tiles = front.shape[0] // tile
    width = front.shape[1]
    col_tiles = width // tile
    per = xw[0].shape[2] // tile
    total = RMAX * row_tiles

    def whole(array):
        return pl.BlockSpec(array.shape, lambda i: (0,) * array.ndim)

    block = pl.BlockSpec((tile, width), lambda i: (i, 0))
    pivots = pivots.reshape(1, tile)
    return pl.pallas_call(
        functools.partial(update_kernel, len(xw), len(vz), per, row_tiles, col_tiles, tile),
        grid=(row_tiles,),
        out_shape=pltpu.VMEM(front.shape, front.dtype),
        in_specs=[block, whole(dinv), whole(pivots), whole(keep)] + [whole(a) for a in xw] + [whole(a) for a in vz],
        out_specs=block,
        scratch_shapes=[
            pltpu.VMEM((tile // LANES, total, LANES), jnp.float32),
            pltpu.VMEM((width // LANES, total, LANES), jnp.float32),
            pltpu.VMEM((col_tiles * RMAX, tile), jnp.float32),
            pltpu.VMEM((col_tiles * RMAX, width), jnp.float32),
        ],
        compiler_params=pltpu.CompilerParams(vmem_limit_bytes=24 * MIB),
        cost_estimate=pl.CostEstimate(flops=2 * front.size * 256, bytes_accessed=2 * front.size * 4, transcendentals=0),
        name="front_less_update",
    )(in_hbm(front), dinv, pivots, keep, *xw, *vz)


def add_kernel(row_tiles, pieces, col_tiles, rows, tile, row_map, base, arrived, out, held, got, got_sem, out_sem):
    def at(a, p):
        return pl.ds(pl.multiple_of(row_map[0, a] * tile + p * rows, rows), rows)

    def fetch(a):
        return pltpu.make_async_copy(arrived.at[pl.ds(a * pieces, pieces)], got.at[a], got_sem.at[a])

    def store(a):
        return pltpu.make_async_copy(held.at[a], out.at[pl.ds(row_map[0, a] * tile, tile), :], out_sem.at[a])

    for a in range(row_tiles):
        fetch(a).start()
    for a in range(row_tiles):
        fetch(a).wait()
        for p in range(pieces):
            for j in range(col_tiles):
                span = pl.ds(j * tile, tile)
                held[a, pl.ds(p * rows, rows), span] = base[at(a, p), span] + got[a, p, j]
        store(a).start()
    for a in range(row_tiles):
        store(a).wait()


def add_child(base, arrived, row_map, tile):
    row_tiles = base.shape[0] // tile
    count, col_tiles, rows, _ = arrived.shape
    pieces = count // row_tiles
    return pl.pallas_call(
        functools.partial(add_kernel, row_tiles, pieces, col_tiles, rows, tile),
        out_shape=pltpu.HBM(base.shape, base.dtype),
        in_specs=[
            pl.BlockSpec(memory_space=pltpu.SMEM),
            pl.BlockSpec(memory_space=pltpu.VMEM),
            pl.BlockSpec(memory_space=pltpu.HBM),
        ],
        out_specs=pl.BlockSpec(memory_space=pltpu.HBM),
        scratch_shapes=[
            pltpu.VMEM((row_tiles, tile, base.shape[1]), base.dtype),
            pltpu.VMEM((row_tiles, pieces, col_tiles, rows, tile), base.dtype),
            pltpu.SemaphoreType.DMA((row_tiles,)),
            pltpu.SemaphoreType.DMA((row_tiles,)),
        ],
        compiler_params=pltpu.CompilerParams(vmem_limit_bytes=24 * MIB),
        cost_estimate=pl.CostEstimate(flops=base.size, bytes_accessed=3 * base.size * 4, transcendentals=0),
        name="add_child",
    )(in_hbm(row_map), in_vmem(base), in_hbm(arrived))


def swap(array, m):
    size = lax.axis_size("col") * lax.axis_size("leaf")
    return lax.ppermute(array, GROUP, [(d, d ^ m) for d in range(size)])


def gather_row(array):
    size = lax.axis_size("row")
    return [array] + [lax.ppermute(array, "row", [(y, y ^ m) for y in range(size)]) for m in range(1, size)]


def on_device(
    front,
    child,
    row_map,
    col_map,
    x_fac,
    w_fac,
    v_fac,
    z_fac,
    dinv,
    pivots,
    rank_rows,
    rank_cols,
    admissible,
):
    tile = dinv.shape[0]
    row_tiles = front.shape[0] // tile
    col_tiles = front.shape[1] // tile
    devices = lax.axis_size("col") * lax.axis_size("leaf")
    per = x_fac.shape[1] // tile
    chunk = v_fac.shape[1] // tile

    mine = jnp.pad(x_fac, ((0, row_tiles), (0, 0))) + jnp.pad(w_fac, ((row_tiles, 0), (0, 0)))
    line = [mine] + [swap(mine, m) for m in range(NEAR, devices, NEAR)]
    placed = place(child, col_map, tile).reshape(devices, col_tiles, child.shape[0], tile)
    line, placed, v_fac, z_fac, rank_rows, rank_cols, admissible = lax.optimization_barrier(
        (line, placed, v_fac, z_fac, rank_rows, rank_cols, admissible)
    )
    line = jnp.stack(line)
    vz = gather_row(jnp.concatenate([v_fac, z_fac], axis=0))
    xw = [line] + [swap(line, m) for m in range(1, NEAR)]
    arrived = lax.all_to_all(placed, GROUP, split_axis=0, concat_axis=0, tiled=True)

    far = np.arange(0, devices, NEAR, dtype=np.int32)
    source = group_index() ^ (far + np.arange(NEAR, dtype=np.int32)[:, None])
    r = source * per + np.arange(per, dtype=np.int32)[:, None, None]
    source = lax.axis_index("row") ^ np.arange(lax.axis_size("row"), dtype=np.int32)
    s = source[:, None] * chunk + np.arange(chunk, dtype=np.int32)
    keep_rows = r.reshape(RMAX, 1) < rank_rows[None, :]
    keep_cols = s.reshape(1, RMAX) < rank_cols[:, None]
    dense = (admissible == 0)[None, :, :, None]
    keep = (keep_rows[:, :, None, None] & keep_cols[None, None]) | dense
    keep = keep.astype(jnp.float32).reshape(RMAX * row_tiles, col_tiles * RMAX)

    base = subtract_update(front, dinv, pivots, keep, xw, vz)
    return add_child(base, arrived, row_map, tile)


def solution(mesh):
    return jax.shard_map(
        on_device,
        mesh=mesh,
        in_specs=(
            P("row", GROUP),
            P(("row", "col", "leaf"), None),
            P("row", None),
            P(),
            P("row", GROUP),
            P("row", GROUP),
            P(GROUP, "row"),
            P(GROUP, "row"),
            P(),
            P(),
            P("row"),
            P(GROUP),
            P("row", GROUP),
        ),
        out_specs=P("row", GROUP),
        check_vma=False,
    )
```

```python
import functools

import jax
import jax.numpy as jnp
import numpy as np
from jax import lax
from jax.experimental import pallas as pl
from jax.experimental.pallas import tpu as pltpu
from jax.sharding import PartitionSpec as P

RMAX = 64
LANES = 128
NEAR = 4
WINDOW = 5
GROUP = ("col", "leaf")
HIGHEST = lax.Precision.HIGHEST
MIB = 1 << 20


def group_index():
    return lax.axis_index("col") * lax.axis_size("leaf") + lax.axis_index("leaf")


def in_hbm(array):
    return pltpu.with_memory_space_constraint(array, pltpu.HBM)


def place_kernel(tiles, tile, col_tiles, col_map, child, *rest):
    pieces = rest[: tiles // col_tiles]
    inverse, sem = rest[tiles // col_tiles :]
    me = group_index()
    for b in range(tiles):
        inverse[col_map[b]] = b

    def copy(m, j):
        b = inverse[(me ^ m) * col_tiles + j]
        span = pl.ds(pl.multiple_of(b * tile, tile), tile)
        return pltpu.make_async_copy(child.at[:, span], pieces[m].at[j], sem.at[m, j])

    order = [(m, j) for m in reversed(range(len(pieces))) for j in range(col_tiles)]
    for m, j in order:
        copy(m, j).start()
    for m, j in order:
        copy(m, j).wait()


def in_vmem(array):
    return pltpu.with_memory_space_constraint(array, pltpu.VMEM)


def place(child, col_map, tile, devices):
    rows = child.shape[0]
    tiles = col_map.shape[0]
    col_tiles = tiles // devices
    return pl.pallas_call(
        functools.partial(place_kernel, tiles, tile, col_tiles),
        out_shape=[pltpu.VMEM((col_tiles, rows, tile), child.dtype)] * devices,
        in_specs=[pl.BlockSpec(memory_space=pltpu.SMEM), pl.BlockSpec(memory_space=pltpu.HBM)],
        out_specs=[pl.BlockSpec(memory_space=pltpu.VMEM)] * devices,
        scratch_shapes=[pltpu.SMEM((tiles,), jnp.int32), pltpu.SemaphoreType.DMA((devices, col_tiles))],
        compiler_params=pltpu.CompilerParams(vmem_limit_bytes=2 * MIB),
        cost_estimate=pl.CostEstimate(flops=0, bytes_accessed=2 * child.size * 4, transcendentals=0),
        name="place_child",
    )(in_hbm(col_map), in_hbm(child))


def dot(a, b, contract=((1,), (0,))):
    return lax.dot_general(a, b, (contract, ((), ())), precision=HIGHEST, preferred_element_type=jnp.float32)


def update_kernel(
    parts, halves, per, row_tiles, col_tiles, tile,
    front, dinv, pivots, keep, *rest,
):
    xw = rest[:parts]
    vz = rest[parts : parts + halves]
    out, xs, ts, vs, zs = rest[parts + halves :]
    step = pl.program_id(0)
    chunk = vz[0].shape[1] // tile
    slots = xw[0].shape[0]
    rows = slots * row_tiles

    @pl.when(step == 0)
    def _():
        hot = (lax.broadcasted_iota(jnp.int32, (tile, tile), 0) == pivots[...]).astype(jnp.float32)
        turned = dot(hot, dinv[...])
        zs[...] = jnp.zeros_like(zs)
        for h in range(halves):
            for j in range(col_tiles):
                for p in range(chunk):
                    r = j * RMAX + h * chunk + p
                    span = pl.ds(p * tile, tile)
                    vs[pl.ds(r, 1), :] = vz[h][pl.ds(j, 1), span]
                    zs[pl.ds(r, 1), pl.ds(j * tile, tile)] = vz[h][pl.ds(col_tiles + j, 1), span]
        dv = dot(turned, vs[...], ((1,), (1,)))
        for q in range(per):
            span = pl.ds(q * tile, tile)
            for n in range(parts):
                at = pl.ds((q * parts + n) * rows, rows)
                left = xw[n][:, :row_tiles, span].reshape(rows, tile)
                for g in range(tile // LANES):
                    xs[g, at, :] = left[:, g * LANES : (g + 1) * LANES]
                core = dot(xw[n][:, row_tiles:, span].reshape(rows, tile), dv)
                kept = jnp.where(keep[at, :] > 0, core, 0.0)
                right = dot(kept, zs[...])
                for g in range(right.shape[1] // LANES):
                    ts[g, at, :] = right[:, g * LANES : (g + 1) * LANES]

    mine = pl.ds(step, RMAX, stride=row_tiles)
    left = jnp.concatenate([xs[g, mine, :] for g in range(xs.shape[0])], axis=1)
    right = jnp.concatenate([ts[g, mine, :] for g in range(ts.shape[0])], axis=1)
    out[...] = front[...] - dot(left, right, ((0,), (0,)))


def subtract_update(front, dinv, pivots, keep, xw, vz):
    tile = dinv.shape[0]
    row_tiles = front.shape[0] // tile
    width = front.shape[1]
    col_tiles = width // tile
    per = xw[0].shape[2] // tile
    total = RMAX * row_tiles

    def whole(array):
        return pl.BlockSpec(array.shape, lambda i: (0,) * array.ndim)

    block = pl.BlockSpec((tile, width), lambda i: (i, 0))
    pivots = pivots.reshape(1, tile)
    return pl.pallas_call(
        functools.partial(update_kernel, len(xw), len(vz), per, row_tiles, col_tiles, tile),
        grid=(row_tiles,),
        out_shape=pltpu.VMEM(front.shape, front.dtype),
        in_specs=[block, whole(dinv), whole(pivots), whole(keep)] + [whole(a) for a in xw] + [whole(a) for a in vz],
        out_specs=block,
        scratch_shapes=[
            pltpu.VMEM((tile // LANES, total, LANES), jnp.float32),
            pltpu.VMEM((width // LANES, total, LANES), jnp.float32),
            pltpu.VMEM((col_tiles * RMAX, tile), jnp.float32),
            pltpu.VMEM((col_tiles * RMAX, width), jnp.float32),
        ],
        compiler_params=pltpu.CompilerParams(vmem_limit_bytes=24 * MIB),
        cost_estimate=pl.CostEstimate(flops=2 * front.size * 256, bytes_accessed=2 * front.size * 4, transcendentals=0),
        name="front_less_update",
    )(in_hbm(front), dinv, pivots, keep, *xw, *vz)


def add_kernel(members, tile, row_map, base, *rest):
    arrived = rest[: len(members)]
    out, held, sem = rest[-3:]
    me = group_index()
    col_tiles, rows, _ = arrived[0].shape
    per_tile = tile // rows

    def at(n):
        source = me ^ members[n]
        low = row_map[0, source // per_tile] * tile + source % per_tile * rows
        return pl.ds(pl.multiple_of(low, rows), rows)

    def store(n):
        return pltpu.make_async_copy(held.at[n], out.at[at(n), :], sem.at[n])

    for n in range(len(members)):
        for j in range(col_tiles):
            span = pl.ds(j * tile, tile)
            held[n, :, span] = base[at(n), span] + arrived[n][j]
        store(n).start()
    for n in range(len(members)):
        store(n).wait()


def add_child(out, base, arrived, members, row_map, tile):
    rows = arrived[0].shape[1]
    inner = pl.BlockSpec(memory_space=pltpu.VMEM)
    outer = pl.BlockSpec(memory_space=pltpu.HBM)
    size = len(members) * rows * base.shape[1]
    before = [] if out is None else [out]
    return pl.pallas_call(
        functools.partial(add_kernel, members, tile),
        out_shape=pltpu.HBM(base.shape, base.dtype),
        in_specs=[pl.BlockSpec(memory_space=pltpu.SMEM)] + [inner] * (1 + len(members)) + [outer] * len(before),
        out_specs=outer,
        scratch_shapes=[
            pltpu.VMEM((len(members), rows, base.shape[1]), base.dtype),
            pltpu.SemaphoreType.DMA((len(members),)),
        ],
        input_output_aliases={2 + len(members): 0} if before else {},
        compiler_params=pltpu.CompilerParams(vmem_limit_bytes=16 * MIB),
        cost_estimate=pl.CostEstimate(flops=size, bytes_accessed=size * 4, transcendentals=0),
        name="add_child",
    )(in_hbm(row_map), in_vmem(base), *[in_vmem(piece) for piece in arrived], *before)


class Sender:
    def __init__(self):
        self.arrived = []

    def send(self, array, axes, m):
        spot = len(self.arrived) - WINDOW
        if spot >= 0:
            array, self.arrived[spot] = lax.optimization_barrier((array, self.arrived[spot]))
        size = int(np.prod([lax.axis_size(axis) for axis in axes]))
        self.arrived.append(lax.ppermute(array, axes, [(d, d ^ m) for d in range(size)]))
        return len(self.arrived) - 1


def on_device(
    front,
    child,
    row_map,
    col_map,
    x_fac,
    w_fac,
    v_fac,
    z_fac,
    dinv,
    pivots,
    rank_rows,
    rank_cols,
    admissible,
):
    tile = dinv.shape[0]
    row_tiles = front.shape[0] // tile
    col_tiles = front.shape[1] // tile
    devices = lax.axis_size("col") * lax.axis_size("leaf")
    per = x_fac.shape[1] // tile
    chunk = v_fac.shape[1] // tile

    sender = Sender()
    mine = jnp.pad(x_fac, ((0, row_tiles), (0, 0))) + jnp.pad(w_fac, ((row_tiles, 0), (0, 0)))
    mine, child = lax.optimization_barrier((mine, child))
    line = [sender.send(mine, GROUP, m) for m in range(NEAR, devices, NEAR)]
    pieces = place(child, col_map, tile, devices)
    pieces, v_fac, z_fac, rank_rows, rank_cols, admissible = lax.optimization_barrier(
        (pieces, v_fac, z_fac, rank_rows, rank_cols, admissible)
    )

    half = devices // 2
    spots = {}
    crossing = list(reversed(range(half, devices)))
    local = [m for pair in zip(reversed(range(NEAR, half)), [3, 2, 1] + [None] * half) for m in pair if m]
    between = [("xw", m) for m in range(1, NEAR)] + [("vz", m) for m in range(1, lax.axis_size("row"))]
    between += [("child", m) for m in local]
    gaps = len(crossing) - 2
    xw, vz = [None], [None]
    for n, m in enumerate(crossing):
        for i, (kind, other) in enumerate(between):
            if n >= 2 and i * gaps // len(between) == n - 2:
                if kind == "xw":
                    if xw == [None]:
                        xw[0] = jnp.stack([mine] + [sender.arrived[i] for i in line])
                    xw.append(sender.send(xw[0], GROUP, other))
                elif kind == "vz":
                    if vz == [None]:
                        vz[0] = jnp.concatenate([v_fac, z_fac], axis=0)
                    vz.append(sender.send(vz[0], ("row",), other))
                else:
                    spots[other] = sender.send(pieces[other], GROUP, other)
        spots[m] = sender.send(pieces[m], GROUP, m)
    xw = xw[:1] + [sender.arrived[i] for i in xw[1:]]
    vz = vz[:1] + [sender.arrived[i] for i in vz[1:]]
    order = [0] + sorted(spots, key=lambda m: spots[m])
    got = {m: sender.arrived[spots[m]] for m in spots}
    got[0] = pieces[0]

    far = np.arange(0, devices, NEAR, dtype=np.int32)
    source = group_index() ^ (far + np.arange(NEAR, dtype=np.int32)[:, None])
    r = source * per + np.arange(per, dtype=np.int32)[:, None, None]
    source = lax.axis_index("row") ^ np.arange(lax.axis_size("row"), dtype=np.int32)
    s = source[:, None] * chunk + np.arange(chunk, dtype=np.int32)
    keep_rows = r.reshape(RMAX, 1) < rank_rows[None, :]
    keep_cols = s.reshape(1, RMAX) < rank_cols[:, None]
    dense = (admissible == 0)[None, :, :, None]
    keep = (keep_rows[:, :, None, None] & keep_cols[None, None]) | dense
    keep = keep.astype(jnp.float32).reshape(RMAX * row_tiles, col_tiles * RMAX)

    base = subtract_update(front, dinv, pivots, keep, xw, vz)
    out = None
    for members in (order[: half - 1], order[half - 1 : -2], order[-2:]):
        out = add_child(out, base, [got[m] for m in members], members, row_map, tile)
    return out


def solution(mesh):
    return jax.shard_map(
        on_device,
        mesh=mesh,
        in_specs=(
            P("row", GROUP),
            P(("row", "col", "leaf"), None),
            P("row", None),
            P(),
            P("row", GROUP),
            P("row", GROUP),
            P(GROUP, "row"),
            P(GROUP, "row"),
            P(),
            P(),
            P("row"),
            P(GROUP),
            P("row", GROUP),
        ),
        out_specs=P("row", GROUP),
        check_vma=False,
    )
```

```python
import functools

import jax
import jax.numpy as jnp
import numpy as np
from jax import lax
from jax.experimental import pallas as pl
from jax.experimental.pallas import tpu as pltpu
from jax.sharding import PartitionSpec as P

RMAX = 64
LANES = 128
NEAR = 4
WINDOW = 5
GROUP = ("col", "leaf")
HIGHEST = lax.Precision.HIGHEST
MIB = 1 << 20


def group_index():
    return lax.axis_index("col") * lax.axis_size("leaf") + lax.axis_index("leaf")


def in_hbm(array):
    return pltpu.with_memory_space_constraint(array, pltpu.HBM)


def place_kernel(tiles, tile, col_tiles, col_map, child, *rest):
    pieces = rest[: tiles // col_tiles]
    inverse, sem = rest[tiles // col_tiles :]
    me = group_index()
    for b in range(tiles):
        inverse[col_map[b]] = b

    def copy(m, j):
        b = inverse[(me ^ m) * col_tiles + j]
        span = pl.ds(pl.multiple_of(b * tile, tile), tile)
        return pltpu.make_async_copy(child.at[:, span], pieces[m].at[j], sem.at[m, j])

    order = [(m, j) for m in reversed(range(len(pieces))) for j in range(col_tiles)]
    for m, j in order:
        copy(m, j).start()
    for m, j in order:
        copy(m, j).wait()


def in_vmem(array):
    return pltpu.with_memory_space_constraint(array, pltpu.VMEM)


def place(child, col_map, tile, devices):
    rows = child.shape[0]
    tiles = col_map.shape[0]
    col_tiles = tiles // devices
    return pl.pallas_call(
        functools.partial(place_kernel, tiles, tile, col_tiles),
        out_shape=[pltpu.VMEM((col_tiles, rows, tile), child.dtype)] * devices,
        in_specs=[pl.BlockSpec(memory_space=pltpu.SMEM), pl.BlockSpec(memory_space=pltpu.HBM)],
        out_specs=[pl.BlockSpec(memory_space=pltpu.VMEM)] * devices,
        scratch_shapes=[pltpu.SMEM((tiles,), jnp.int32), pltpu.SemaphoreType.DMA((devices, col_tiles))],
        compiler_params=pltpu.CompilerParams(vmem_limit_bytes=2 * MIB),
        cost_estimate=pl.CostEstimate(flops=0, bytes_accessed=2 * child.size * 4, transcendentals=0),
        name="place_child",
    )(in_hbm(col_map), in_hbm(child))


def dot(a, b, contract=((1,), (0,))):
    return lax.dot_general(a, b, (contract, ((), ())), precision=HIGHEST, preferred_element_type=jnp.float32)


def log2(size):
    return size.bit_length() - 1


def update_kernel(
    parts, halves, per, row_tiles, col_tiles, tile,
    front, dinv, pivots, rank_rows, rank_cols, admissible, *rest,
):
    xw = rest[:parts]
    vz = rest[parts : parts + halves]
    out, xs, ts, vs, zs = rest[parts + halves :]
    step = pl.program_id(0)
    chunk = vz[0].shape[1] // tile
    slots = xw[0].shape[0]
    rows = slots * row_tiles

    @pl.when(step == 0)
    def _():
        hot = (lax.broadcasted_iota(jnp.int32, (tile, tile), 0) == pivots[...]).astype(jnp.float32)
        turned = dot(hot, dinv[...])
        zs[...] = jnp.zeros_like(zs)
        for h in range(halves):
            for j in range(col_tiles):
                for p in range(chunk):
                    r = j * RMAX + h * chunk + p
                    span = pl.ds(p * tile, tile)
                    vs[pl.ds(r, 1), :] = vz[h][pl.ds(j, 1), span]
                    zs[pl.ds(r, 1), pl.ds(j * tile, tile)] = vz[h][pl.ds(col_tiles + j, 1), span]
        dv = dot(turned, vs[...], ((1,), (1,)))

        row = lax.broadcasted_iota(jnp.int32, (row_tiles, col_tiles * RMAX), 0)
        lane = lax.broadcasted_iota(jnp.int32, (row_tiles, col_tiles * RMAX), 1)
        top_r, top_s = jnp.zeros_like(row), jnp.zeros_like(row)
        for i in range(row_tiles):
            for j in range(col_tiles):
                here = (row == i) & (lane >> log2(RMAX) == j)
                dense = admissible[i, j] == 0
                top_r = jnp.where(here, jnp.where(dense, RMAX, rank_rows[i]), top_r)
                top_s = jnp.where(here, jnp.where(dense, RMAX, rank_cols[j]), top_s)
        half = (lane & (RMAX - 1)) >> log2(chunk)
        s = ((lax.axis_index("row") ^ half) << log2(chunk)) + (lane & (chunk - 1))
        top_r = jnp.where(s < top_s, top_r, 0)
        top_r = jnp.broadcast_to(top_r[None], (slots,) + top_r.shape).reshape(rows, -1)
        slot = lax.broadcasted_iota(jnp.int32, top_r.shape, 0) >> log2(row_tiles)
        me = group_index()
        for q in range(per):
            span = pl.ds(q * tile, tile)
            for n in range(parts):
                at = pl.ds((q * parts + n) * rows, rows)
                left = xw[n][:, :row_tiles, span].reshape(rows, tile)
                for g in range(tile // LANES):
                    xs[g, at, :] = left[:, g * LANES : (g + 1) * LANES]
                core = dot(xw[n][:, row_tiles:, span].reshape(rows, tile), dv)
                r = (me ^ (slot * parts + n)) * per + q
                kept = jnp.where(r < top_r, core, 0.0)
                right = dot(kept, zs[...])
                for g in range(right.shape[1] // LANES):
                    ts[g, at, :] = right[:, g * LANES : (g + 1) * LANES]

    mine = pl.ds(step, RMAX, stride=row_tiles)
    left = jnp.concatenate([xs[g, mine, :] for g in range(xs.shape[0])], axis=1)
    right = jnp.concatenate([ts[g, mine, :] for g in range(ts.shape[0])], axis=1)
    out[...] = front[...] - dot(left, right, ((0,), (0,)))


def subtract_update(front, dinv, pivots, rank_rows, rank_cols, admissible, xw, vz):
    tile = dinv.shape[0]
    row_tiles = front.shape[0] // tile
    width = front.shape[1]
    col_tiles = width // tile
    per = xw[0].shape[2] // tile
    total = RMAX * row_tiles

    whole = pl.BlockSpec(memory_space=pltpu.VMEM)
    scalars = pl.BlockSpec(memory_space=pltpu.SMEM)
    block = pl.BlockSpec((tile, width), lambda i: (i, 0))
    pivots = pivots.reshape(1, tile)
    return pl.pallas_call(
        functools.partial(update_kernel, len(xw), len(vz), per, row_tiles, col_tiles, tile),
        grid=(row_tiles,),
        out_shape=pltpu.VMEM(front.shape, front.dtype),
        in_specs=[block] + [whole] * 2 + [scalars] * 3 + [whole] * (len(xw) + len(vz)),
        out_specs=block,
        scratch_shapes=[
            pltpu.VMEM((tile // LANES, total, LANES), jnp.float32),
            pltpu.VMEM((width // LANES, total, LANES), jnp.float32),
            pltpu.VMEM((col_tiles * RMAX, tile), jnp.float32),
            pltpu.VMEM((col_tiles * RMAX, width), jnp.float32),
        ],
        compiler_params=pltpu.CompilerParams(vmem_limit_bytes=8 * MIB),
        cost_estimate=pl.CostEstimate(flops=2 * front.size * 256, bytes_accessed=2 * front.size * 4, transcendentals=0),
        name="front_less_update",
    )(in_hbm(front), dinv, pivots, rank_rows, rank_cols, admissible, *xw, *vz)


def add_kernel(members, tile, row_map, base, *rest):
    arrived = rest[: len(members)]
    out, held, sem = rest[-3:]
    me = group_index()
    col_tiles, rows, _ = arrived[0].shape
    per_tile = tile // rows

    def at(n):
        source = me ^ members[n]
        low = row_map[0, source // per_tile] * tile + source % per_tile * rows
        return pl.ds(pl.multiple_of(low, rows), rows)

    def store(n):
        return pltpu.make_async_copy(held.at[n], out.at[at(n), :], sem.at[n])

    for n in range(len(members)):
        for j in range(col_tiles):
            span = pl.ds(j * tile, tile)
            held[n, :, span] = base[at(n), span] + arrived[n][j]
        store(n).start()
    for n in range(len(members)):
        store(n).wait()


def add_child(out, base, arrived, members, row_map, tile):
    rows = arrived[0].shape[1]
    inner = pl.BlockSpec(memory_space=pltpu.VMEM)
    outer = pl.BlockSpec(memory_space=pltpu.HBM)
    size = len(members) * rows * base.shape[1]
    before = [] if out is None else [out]
    return pl.pallas_call(
        functools.partial(add_kernel, members, tile),
        out_shape=pltpu.HBM(base.shape, base.dtype),
        in_specs=[pl.BlockSpec(memory_space=pltpu.SMEM)] + [inner] * (1 + len(members)) + [outer] * len(before),
        out_specs=outer,
        scratch_shapes=[
            pltpu.VMEM((len(members), rows, base.shape[1]), base.dtype),
            pltpu.SemaphoreType.DMA((len(members),)),
        ],
        input_output_aliases={2 + len(members): 0} if before else {},
        compiler_params=pltpu.CompilerParams(vmem_limit_bytes=4 * MIB),
        cost_estimate=pl.CostEstimate(flops=size, bytes_accessed=size * 4, transcendentals=0),
        name="add_child",
    )(in_hbm(row_map), in_vmem(base), *[in_vmem(piece) for piece in arrived], *before)


class Sender:
    def __init__(self):
        self.arrived = []

    def send(self, array, axes, m):
        spot = len(self.arrived) - WINDOW
        if spot >= 0:
            array, self.arrived[spot] = lax.optimization_barrier((array, self.arrived[spot]))
        size = int(np.prod([lax.axis_size(axis) for axis in axes]))
        self.arrived.append(lax.ppermute(array, axes, [(d, d ^ m) for d in range(size)]))
        return len(self.arrived) - 1


def on_device(
    front,
    child,
    row_map,
    col_map,
    x_fac,
    w_fac,
    v_fac,
    z_fac,
    dinv,
    pivots,
    rank_rows,
    rank_cols,
    admissible,
):
    tile = dinv.shape[0]
    row_tiles = front.shape[0] // tile
    col_tiles = front.shape[1] // tile
    devices = lax.axis_size("col") * lax.axis_size("leaf")

    sender = Sender()
    mine = jnp.pad(x_fac, ((0, row_tiles), (0, 0))) + jnp.pad(w_fac, ((row_tiles, 0), (0, 0)))
    mine, child = lax.optimization_barrier((mine, child))
    line = [sender.send(mine, GROUP, m) for m in range(NEAR, devices, NEAR)]
    pieces = place(child, col_map, tile, devices)
    pieces, v_fac, z_fac, rank_rows, rank_cols, admissible = lax.optimization_barrier(
        (pieces, v_fac, z_fac, rank_rows, rank_cols, admissible)
    )

    pieces = list(pieces)
    half = devices // 2
    crossing = list(reversed(range(half, devices)))
    local = [m for pair in zip(reversed(range(NEAR, half)), [3, 2, 1] + [None] * half) for m in pair if m]
    between = [("xw", m) for m in range(1, NEAR)] + [("vz", m) for m in range(1, lax.axis_size("row"))]
    ready = len(between)
    between += [("child", m) for m in local]
    gaps = len(crossing) - 2
    turn = [2 + i * gaps // len(between) for i in range(len(between))]
    update_at = turn[ready - 1] + 2
    order, spots, xw, vz = [0], {0: None}, [], []

    def got(m):
        return pieces[0] if m == 0 else sender.arrived[spots[m]]

    def add(out, members):
        return add_child(out, base, [got(m) for m in members], members, row_map, tile)

    for n, m in enumerate(crossing):
        for i, (kind, other) in enumerate(between):
            if turn[i] == n and kind == "xw":
                if not xw:
                    line = jnp.stack([mine] + [sender.arrived[i] for i in line])
                xw.append(sender.send(line, GROUP, other))
            elif turn[i] == n and kind == "vz":
                if not vz:
                    both = jnp.concatenate([v_fac, z_fac], axis=0)
                vz.append(sender.send(both, ("row",), other))
            elif turn[i] == n:
                spots[other] = sender.send(pieces[other], GROUP, other)
                order.append(other)
        if n == update_at:
            xw = [line] + [sender.arrived[i] for i in xw]
            vz = [both] + [sender.arrived[i] for i in vz]
            base = subtract_update(front, dinv, pivots, rank_rows, rank_cols, admissible, xw, vz)
            base, pieces[m] = lax.optimization_barrier((base, pieces[m]))
        if n == len(crossing) - 1:
            out = add(None, order[: half - 1])
            out, pieces[m] = lax.optimization_barrier((out, pieces[m]))
        spots[m] = sender.send(pieces[m], GROUP, m)
        order.append(m)
    return add(add(out, order[half - 1 : -2]), order[-2:])


def solution(mesh):
    return jax.shard_map(
        on_device,
        mesh=mesh,
        in_specs=(
            P("row", GROUP),
            P(("row", "col", "leaf"), None),
            P("row", None),
            P(),
            P("row", GROUP),
            P("row", GROUP),
            P(GROUP, "row"),
            P(GROUP, "row"),
            P(),
            P(),
            P("row"),
            P(GROUP),
            P("row", GROUP),
        ),
        out_specs=P("row", GROUP),
        check_vma=False,
    )
```

```python
import functools

import jax
import jax.numpy as jnp
import numpy as np
from jax import lax
from jax.experimental import pallas as pl
from jax.experimental.pallas import tpu as pltpu
from jax.sharding import PartitionSpec as P

RMAX = 64
LANES = 128
NEAR = 4
WINDOW = 5
GROUP = ("col", "leaf")
HIGHEST = lax.Precision.HIGHEST
MIB = 1 << 20


def group_index():
    return lax.axis_index("col") * lax.axis_size("leaf") + lax.axis_index("leaf")


def in_hbm(array):
    return pltpu.with_memory_space_constraint(array, pltpu.HBM)


def place_kernel(tiles, groups, tile, col_tiles, col_map, child, *rest):
    pieces = rest[: tiles // col_tiles]
    inverse, held, in_sem, out_sem = rest[tiles // col_tiles :]
    width = tiles // groups * tile
    me = group_index()

    def fetch(g):
        span = pl.ds(g * width, width)
        return pltpu.make_async_copy(child.at[:, span], held.at[:, span], in_sem.at[g])

    def store(m, j):
        b = inverse[(me ^ m) * col_tiles + j]
        span = pl.ds(pl.multiple_of(b * tile, tile), tile)
        return pltpu.make_async_copy(held.at[:, span], pieces[m].at[j], out_sem.at[m, j])

    for g in range(groups):
        fetch(g).start()
    for b in range(tiles):
        inverse[col_map[b]] = b
    for g in range(groups):
        fetch(g).wait()
    order = [(m, j) for m in reversed(range(len(pieces))) for j in range(col_tiles)]
    for m, j in order:
        store(m, j).start()
    for m, j in order:
        store(m, j).wait()


def in_vmem(array):
    return pltpu.with_memory_space_constraint(array, pltpu.VMEM)


def place(child, col_map, tile, devices):
    rows = child.shape[0]
    tiles = col_map.shape[0]
    col_tiles = tiles // devices
    groups = 8
    return pl.pallas_call(
        functools.partial(place_kernel, tiles, groups, tile, col_tiles),
        out_shape=[pltpu.HBM((col_tiles, rows, tile), child.dtype)] * devices,
        in_specs=[pl.BlockSpec(memory_space=pltpu.SMEM), pl.BlockSpec(memory_space=pltpu.HBM)],
        out_specs=[pl.BlockSpec(memory_space=pltpu.HBM)] * devices,
        scratch_shapes=[
            pltpu.SMEM((tiles,), jnp.int32),
            pltpu.VMEM(child.shape, child.dtype),
            pltpu.SemaphoreType.DMA((groups,)),
            pltpu.SemaphoreType.DMA((devices, col_tiles)),
        ],
        compiler_params=pltpu.CompilerParams(vmem_limit_bytes=8 * MIB),
        cost_estimate=pl.CostEstimate(flops=0, bytes_accessed=2 * child.size * 4, transcendentals=0),
        name="place_child",
    )(in_hbm(col_map), in_hbm(child))


def dot(a, b, contract=((1,), (0,))):
    return lax.dot_general(a, b, (contract, ((), ())), precision=HIGHEST, preferred_element_type=jnp.float32)


def log2(size):
    return size.bit_length() - 1


def update_kernel(
    parts, halves, per, row_tiles, col_tiles, tile,
    front, dinv, pivots, rank_rows, rank_cols, admissible, *rest,
):
    xw = rest[:parts]
    vz = rest[parts : parts + halves]
    out, xs, ts, vs, zs = rest[parts + halves :]
    step = pl.program_id(0)
    chunk = vz[0].shape[1] // tile
    slots = xw[0].shape[0]
    rows = slots * row_tiles

    @pl.when(step == 0)
    def _():
        hot = (lax.broadcasted_iota(jnp.int32, (tile, tile), 0) == pivots[...]).astype(jnp.float32)
        turned = dot(hot, dinv[...])
        zs[...] = jnp.zeros_like(zs)
        for h in range(halves):
            for j in range(col_tiles):
                for p in range(chunk):
                    r = j * RMAX + h * chunk + p
                    span = pl.ds(p * tile, tile)
                    vs[pl.ds(r, 1), :] = vz[h][pl.ds(j, 1), span]
                    zs[pl.ds(r, 1), pl.ds(j * tile, tile)] = vz[h][pl.ds(col_tiles + j, 1), span]
        dv = dot(turned, vs[...], ((1,), (1,)))

        row = lax.broadcasted_iota(jnp.int32, (row_tiles, col_tiles * RMAX), 0)
        lane = lax.broadcasted_iota(jnp.int32, (row_tiles, col_tiles * RMAX), 1)
        top_r, top_s = jnp.zeros_like(row), jnp.zeros_like(row)
        for i in range(row_tiles):
            for j in range(col_tiles):
                here = (row == i) & (lane >> log2(RMAX) == j)
                dense = admissible[i, j] == 0
                top_r = jnp.where(here, jnp.where(dense, RMAX, rank_rows[i]), top_r)
                top_s = jnp.where(here, jnp.where(dense, RMAX, rank_cols[j]), top_s)
        half = (lane & (RMAX - 1)) >> log2(chunk)
        s = ((lax.axis_index("row") ^ half) << log2(chunk)) + (lane & (chunk - 1))
        top_r = jnp.where(s < top_s, top_r, 0)
        top_r = jnp.broadcast_to(top_r[None], (slots,) + top_r.shape).reshape(rows, -1)
        slot = lax.broadcasted_iota(jnp.int32, top_r.shape, 0) >> log2(row_tiles)
        me = group_index()
        for q in range(per):
            span = pl.ds(q * tile, tile)
            for n in range(parts):
                at = pl.ds((q * parts + n) * rows, rows)
                left = xw[n][:, :row_tiles, span].reshape(rows, tile)
                for g in range(tile // LANES):
                    xs[g, at, :] = left[:, g * LANES : (g + 1) * LANES]
                core = dot(xw[n][:, row_tiles:, span].reshape(rows, tile), dv)
                r = (me ^ (slot * parts + n)) * per + q
                kept = jnp.where(r < top_r, core, 0.0)
                right = dot(kept, zs[...])
                for g in range(right.shape[1] // LANES):
                    ts[g, at, :] = right[:, g * LANES : (g + 1) * LANES]

    mine = pl.ds(step, RMAX, stride=row_tiles)
    left = jnp.concatenate([xs[g, mine, :] for g in range(xs.shape[0])], axis=1)
    right = jnp.concatenate([ts[g, mine, :] for g in range(ts.shape[0])], axis=1)
    out[...] = front[...] - dot(left, right, ((0,), (0,)))


def subtract_update(front, dinv, pivots, rank_rows, rank_cols, admissible, xw, vz):
    tile = dinv.shape[0]
    row_tiles = front.shape[0] // tile
    width = front.shape[1]
    col_tiles = width // tile
    per = xw[0].shape[2] // tile
    total = RMAX * row_tiles

    whole = pl.BlockSpec(memory_space=pltpu.VMEM)

    def once(array):
        return pl.BlockSpec(array.shape, lambda i: (0,) * array.ndim, pipeline_mode=pl.Buffered(1))

    scalars = pl.BlockSpec(memory_space=pltpu.SMEM)
    block = pl.BlockSpec((tile, width), lambda i: (i, 0))
    pivots = pivots.reshape(1, tile)
    return pl.pallas_call(
        functools.partial(update_kernel, len(xw), len(vz), per, row_tiles, col_tiles, tile),
        grid=(row_tiles,),
        out_shape=pltpu.VMEM(front.shape, front.dtype),
        in_specs=[block] + [whole] * 2 + [scalars] * 3 + [once(array) for array in (*xw, *vz)],
        out_specs=block,
        scratch_shapes=[
            pltpu.VMEM((tile // LANES, total, LANES), jnp.float32),
            pltpu.VMEM((width // LANES, total, LANES), jnp.float32),
            pltpu.VMEM((col_tiles * RMAX, tile), jnp.float32),
            pltpu.VMEM((col_tiles * RMAX, width), jnp.float32),
        ],
        compiler_params=pltpu.CompilerParams(vmem_limit_bytes=8 * MIB),
        cost_estimate=pl.CostEstimate(flops=2 * front.size * 256, bytes_accessed=2 * front.size * 4, transcendentals=0),
        name="front_less_update",
    )(in_hbm(front), dinv, pivots, rank_rows, rank_cols, admissible, *[in_hbm(array) for array in (*xw, *vz)])


def add_kernel(members, tile, row_map, base, *rest):
    arrived = rest[: len(members)]
    out, held, sem = rest[-3:]
    me = group_index()
    col_tiles, rows, _ = arrived[0].shape
    per_tile = tile // rows

    def at(n):
        source = me ^ members[n]
        low = row_map[0, source // per_tile] * tile + source % per_tile * rows
        return pl.ds(pl.multiple_of(low, rows), rows)

    def store(n):
        return pltpu.make_async_copy(held.at[n], out.at[at(n), :], sem.at[n])

    for n in range(len(members)):
        for j in range(col_tiles):
            span = pl.ds(j * tile, tile)
            held[n, :, span] = base[at(n), span] + arrived[n][j]
        store(n).start()
    for n in range(len(members)):
        store(n).wait()


def add_child(out, base, arrived, members, row_map, tile):
    rows = arrived[0].shape[1]
    inner = pl.BlockSpec(memory_space=pltpu.VMEM)
    outer = pl.BlockSpec(memory_space=pltpu.HBM)
    size = len(members) * rows * base.shape[1]
    before = [] if out is None else [out]
    return pl.pallas_call(
        functools.partial(add_kernel, members, tile),
        out_shape=pltpu.HBM(base.shape, base.dtype),
        in_specs=[pl.BlockSpec(memory_space=pltpu.SMEM)] + [inner] * (1 + len(members)) + [outer] * len(before),
        out_specs=outer,
        scratch_shapes=[
            pltpu.VMEM((len(members), rows, base.shape[1]), base.dtype),
            pltpu.SemaphoreType.DMA((len(members),)),
        ],
        input_output_aliases={2 + len(members): 0} if before else {},
        compiler_params=pltpu.CompilerParams(vmem_limit_bytes=4 * MIB),
        cost_estimate=pl.CostEstimate(flops=size, bytes_accessed=size * 4, transcendentals=0),
        name="add_child",
    )(in_hbm(row_map), in_vmem(base), *[in_vmem(piece) for piece in arrived], *before)


class Sender:
    def __init__(self):
        self.arrived = []

    def send(self, array, axes, m):
        spot = len(self.arrived) - WINDOW
        if spot >= 0:
            array, self.arrived[spot] = lax.optimization_barrier((array, self.arrived[spot]))
        size = int(np.prod([lax.axis_size(axis) for axis in axes]))
        self.arrived.append(lax.ppermute(array, axes, [(d, d ^ m) for d in range(size)]))
        return len(self.arrived) - 1


def on_device(
    front,
    child,
    row_map,
    col_map,
    x_fac,
    w_fac,
    v_fac,
    z_fac,
    dinv,
    pivots,
    rank_rows,
    rank_cols,
    admissible,
):
    tile = dinv.shape[0]
    row_tiles = front.shape[0] // tile
    col_tiles = front.shape[1] // tile
    devices = lax.axis_size("col") * lax.axis_size("leaf")

    sender = Sender()
    mine = jnp.pad(x_fac, ((0, row_tiles), (0, 0))) + jnp.pad(w_fac, ((row_tiles, 0), (0, 0)))
    mine, child = lax.optimization_barrier((mine, child))
    line = [sender.send(mine, GROUP, m) for m in range(NEAR, devices, NEAR)]
    pieces = place(child, col_map, tile, devices)
    pieces, v_fac, z_fac, rank_rows, rank_cols, admissible = lax.optimization_barrier(
        (pieces, v_fac, z_fac, rank_rows, rank_cols, admissible)
    )

    pieces = list(pieces)
    half = devices // 2
    crossing = list(reversed(range(half, devices)))
    local = [m for pair in zip(reversed(range(NEAR, half)), [3] + [None] * half) for m in pair if m] + [2, 1]
    factors = [("xw", m) for m in range(1, NEAR)] + [("vz", m) for m in range(1, lax.axis_size("row"))]
    gaps = len(crossing) - 2
    early = gaps * 7 // 6 - len(factors)
    between = factors + [("child", m) for m in local[:early]]
    order, spots, xw, vz = [0], {}, [], []

    def send(m):
        spots[m] = sender.send(pieces[m], GROUP, m)
        order.append(m)

    def add(out, members):
        got = [sender.arrived[spots[m]] if m else pieces[0] for m in members]
        return add_child(out, base, got, members, row_map, tile)

    for n, m in enumerate(crossing):
        for i, (kind, other) in enumerate(between):
            if n == 2 + i * gaps // len(between):
                if kind == "child":
                    send(other)
                elif kind == "xw":
                    if not xw:
                        line = jnp.stack([mine] + [sender.arrived[i] for i in line])
                    xw.append(sender.send(line, GROUP, other))
                else:
                    if not vz:
                        both = jnp.concatenate([v_fac, z_fac], axis=0)
                    vz.append(sender.send(both, ("row",), other))
        send(m)
    xw = [line] + [sender.arrived[i] for i in xw]
    vz = [both] + [sender.arrived[i] for i in vz]
    base = subtract_update(front, dinv, pivots, rank_rows, rank_cols, admissible, xw, vz)
    done = len(order) - WINDOW
    for n, m in enumerate(local[early:]):
        if n == 0:
            base, pieces[m] = lax.optimization_barrier((base, pieces[m]))
        if n == 1:
            out = add(None, order[:done])
            out, pieces[m] = lax.optimization_barrier((out, pieces[m]))
        send(m)
    out = add(out, order[done : done + WINDOW - 1])
    return add(out, order[done + WINDOW - 1 :])


def solution(mesh):
    return jax.shard_map(
        on_device,
        mesh=mesh,
        in_specs=(
            P("row", GROUP),
            P(("row", "col", "leaf"), None),
            P("row", None),
            P(),
            P("row", GROUP),
            P("row", GROUP),
            P(GROUP, "row"),
            P(GROUP, "row"),
            P(),
            P(),
            P("row"),
            P(GROUP),
            P("row", GROUP),
        ),
        out_specs=P("row", GROUP),
        check_vma=False,
    )
```

```python
import functools

import jax
import jax.numpy as jnp
import numpy as np
from jax import lax
from jax.experimental import pallas as pl
from jax.experimental.pallas import tpu as pltpu
from jax.sharding import PartitionSpec as P

RMAX = 64
LANES = 128
NEAR = 4
WINDOW = 5
GROUP = ("col", "leaf")
HIGHEST = lax.Precision.HIGHEST
MIB = 1 << 20


def group_index():
    return lax.axis_index("col") * lax.axis_size("leaf") + lax.axis_index("leaf")


def in_hbm(array):
    return pltpu.with_memory_space_constraint(array, pltpu.HBM)


def place_kernel(tiles, groups, tile, col_tiles, col_map, child, *rest):
    pieces = rest[: tiles // col_tiles]
    inverse, held, in_sem, out_sem = rest[tiles // col_tiles :]
    width = tiles // groups * tile
    me = group_index()

    def fetch(g):
        span = pl.ds(g * width, width)
        return pltpu.make_async_copy(child.at[:, span], held.at[:, span], in_sem.at[g])

    def store(m, j):
        b = inverse[(me ^ m) * col_tiles + j]
        span = pl.ds(pl.multiple_of(b * tile, tile), tile)
        return pltpu.make_async_copy(held.at[:, span], pieces[m].at[j], out_sem.at[m, j])

    for g in range(groups):
        fetch(g).start()
    for b in range(tiles):
        inverse[col_map[b]] = b
    for g in range(groups):
        fetch(g).wait()
    order = [(m, j) for m in reversed(range(len(pieces))) for j in range(col_tiles)]
    for m, j in order:
        store(m, j).start()
    for m, j in order:
        store(m, j).wait()


def in_vmem(array):
    return pltpu.with_memory_space_constraint(array, pltpu.VMEM)


def place(child, col_map, tile, devices):
    rows = child.shape[0]
    tiles = col_map.shape[0]
    col_tiles = tiles // devices
    groups = 8
    return pl.pallas_call(
        functools.partial(place_kernel, tiles, groups, tile, col_tiles),
        out_shape=[pltpu.HBM((col_tiles, rows, tile), child.dtype)] * devices,
        in_specs=[pl.BlockSpec(memory_space=pltpu.SMEM), pl.BlockSpec(memory_space=pltpu.HBM)],
        out_specs=[pl.BlockSpec(memory_space=pltpu.HBM)] * devices,
        scratch_shapes=[
            pltpu.SMEM((tiles,), jnp.int32),
            pltpu.VMEM(child.shape, child.dtype),
            pltpu.SemaphoreType.DMA((groups,)),
            pltpu.SemaphoreType.DMA((devices, col_tiles)),
        ],
        compiler_params=pltpu.CompilerParams(vmem_limit_bytes=8 * MIB),
        cost_estimate=pl.CostEstimate(flops=0, bytes_accessed=2 * child.size * 4, transcendentals=0),
        name="place_child",
    )(in_hbm(col_map), in_hbm(child))


def dot(a, b, contract=((1,), (0,))):
    return lax.dot_general(a, b, (contract, ((), ())), precision=HIGHEST, preferred_element_type=jnp.float32)


def log2(size):
    return size.bit_length() - 1


def factor_kernel(parts, halves, col_tiles, row_tiles, dinv, pivots, rank_rows, rank_cols, admissible, *rest):
    xw = rest[:parts]
    vz = rest[parts : parts + halves]
    left, right, ws, vs, zs = rest[parts + halves :]
    tile = dinv.shape[0]
    per = xw[0].shape[2] // tile
    chunk = vz[0].shape[1] // tile
    slots = xw[0].shape[0]
    rows = slots * row_tiles

    zs[...] = jnp.zeros_like(zs)
    for h in range(halves):
        for j in range(col_tiles):
            for p in range(chunk):
                at = pl.ds(j * RMAX + h * chunk + p, 1)
                span = pl.ds(p * tile, tile)
                vs[at, :] = vz[h][pl.ds(j, 1), span]
                zs[at, pl.ds(j * tile, tile)] = vz[h][pl.ds(col_tiles + j, 1), span]
    for q in range(per):
        for n in range(parts):
            at = pl.ds((q * parts + n) * rows, rows)
            span = pl.ds(q * tile, tile)
            mine = xw[n][:, :row_tiles, span].reshape(rows, tile)
            for g in range(tile // LANES):
                left[g, at, :] = mine[:, g * LANES : (g + 1) * LANES]
            ws[at, :] = xw[n][:, row_tiles:, span].reshape(rows, tile)

    hot = (lax.broadcasted_iota(jnp.int32, (tile, tile), 0) == pivots[...]).astype(jnp.float32)
    dv = dot(dot(hot, dinv[...]), vs[...], ((1,), (1,)))
    core = dot(ws[...], dv)

    row = lax.broadcasted_iota(jnp.int32, (row_tiles, col_tiles * RMAX), 0)
    lane = lax.broadcasted_iota(jnp.int32, (row_tiles, col_tiles * RMAX), 1)
    top_r, top_s = jnp.zeros_like(row), jnp.zeros_like(row)
    for i in range(row_tiles):
        for j in range(col_tiles):
            here = (row == i) & (lane >> log2(RMAX) == j)
            dense = admissible[i, j] == 0
            top_r = jnp.where(here, jnp.where(dense, RMAX, rank_rows[i]), top_r)
            top_s = jnp.where(here, jnp.where(dense, RMAX, rank_cols[j]), top_s)
    half = (lane & (RMAX - 1)) >> log2(chunk)
    s = ((lax.axis_index("row") ^ half) << log2(chunk)) + (lane & (chunk - 1))
    top_r = jnp.where(s < top_s, top_r, 0)
    top_r = jnp.broadcast_to(top_r[None], (RMAX,) + top_r.shape).reshape(core.shape)
    k = lax.broadcasted_iota(jnp.int32, core.shape, 0)
    source = ((k >> log2(row_tiles)) & (slots - 1)) * parts + ((k >> log2(rows)) & (parts - 1))
    r = (group_index() ^ source) * per + (k >> log2(rows * parts))
    product = dot(jnp.where(r < top_r, core, 0.0), zs[...])
    for g in range(right.shape[0]):
        right[g, :, :] = product[:, g * LANES : (g + 1) * LANES]


def factors(dinv, pivots, rank_rows, rank_cols, admissible, xw, vz):
    tile = dinv.shape[0]
    row_tiles, col_tiles = admissible.shape
    total = RMAX * row_tiles
    inner = pl.BlockSpec(memory_space=pltpu.VMEM)
    scalars = pl.BlockSpec(memory_space=pltpu.SMEM)
    return pl.pallas_call(
        functools.partial(factor_kernel, len(xw), len(vz), col_tiles, row_tiles),
        out_shape=[
            pltpu.HBM((tile // LANES, total, LANES), jnp.float32),
            pltpu.HBM((col_tiles * tile // LANES, total, LANES), jnp.float32),
        ],
        in_specs=[inner] * 2 + [scalars] * 3 + [inner] * (len(xw) + len(vz)),
        out_specs=[inner] * 2,
        scratch_shapes=[
            pltpu.VMEM((total, tile), jnp.float32),
            pltpu.VMEM((col_tiles * RMAX, tile), jnp.float32),
            pltpu.VMEM((col_tiles * RMAX, col_tiles * tile), jnp.float32),
        ],
        compiler_params=pltpu.CompilerParams(vmem_limit_bytes=12 * MIB),
        cost_estimate=pl.CostEstimate(flops=2 * total * tile * tile, bytes_accessed=16 * total * tile, transcendentals=0),
        name="update_factors",
    )(dinv, pivots.reshape(1, tile), rank_rows, rank_cols, admissible, *[in_hbm(array) for array in (*xw, *vz)])


def halves_of(array):
    high = array.astype(jnp.bfloat16)
    return high, (array - high.astype(jnp.float32)).astype(jnp.bfloat16)


def finish_kernel(count, tile, row_map, front, left, right, *rest):
    pieces = rest[:count]
    out, held, in_sem, out_sem = rest[count:]
    me = group_index()
    col_tiles, rows, _ = pieces[0].shape
    per_tile = tile // rows
    groups = count // per_tile

    def target(g):
        return row_map[0, lax.div(me ^ (g * per_tile), per_tile)]

    def at(g):
        return pl.ds(pl.multiple_of(target(g) * tile, tile), tile)

    def fetch(g):
        return pltpu.make_async_copy(front.at[at(g), :], held.at[g], in_sem.at[g])

    def store(g):
        return pltpu.make_async_copy(held.at[g], out.at[at(g), :], out_sem.at[g])

    for g in range(groups):
        fetch(g).start()
    for g in range(groups):
        mine = pl.ds(target(g), RMAX, stride=left.shape[1] // RMAX)
        a, b = halves_of(jnp.concatenate([left[n, mine, :] for n in range(left.shape[0])], axis=1))
        c, d = halves_of(jnp.concatenate([right[n, mine, :] for n in range(right.shape[0])], axis=1))
        update = lax.dot_general(
            jnp.concatenate([a, a, b, b], axis=0),
            jnp.concatenate([c, d, c, d], axis=0),
            (((0,), (0,)), ((), ())),
            preferred_element_type=jnp.float32,
        )
        fetch(g).wait()
        held[g] = held[g] - update
        for p in range(per_tile):
            m = g * per_tile + p
            low = pl.ds(pl.multiple_of(lax.rem(me ^ m, per_tile) * rows, rows), rows)
            for j in range(col_tiles):
                span = pl.ds(j * tile, tile)
                held[g, low, span] = held[g, low, span] + pieces[m][j]
        store(g).start()
    for g in range(groups):
        store(g).wait()


def finish(front, left, right, pieces, row_map, tile):
    row_tiles = front.shape[0] // tile
    inner = pl.BlockSpec(memory_space=pltpu.VMEM)
    outer = pl.BlockSpec(memory_space=pltpu.HBM)
    return pl.pallas_call(
        functools.partial(finish_kernel, len(pieces), tile),
        out_shape=pltpu.HBM(front.shape, front.dtype),
        in_specs=[pl.BlockSpec(memory_space=pltpu.SMEM), outer] + [inner] * (2 + len(pieces)),
        out_specs=outer,
        scratch_shapes=[
            pltpu.VMEM((row_tiles, tile, front.shape[1]), front.dtype),
            pltpu.SemaphoreType.DMA((row_tiles,)),
            pltpu.SemaphoreType.DMA((row_tiles,)),
        ],
        compiler_params=pltpu.CompilerParams(vmem_limit_bytes=16 * MIB),
        cost_estimate=pl.CostEstimate(flops=2 * front.size * 256, bytes_accessed=3 * front.size * 4, transcendentals=0),
        name="finish",
    )(in_hbm(row_map), in_hbm(front), left, right, *[in_vmem(piece) for piece in pieces])


class Sender:
    def __init__(self):
        self.arrived = []

    def send(self, array, axes, m):
        spot = len(self.arrived) - WINDOW
        if spot >= 0:
            array, self.arrived[spot] = lax.optimization_barrier((array, self.arrived[spot]))
        size = int(np.prod([lax.axis_size(axis) for axis in axes]))
        self.arrived.append(lax.ppermute(array, axes, [(d, d ^ m) for d in range(size)]))
        return len(self.arrived) - 1


def on_device(
    front,
    child,
    row_map,
    col_map,
    x_fac,
    w_fac,
    v_fac,
    z_fac,
    dinv,
    pivots,
    rank_rows,
    rank_cols,
    admissible,
):
    tile = dinv.shape[0]
    row_tiles = front.shape[0] // tile
    col_tiles = front.shape[1] // tile
    devices = lax.axis_size("col") * lax.axis_size("leaf")

    sender = Sender()
    mine = jnp.pad(x_fac, ((0, row_tiles), (0, 0))) + jnp.pad(w_fac, ((row_tiles, 0), (0, 0)))
    mine, child = lax.optimization_barrier((mine, child))
    line = [sender.send(mine, GROUP, m) for m in range(NEAR, devices, NEAR)]
    pieces = place(child, col_map, tile, devices)
    pieces, v_fac, z_fac, rank_rows, rank_cols, admissible = lax.optimization_barrier(
        (pieces, v_fac, z_fac, rank_rows, rank_cols, admissible)
    )

    pieces = list(pieces)
    half = devices // 2
    crossing = list(reversed(range(half, devices)))
    local = [m for pair in zip(reversed(range(NEAR, half)), [3, 2, 1] + [None] * half) for m in pair if m]
    between = [("xw", m) for m in range(1, NEAR)] + [("vz", m) for m in range(1, lax.axis_size("row"))]
    between += [("child", m) for m in local]
    gaps = len(crossing) - 2
    spots, xw, vz = {}, [], []
    for n, m in enumerate(crossing):
        for i, (kind, other) in enumerate(between):
            if n == 2 + i * gaps // len(between):
                if kind == "child":
                    if other == local[-3]:
                        given = [line] + [sender.arrived[i] for i in xw], [both] + [sender.arrived[i] for i in vz]
                        left, right = factors(dinv, pivots, rank_rows, rank_cols, admissible, *given)
                        left, right, pieces[other] = lax.optimization_barrier((left, right, pieces[other]))
                    spots[other] = sender.send(pieces[other], GROUP, other)
                elif kind == "xw":
                    if not xw:
                        line = jnp.stack([mine] + [sender.arrived[i] for i in line])
                    xw.append(sender.send(line, GROUP, other))
                else:
                    if not vz:
                        both = jnp.concatenate([v_fac, z_fac], axis=0)
                    vz.append(sender.send(both, ("row",), other))
        spots[m] = sender.send(pieces[m], GROUP, m)
    got = [pieces[0]] + [sender.arrived[spots[m]] for m in range(1, devices)]
    return finish(front, left, right, got, row_map, tile)


def solution(mesh):
    return jax.shard_map(
        on_device,
        mesh=mesh,
        in_specs=(
            P("row", GROUP),
            P(("row", "col", "leaf"), None),
            P("row", None),
            P(),
            P("row", GROUP),
            P("row", GROUP),
            P(GROUP, "row"),
            P(GROUP, "row"),
            P(),
            P(),
            P("row"),
            P(GROUP),
            P("row", GROUP),
        ),
        out_specs=P("row", GROUP),
        check_vma=False,
    )
```

```python
import functools

import jax
import jax.numpy as jnp
import numpy as np
from jax import lax
from jax.experimental import pallas as pl
from jax.experimental.pallas import tpu as pltpu
from jax.sharding import PartitionSpec as P

RMAX = 64
LANES = 128
NEAR = 4
WINDOW = 5
GROUP = ("col", "leaf")
HIGHEST = lax.Precision.HIGHEST
MIB = 1 << 20


def group_index():
    return lax.axis_index("col") * lax.axis_size("leaf") + lax.axis_index("leaf")


def in_hbm(array):
    return pltpu.with_memory_space_constraint(array, pltpu.HBM)


def place_kernel(members, tiles, tile, col_tiles, col_map, child, *rest):
    pieces = rest[: len(members)]
    inverse, held, in_sem, out_sem = rest[len(members) :]
    me = group_index()

    def fetch(n, j):
        b = inverse[(me ^ members[n]) * col_tiles + j]
        span = pl.ds(pl.multiple_of(b * tile, tile), tile)
        return pltpu.make_async_copy(child.at[:, span], held.at[n, j], in_sem.at[n, j])

    def store(n):
        return pltpu.make_async_copy(held.at[n], pieces[n], out_sem.at[n])

    for b in range(tiles):
        inverse[col_map[b]] = b
    for n in range(len(members)):
        for j in range(col_tiles):
            fetch(n, j).start()
    for n in range(len(members)):
        for j in range(col_tiles):
            fetch(n, j).wait()
        store(n).start()
    for n in range(len(members)):
        store(n).wait()


def in_vmem(array):
    return pltpu.with_memory_space_constraint(array, pltpu.VMEM)


def place(child, col_map, tile, devices, members):
    rows = child.shape[0]
    tiles = col_map.shape[0]
    col_tiles = tiles // devices
    count = len(members)
    pieces = pl.pallas_call(
        functools.partial(place_kernel, members, tiles, tile, col_tiles),
        out_shape=[pltpu.HBM((col_tiles, rows, tile), child.dtype)] * count,
        in_specs=[pl.BlockSpec(memory_space=pltpu.SMEM), pl.BlockSpec(memory_space=pltpu.HBM)],
        out_specs=[pl.BlockSpec(memory_space=pltpu.HBM)] * count,
        scratch_shapes=[
            pltpu.SMEM((tiles,), jnp.int32),
            pltpu.VMEM((count, col_tiles, rows, tile), child.dtype),
            pltpu.SemaphoreType.DMA((count, col_tiles)),
            pltpu.SemaphoreType.DMA((count,)),
        ],
        compiler_params=pltpu.CompilerParams(vmem_limit_bytes=6 * MIB),
        cost_estimate=pl.CostEstimate(flops=0, bytes_accessed=child.size * 4, transcendentals=0),
        name="place_child",
    )(in_hbm(col_map), in_hbm(child))
    return dict(zip(members, pieces))


def dot(a, b, contract=((1,), (0,))):
    return lax.dot_general(a, b, (contract, ((), ())), precision=HIGHEST, preferred_element_type=jnp.float32)


def log2(size):
    return size.bit_length() - 1


def factor_kernel(parts, halves, col_tiles, row_tiles, dinv, pivots, rank_rows, rank_cols, admissible, *rest):
    xw = rest[:parts]
    vz = rest[parts : parts + halves]
    left, right, ws, vs, zs = rest[parts + halves :]
    tile = dinv.shape[0]
    per = xw[0].shape[2] // tile
    chunk = vz[0].shape[1] // tile
    slots = xw[0].shape[0]
    rows = slots * row_tiles

    zs[...] = jnp.zeros_like(zs)
    for h in range(halves):
        for j in range(col_tiles):
            for p in range(chunk):
                at = pl.ds(j * RMAX + h * chunk + p, 1)
                span = pl.ds(p * tile, tile)
                vs[at, :] = vz[h][pl.ds(j, 1), span]
                zs[at, pl.ds(j * tile, tile)] = vz[h][pl.ds(col_tiles + j, 1), span]
    for q in range(per):
        for n in range(parts):
            at = pl.ds((q * parts + n) * rows, rows)
            span = pl.ds(q * tile, tile)
            mine = xw[n][:, :row_tiles, span].reshape(rows, tile)
            for g in range(tile // LANES):
                left[g, at, :] = mine[:, g * LANES : (g + 1) * LANES]
            ws[at, :] = xw[n][:, row_tiles:, span].reshape(rows, tile)

    hot = (lax.broadcasted_iota(jnp.int32, (tile, tile), 0) == pivots[...]).astype(jnp.float32)
    dv = dot(dot(hot, dinv[...]), vs[...], ((1,), (1,)))
    core = dot(ws[...], dv)

    row = lax.broadcasted_iota(jnp.int32, (row_tiles, col_tiles * RMAX), 0)
    lane = lax.broadcasted_iota(jnp.int32, (row_tiles, col_tiles * RMAX), 1)
    top_r, top_s = jnp.zeros_like(row), jnp.zeros_like(row)
    for i in range(row_tiles):
        for j in range(col_tiles):
            here = (row == i) & (lane >> log2(RMAX) == j)
            dense = admissible[i, j] == 0
            top_r = jnp.where(here, jnp.where(dense, RMAX, rank_rows[i]), top_r)
            top_s = jnp.where(here, jnp.where(dense, RMAX, rank_cols[j]), top_s)
    half = (lane & (RMAX - 1)) >> log2(chunk)
    s = ((lax.axis_index("row") ^ half) << log2(chunk)) + (lane & (chunk - 1))
    top_r = jnp.where(s < top_s, top_r, 0)
    top_r = jnp.broadcast_to(top_r[None], (RMAX,) + top_r.shape).reshape(core.shape)
    k = lax.broadcasted_iota(jnp.int32, core.shape, 0)
    source = ((k >> log2(row_tiles)) & (slots - 1)) * parts + ((k >> log2(rows)) & (parts - 1))
    r = (group_index() ^ source) * per + (k >> log2(rows * parts))
    product = dot(jnp.where(r < top_r, core, 0.0), zs[...])
    for g in range(right.shape[0]):
        right[g, :, :] = product[:, g * LANES : (g + 1) * LANES]


def factors(dinv, pivots, rank_rows, rank_cols, admissible, xw, vz):
    tile = dinv.shape[0]
    row_tiles, col_tiles = admissible.shape
    total = RMAX * row_tiles
    inner = pl.BlockSpec(memory_space=pltpu.VMEM)
    scalars = pl.BlockSpec(memory_space=pltpu.SMEM)
    return pl.pallas_call(
        functools.partial(factor_kernel, len(xw), len(vz), col_tiles, row_tiles),
        out_shape=[
            pltpu.VMEM((tile // LANES, total, LANES), jnp.float32),
            pltpu.VMEM((col_tiles * tile // LANES, total, LANES), jnp.float32),
        ],
        in_specs=[inner] * 2 + [scalars] * 3 + [inner] * (len(xw) + len(vz)),
        out_specs=[inner] * 2,
        scratch_shapes=[
            pltpu.VMEM((total, tile), jnp.float32),
            pltpu.VMEM((col_tiles * RMAX, tile), jnp.float32),
            pltpu.VMEM((col_tiles * RMAX, col_tiles * tile), jnp.float32),
        ],
        compiler_params=pltpu.CompilerParams(vmem_limit_bytes=12 * MIB),
        cost_estimate=pl.CostEstimate(flops=2 * total * tile * tile, bytes_accessed=16 * total * tile, transcendentals=0),
        name="update_factors",
    )(dinv, pivots.reshape(1, tile), rank_rows, rank_cols, admissible, *[in_hbm(array) for array in (*xw, *vz)])


def halves_of(array):
    high = array.astype(jnp.bfloat16)
    return high, (array - high.astype(jnp.float32)).astype(jnp.bfloat16)


def finish_kernel(count, tile, row_map, front, left, right, *rest):
    own, out, held, kept, in_sem, out_sem, own_sem = rest[count - 1 :]
    pieces = (kept, *rest[: count - 1])
    me = group_index()
    col_tiles, rows, _ = kept.shape
    per_tile = tile // rows
    groups = count // per_tile

    def target(g):
        return row_map[0, lax.div(me ^ (g * per_tile), per_tile)]

    def at(g):
        return pl.ds(pl.multiple_of(target(g) * tile, tile), tile)

    def fetch(g):
        return pltpu.make_async_copy(front.at[at(g), :], held.at[g], in_sem.at[g])

    def store(g):
        return pltpu.make_async_copy(held.at[g], out.at[at(g), :], out_sem.at[g])

    fetch_own = pltpu.make_async_copy(own, kept, own_sem)
    fetch_own.start()
    for g in range(groups):
        fetch(g).start()
    fetch_own.wait()
    for g in range(groups):
        mine = pl.ds(target(g), RMAX, stride=left.shape[1] // RMAX)
        a, b = halves_of(jnp.concatenate([left[n, mine, :] for n in range(left.shape[0])], axis=1))
        c, d = halves_of(jnp.concatenate([right[n, mine, :] for n in range(right.shape[0])], axis=1))
        update = lax.dot_general(
            jnp.concatenate([a, a, b, b], axis=0),
            jnp.concatenate([c, d, c, d], axis=0),
            (((0,), (0,)), ((), ())),
            preferred_element_type=jnp.float32,
        )
        fetch(g).wait()
        held[g] = held[g] - update
        for p in range(per_tile):
            m = g * per_tile + p
            low = pl.ds(pl.multiple_of(lax.rem(me ^ m, per_tile) * rows, rows), rows)
            for j in range(col_tiles):
                span = pl.ds(j * tile, tile)
                held[g, low, span] = held[g, low, span] + pieces[m][j]
        store(g).start()
    for g in range(groups):
        store(g).wait()


def finish(front, left, right, pieces, row_map, tile):
    row_tiles = front.shape[0] // tile
    inner = pl.BlockSpec(memory_space=pltpu.VMEM)
    outer = pl.BlockSpec(memory_space=pltpu.HBM)
    return pl.pallas_call(
        functools.partial(finish_kernel, len(pieces), tile),
        out_shape=pltpu.HBM(front.shape, front.dtype),
        in_specs=[pl.BlockSpec(memory_space=pltpu.SMEM), outer] + [inner] * (1 + len(pieces)) + [outer],
        out_specs=outer,
        scratch_shapes=[
            pltpu.VMEM((row_tiles, tile, front.shape[1]), front.dtype),
            pltpu.VMEM(pieces[0].shape, front.dtype),
            pltpu.SemaphoreType.DMA((row_tiles,)),
            pltpu.SemaphoreType.DMA((row_tiles,)),
            pltpu.SemaphoreType.DMA,
        ],
        compiler_params=pltpu.CompilerParams(vmem_limit_bytes=16 * MIB),
        cost_estimate=pl.CostEstimate(flops=2 * front.size * 256, bytes_accessed=3 * front.size * 4, transcendentals=0),
        name="finish",
    )(
        in_hbm(row_map), in_hbm(front), in_vmem(left), in_vmem(right), *[in_vmem(piece) for piece in pieces[1:]], in_hbm(pieces[0])
    )


class Sender:
    def __init__(self):
        self.arrived = []

    def send(self, array, axes, m):
        spot = len(self.arrived) - WINDOW
        if spot >= 0:
            array, self.arrived[spot] = lax.optimization_barrier((array, self.arrived[spot]))
        size = int(np.prod([lax.axis_size(axis) for axis in axes]))
        self.arrived.append(lax.ppermute(array, axes, [(d, d ^ m) for d in range(size)]))
        return len(self.arrived) - 1


def on_device(
    front,
    child,
    row_map,
    col_map,
    x_fac,
    w_fac,
    v_fac,
    z_fac,
    dinv,
    pivots,
    rank_rows,
    rank_cols,
    admissible,
):
    tile = dinv.shape[0]
    row_tiles = front.shape[0] // tile
    col_tiles = front.shape[1] // tile
    devices = lax.axis_size("col") * lax.axis_size("leaf")

    sender = Sender()
    spots = {}

    def send(m):
        spots[m] = sender.send(pieces[m], GROUP, m)

    def arrivals(own, chosen):
        return [own] + [sender.arrived[i] for i in chosen]

    half = devices // 2
    crossing = list(reversed(range(half, devices)))
    local = [m for pair in zip(reversed(range(NEAR, half)), [3, 2, 1] + [None] * half) for m in pair if m]
    mine = jnp.pad(x_fac, ((0, row_tiles), (0, 0))) + jnp.pad(w_fac, ((row_tiles, 0), (0, 0)))
    mine, child = lax.optimization_barrier((mine, child))
    first = [sender.send(mine, GROUP, m) for m in range(NEAR, devices, NEAR)]
    pieces = place(child, col_map, tile, devices, crossing)
    pieces, child, v_fac, z_fac = lax.optimization_barrier((pieces, child, v_fac, z_fac))
    for m in crossing[:2]:
        send(m)
    pieces.update(place(child, col_map, tile, devices, [*local, 0]))

    between = [("xw", m) for m in range(1, NEAR)] + [("vz", m) for m in range(1, lax.axis_size("row"))]
    between += [("child", m) for m in local]
    gaps = len(crossing) - 2
    xw, vz = [], []
    for n, m in enumerate(crossing[2:]):
        for i, (kind, other) in enumerate(between):
            if n == i * gaps // len(between):
                if kind == "child":
                    if other == local[-3]:
                        given = arrivals(line, xw), arrivals(both, vz)
                        left, right = factors(dinv, pivots, rank_rows, rank_cols, admissible, *given)
                        left, right, pieces[other] = lax.optimization_barrier((left, right, pieces[other]))
                    send(other)
                elif kind == "xw":
                    if not xw:
                        line = jnp.stack(arrivals(mine, first))
                    xw.append(sender.send(line, GROUP, other))
                else:
                    if not vz:
                        both = jnp.concatenate([v_fac, z_fac], axis=0)
                    vz.append(sender.send(both, ("row",), other))
        send(m)
    got = arrivals(pieces[0], [spots[m] for m in range(1, devices)])
    return finish(front, left, right, got, row_map, tile)


def solution(mesh):
    return jax.shard_map(
        on_device,
        mesh=mesh,
        in_specs=(
            P("row", GROUP),
            P(("row", "col", "leaf"), None),
            P("row", None),
            P(),
            P("row", GROUP),
            P("row", GROUP),
            P(GROUP, "row"),
            P(GROUP, "row"),
            P(),
            P(),
            P("row"),
            P(GROUP),
            P("row", GROUP),
        ),
        out_specs=P("row", GROUP),
        check_vma=False,
    )
```

```python
import functools

import jax
import jax.numpy as jnp
import numpy as np
from jax import lax
from jax.experimental import pallas as pl
from jax.experimental.pallas import tpu as pltpu
from jax.sharding import PartitionSpec as P

RMAX = 64
LANES = 128
NEAR = 4
WINDOW = 5
GROUP = ("col", "leaf")
HIGHEST = lax.Precision.HIGHEST
MIB = 1 << 20


def group_index():
    return lax.axis_index("col") * lax.axis_size("leaf") + lax.axis_index("leaf")


def in_hbm(array):
    return pltpu.with_memory_space_constraint(array, pltpu.HBM)


def place_kernel(tiles, groups, tile, col_tiles, col_map, child, *rest):
    pieces = rest[: tiles // col_tiles]
    inverse, held, in_sem, out_sem = rest[tiles // col_tiles :]
    width = tiles // groups * tile
    me = group_index()

    def fetch(g):
        span = pl.ds(g * width, width)
        return pltpu.make_async_copy(child.at[:, span], held.at[:, span], in_sem.at[g])

    def store(m, j):
        b = inverse[(me ^ m) * col_tiles + j]
        span = pl.ds(pl.multiple_of(b * tile, tile), tile)
        return pltpu.make_async_copy(held.at[:, span], pieces[m].at[j], out_sem.at[m, j])

    for g in range(groups):
        fetch(g).start()
    for b in range(tiles):
        inverse[col_map[b]] = b
    for g in range(groups):
        fetch(g).wait()
    order = [(m, j) for m in reversed(range(len(pieces))) for j in range(col_tiles)]
    for m, j in order:
        store(m, j).start()
    for m, j in order:
        store(m, j).wait()


def in_vmem(array):
    return pltpu.with_memory_space_constraint(array, pltpu.VMEM)


def place(child, col_map, tile, devices):
    rows = child.shape[0]
    tiles = col_map.shape[0]
    col_tiles = tiles // devices
    groups = 8
    return pl.pallas_call(
        functools.partial(place_kernel, tiles, groups, tile, col_tiles),
        out_shape=[pltpu.HBM((col_tiles, rows, tile), child.dtype)] * devices,
        in_specs=[pl.BlockSpec(memory_space=pltpu.SMEM), pl.BlockSpec(memory_space=pltpu.HBM)],
        out_specs=[pl.BlockSpec(memory_space=pltpu.HBM)] * devices,
        scratch_shapes=[
            pltpu.SMEM((tiles,), jnp.int32),
            pltpu.VMEM(child.shape, child.dtype),
            pltpu.SemaphoreType.DMA((groups,)),
            pltpu.SemaphoreType.DMA((devices, col_tiles)),
        ],
        compiler_params=pltpu.CompilerParams(vmem_limit_bytes=8 * MIB),
        cost_estimate=pl.CostEstimate(flops=0, bytes_accessed=2 * child.size * 4, transcendentals=0),
        name="place_child",
    )(in_hbm(col_map), in_hbm(child))


def dot(a, b, contract=((1,), (0,))):
    return lax.dot_general(a, b, (contract, ((), ())), precision=HIGHEST, preferred_element_type=jnp.float32)


def log2(size):
    return size.bit_length() - 1


def factor_kernel(parts, halves, col_tiles, row_tiles, dinv, pivots, rank_rows, rank_cols, admissible, *rest):
    xw = rest[:parts]
    vz = rest[parts : parts + halves]
    left, right, ws, vs, zs = rest[parts + halves :]
    tile = dinv.shape[0]
    per = xw[0].shape[2] // tile
    chunk = vz[0].shape[1] // tile
    slots = xw[0].shape[0]
    rows = slots * row_tiles

    zs[...] = jnp.zeros_like(zs)
    for h in range(halves):
        for j in range(col_tiles):
            for p in range(chunk):
                at = pl.ds(j * RMAX + h * chunk + p, 1)
                span = pl.ds(p * tile, tile)
                vs[at, :] = vz[h][pl.ds(j, 1), span]
                zs[at, pl.ds(j * tile, tile)] = vz[h][pl.ds(col_tiles + j, 1), span]
    for q in range(per):
        for n in range(parts):
            at = pl.ds((q * parts + n) * rows, rows)
            span = pl.ds(q * tile, tile)
            mine = xw[n][:, :row_tiles, span].reshape(rows, tile)
            for g in range(tile // LANES):
                left[g, at, :] = mine[:, g * LANES : (g + 1) * LANES]
            ws[at, :] = xw[n][:, row_tiles:, span].reshape(rows, tile)

    hot = (lax.broadcasted_iota(jnp.int32, (tile, tile), 0) == pivots[...]).astype(jnp.float32)
    dv = dot(dot(hot, dinv[...]), vs[...], ((1,), (1,)))
    core = dot(ws[...], dv)

    row = lax.broadcasted_iota(jnp.int32, (row_tiles, col_tiles * RMAX), 0)
    lane = lax.broadcasted_iota(jnp.int32, (row_tiles, col_tiles * RMAX), 1)
    top_r, top_s = jnp.zeros_like(row), jnp.zeros_like(row)
    for i in range(row_tiles):
        for j in range(col_tiles):
            here = (row == i) & (lane >> log2(RMAX) == j)
            dense = admissible[i, j] == 0
            top_r = jnp.where(here, jnp.where(dense, RMAX, rank_rows[i]), top_r)
            top_s = jnp.where(here, jnp.where(dense, RMAX, rank_cols[j]), top_s)
    half = (lane & (RMAX - 1)) >> log2(chunk)
    s = ((lax.axis_index("row") ^ half) << log2(chunk)) + (lane & (chunk - 1))
    top_r = jnp.where(s < top_s, top_r, 0)
    top_r = jnp.broadcast_to(top_r[None], (RMAX,) + top_r.shape).reshape(core.shape)
    k = lax.broadcasted_iota(jnp.int32, core.shape, 0)
    source = ((k >> log2(row_tiles)) & (slots - 1)) * parts + ((k >> log2(rows)) & (parts - 1))
    r = (group_index() ^ source) * per + (k >> log2(rows * parts))
    product = dot(jnp.where(r < top_r, core, 0.0), zs[...])
    for g in range(right.shape[0]):
        right[g, :, :] = product[:, g * LANES : (g + 1) * LANES]


def factors(dinv, pivots, rank_rows, rank_cols, admissible, xw, vz):
    tile = dinv.shape[0]
    row_tiles, col_tiles = admissible.shape
    total = RMAX * row_tiles
    inner = pl.BlockSpec(memory_space=pltpu.VMEM)
    scalars = pl.BlockSpec(memory_space=pltpu.SMEM)
    return pl.pallas_call(
        functools.partial(factor_kernel, len(xw), len(vz), col_tiles, row_tiles),
        out_shape=[
            pltpu.VMEM((tile // LANES, total, LANES), jnp.float32),
            pltpu.VMEM((col_tiles * tile // LANES, total, LANES), jnp.float32),
        ],
        in_specs=[inner] * 2 + [scalars] * 3 + [inner] * (len(xw) + len(vz)),
        out_specs=[inner] * 2,
        scratch_shapes=[
            pltpu.VMEM((total, tile), jnp.float32),
            pltpu.VMEM((col_tiles * RMAX, tile), jnp.float32),
            pltpu.VMEM((col_tiles * RMAX, col_tiles * tile), jnp.float32),
        ],
        compiler_params=pltpu.CompilerParams(vmem_limit_bytes=12 * MIB),
        cost_estimate=pl.CostEstimate(flops=2 * total * tile * tile, bytes_accessed=16 * total * tile, transcendentals=0),
        name="update_factors",
    )(dinv, pivots.reshape(1, tile), rank_rows, rank_cols, admissible, *[in_hbm(array) for array in (*xw, *vz)])


def halves_of(array):
    high = array.astype(jnp.bfloat16)
    return high, (array - high.astype(jnp.float32)).astype(jnp.bfloat16)


def finish_kernel(count, tile, row_map, front, left, right, *rest):
    own, out, held, kept, in_sem, out_sem, own_sem = rest[count - 1 :]
    pieces = (kept, *rest[: count - 1])
    me = group_index()
    col_tiles, rows, _ = kept.shape
    per_tile = tile // rows
    groups = count // per_tile

    def target(g):
        return row_map[0, lax.div(me ^ (g * per_tile), per_tile)]

    def at(g):
        return pl.ds(pl.multiple_of(target(g) * tile, tile), tile)

    def fetch(g):
        return pltpu.make_async_copy(front.at[at(g), :], held.at[g], in_sem.at[g])

    def store(g):
        return pltpu.make_async_copy(held.at[g], out.at[at(g), :], out_sem.at[g])

    fetch_own = pltpu.make_async_copy(own, kept, own_sem)
    for g in reversed(range(groups)):
        fetch(g).start()
    fetch_own.start()
    for g in reversed(range(groups)):
        mine = pl.ds(target(g), RMAX, stride=left.shape[1] // RMAX)
        a, b = halves_of(jnp.concatenate([left[n, mine, :] for n in range(left.shape[0])], axis=1))
        c, d = halves_of(jnp.concatenate([right[n, mine, :] for n in range(right.shape[0])], axis=1))
        update = lax.dot_general(
            jnp.concatenate([a, a, b, b], axis=0),
            jnp.concatenate([c, d, c, d], axis=0),
            (((0,), (0,)), ((), ())),
            preferred_element_type=jnp.float32,
        )
        fetch(g).wait()
        held[g] = held[g] - update
        for p in range(per_tile):
            m = g * per_tile + p
            if m == 0:
                fetch_own.wait()
            low = pl.ds(pl.multiple_of(lax.rem(me ^ m, per_tile) * rows, rows), rows)
            for j in range(col_tiles):
                span = pl.ds(j * tile, tile)
                held[g, low, span] = held[g, low, span] + pieces[m][j]
        store(g).start()
    for g in range(groups):
        store(g).wait()


def finish(front, left, right, pieces, row_map, tile):
    row_tiles = front.shape[0] // tile
    inner = pl.BlockSpec(memory_space=pltpu.VMEM)
    outer = pl.BlockSpec(memory_space=pltpu.HBM)
    return pl.pallas_call(
        functools.partial(finish_kernel, len(pieces), tile),
        out_shape=pltpu.HBM(front.shape, front.dtype),
        in_specs=[pl.BlockSpec(memory_space=pltpu.SMEM), outer] + [inner] * (1 + len(pieces)) + [outer],
        out_specs=outer,
        scratch_shapes=[
            pltpu.VMEM((row_tiles, tile, front.shape[1]), front.dtype),
            pltpu.VMEM(pieces[0].shape, front.dtype),
            pltpu.SemaphoreType.DMA((row_tiles,)),
            pltpu.SemaphoreType.DMA((row_tiles,)),
            pltpu.SemaphoreType.DMA,
        ],
        compiler_params=pltpu.CompilerParams(vmem_limit_bytes=16 * MIB),
        cost_estimate=pl.CostEstimate(flops=2 * front.size * 256, bytes_accessed=3 * front.size * 4, transcendentals=0),
        name="finish",
    )(
        in_hbm(row_map), in_hbm(front), in_vmem(left), in_vmem(right), *[in_vmem(piece) for piece in pieces[1:]], in_hbm(pieces[0])
    )


class Sender:
    def __init__(self):
        self.arrived = []

    def send(self, array, axes, m):
        spot = len(self.arrived) - WINDOW
        if spot >= 0:
            array, self.arrived[spot] = lax.optimization_barrier((array, self.arrived[spot]))
        size = int(np.prod([lax.axis_size(axis) for axis in axes]))
        self.arrived.append(lax.ppermute(array, axes, [(d, d ^ m) for d in range(size)]))
        return len(self.arrived) - 1


def on_device(
    front,
    child,
    row_map,
    col_map,
    x_fac,
    w_fac,
    v_fac,
    z_fac,
    dinv,
    pivots,
    rank_rows,
    rank_cols,
    admissible,
):
    tile = dinv.shape[0]
    row_tiles = front.shape[0] // tile
    col_tiles = front.shape[1] // tile
    devices = lax.axis_size("col") * lax.axis_size("leaf")

    sender = Sender()
    mine = jnp.pad(x_fac, ((0, row_tiles), (0, 0))) + jnp.pad(w_fac, ((row_tiles, 0), (0, 0)))
    mine, child = lax.optimization_barrier((mine, child))
    line = [sender.send(mine, GROUP, m) for m in range(NEAR, devices, NEAR)]
    pieces = place(child, col_map, tile, devices)
    pieces, v_fac, z_fac, rank_rows, rank_cols, admissible = lax.optimization_barrier(
        (pieces, v_fac, z_fac, rank_rows, rank_cols, admissible)
    )

    pieces = list(pieces)
    half = devices // 2
    crossing = list(reversed(range(half, devices)))
    local = [m for pair in zip(reversed(range(NEAR, half)), [3, 2, 1] + [None] * half) for m in pair if m]
    between = [("xw", m) for m in range(1, NEAR)] + [("vz", m) for m in range(1, lax.axis_size("row"))]
    between += [("child", m) for m in local]
    gaps = len(crossing) - 2
    spots, xw, vz = {}, [], []
    for n, m in enumerate(crossing):
        for i, (kind, other) in enumerate(between):
            if n == 2 + i * gaps // len(between):
                if kind == "child":
                    if other == local[-3]:
                        given = [line] + [sender.arrived[i] for i in xw], [both] + [sender.arrived[i] for i in vz]
                        left, right = factors(dinv, pivots, rank_rows, rank_cols, admissible, *given)
                        left, right, pieces[other] = lax.optimization_barrier((left, right, pieces[other]))
                    spots[other] = sender.send(pieces[other], GROUP, other)
                elif kind == "xw":
                    if not xw:
                        line = jnp.stack([mine] + [sender.arrived[i] for i in line])
                    xw.append(sender.send(line, GROUP, other))
                else:
                    if not vz:
                        both = jnp.concatenate([v_fac, z_fac], axis=0)
                    vz.append(sender.send(both, ("row",), other))
        spots[m] = sender.send(pieces[m], GROUP, m)
    got = [pieces[0]] + [sender.arrived[spots[m]] for m in range(1, devices)]
    return finish(front, left, right, got, row_map, tile)


def solution(mesh):
    return jax.shard_map(
        on_device,
        mesh=mesh,
        in_specs=(
            P("row", GROUP),
            P(("row", "col", "leaf"), None),
            P("row", None),
            P(),
            P("row", GROUP),
            P("row", GROUP),
            P(GROUP, "row"),
            P(GROUP, "row"),
            P(),
            P(),
            P("row"),
            P(GROUP),
            P("row", GROUP),
        ),
        out_specs=P("row", GROUP),
        check_vma=False,
    )
```

```python
import functools

import jax
import jax.numpy as jnp
import numpy as np
from jax import lax
from jax.experimental import pallas as pl
from jax.experimental.pallas import tpu as pltpu
from jax.sharding import PartitionSpec as P

RMAX = 64
LANES = 128
NEAR = 4
WINDOW = 5
GROUP = ("col", "leaf")
HIGHEST = lax.Precision.HIGHEST
MIB = 1 << 20


def group_index():
    return lax.axis_index("col") * lax.axis_size("leaf") + lax.axis_index("leaf")


def in_hbm(array):
    return pltpu.with_memory_space_constraint(array, pltpu.HBM)


def place_kernel(tiles, groups, tile, col_tiles, col_map, child, *rest):
    pieces = rest[: tiles // col_tiles]
    inverse, held, in_sem, out_sem = rest[tiles // col_tiles :]
    width = tiles // groups * tile
    me = group_index()

    def fetch(g):
        span = pl.ds(g * width, width)
        return pltpu.make_async_copy(child.at[:, span], held.at[:, span], in_sem.at[g])

    def store(m, j):
        b = inverse[(me ^ m) * col_tiles + j]
        span = pl.ds(pl.multiple_of(b * tile, tile), tile)
        return pltpu.make_async_copy(held.at[:, span], pieces[m].at[j], out_sem.at[m, j])

    for g in range(groups):
        fetch(g).start()
    for b in range(tiles):
        inverse[col_map[b]] = b
    for g in range(groups):
        fetch(g).wait()
    order = [(m, j) for m in reversed(range(len(pieces))) for j in range(col_tiles)]
    for m, j in order:
        store(m, j).start()
    for m, j in order:
        store(m, j).wait()


def in_vmem(array):
    return pltpu.with_memory_space_constraint(array, pltpu.VMEM)


def place(child, col_map, tile, devices):
    rows = child.shape[0]
    tiles = col_map.shape[0]
    col_tiles = tiles // devices
    groups = 8
    return pl.pallas_call(
        functools.partial(place_kernel, tiles, groups, tile, col_tiles),
        out_shape=[pltpu.HBM((col_tiles, rows, tile), child.dtype)] * devices,
        in_specs=[pl.BlockSpec(memory_space=pltpu.SMEM), pl.BlockSpec(memory_space=pltpu.HBM)],
        out_specs=[pl.BlockSpec(memory_space=pltpu.HBM)] * devices,
        scratch_shapes=[
            pltpu.SMEM((tiles,), jnp.int32),
            pltpu.VMEM(child.shape, child.dtype),
            pltpu.SemaphoreType.DMA((groups,)),
            pltpu.SemaphoreType.DMA((devices, col_tiles)),
        ],
        compiler_params=pltpu.CompilerParams(vmem_limit_bytes=8 * MIB),
        cost_estimate=pl.CostEstimate(flops=0, bytes_accessed=2 * child.size * 4, transcendentals=0),
        name="place_child",
    )(in_hbm(col_map), in_hbm(child))


def dot(a, b, contract=((1,), (0,))):
    return lax.dot_general(a, b, (contract, ((), ())), precision=HIGHEST, preferred_element_type=jnp.float32)


def log2(size):
    return size.bit_length() - 1


def factor_kernel(parts, halves, col_tiles, row_tiles, dinv, pivots, rank_rows, rank_cols, admissible, *rest):
    xw = rest[:parts]
    vz = rest[parts : parts + halves]
    left, right, ws, vs, zs = rest[parts + halves :]
    tile = dinv.shape[0]
    per = xw[0].shape[2] // tile
    chunk = vz[0].shape[1] // tile
    slots = xw[0].shape[0]
    rows = slots * row_tiles

    zs[...] = jnp.zeros_like(zs)
    for h in range(halves):
        for j in range(col_tiles):
            for p in range(chunk):
                at = pl.ds(j * RMAX + h * chunk + p, 1)
                span = pl.ds(p * tile, tile)
                vs[at, :] = vz[h][pl.ds(j, 1), span]
                zs[at, pl.ds(j * tile, tile)] = vz[h][pl.ds(col_tiles + j, 1), span]
    for q in range(per):
        for n in range(parts):
            at = pl.ds((q * parts + n) * rows, rows)
            span = pl.ds(q * tile, tile)
            mine = xw[n][:, :row_tiles, span].reshape(rows, tile)
            for g in range(tile // LANES):
                left[g, at, :] = mine[:, g * LANES : (g + 1) * LANES]
            ws[at, :] = xw[n][:, row_tiles:, span].reshape(rows, tile)

    hot = (lax.broadcasted_iota(jnp.int32, (tile, tile), 0) == pivots[...]).astype(jnp.float32)
    dv = dot(dot(hot, dinv[...]), vs[...], ((1,), (1,)))
    core = dot(ws[...], dv)

    row = lax.broadcasted_iota(jnp.int32, (row_tiles, col_tiles * RMAX), 0)
    lane = lax.broadcasted_iota(jnp.int32, (row_tiles, col_tiles * RMAX), 1)
    top_r, top_s = jnp.zeros_like(row), jnp.zeros_like(row)
    for i in range(row_tiles):
        for j in range(col_tiles):
            here = (row == i) & (lane >> log2(RMAX) == j)
            dense = admissible[i, j] == 0
            top_r = jnp.where(here, jnp.where(dense, RMAX, rank_rows[i]), top_r)
            top_s = jnp.where(here, jnp.where(dense, RMAX, rank_cols[j]), top_s)
    half = (lane & (RMAX - 1)) >> log2(chunk)
    s = ((lax.axis_index("row") ^ half) << log2(chunk)) + (lane & (chunk - 1))
    top_r = jnp.where(s < top_s, top_r, 0)
    top_r = jnp.broadcast_to(top_r[None], (RMAX,) + top_r.shape).reshape(core.shape)
    k = lax.broadcasted_iota(jnp.int32, core.shape, 0)
    source = ((k >> log2(row_tiles)) & (slots - 1)) * parts + ((k >> log2(rows)) & (parts - 1))
    r = (group_index() ^ source) * per + (k >> log2(rows * parts))
    product = dot(jnp.where(r < top_r, core, 0.0), zs[...])
    for g in range(right.shape[0]):
        right[g, :, :] = product[:, g * LANES : (g + 1) * LANES]


def factors(dinv, pivots, rank_rows, rank_cols, admissible, xw, vz):
    tile = dinv.shape[0]
    row_tiles, col_tiles = admissible.shape
    total = RMAX * row_tiles
    inner = pl.BlockSpec(memory_space=pltpu.VMEM)
    scalars = pl.BlockSpec(memory_space=pltpu.SMEM)
    return pl.pallas_call(
        functools.partial(factor_kernel, len(xw), len(vz), col_tiles, row_tiles),
        out_shape=[
            pltpu.VMEM((tile // LANES, total, LANES), jnp.float32),
            pltpu.VMEM((col_tiles * tile // LANES, total, LANES), jnp.float32),
        ],
        in_specs=[inner] * 2 + [scalars] * 3 + [inner] * (len(xw) + len(vz)),
        out_specs=[inner] * 2,
        scratch_shapes=[
            pltpu.VMEM((total, tile), jnp.float32),
            pltpu.VMEM((col_tiles * RMAX, tile), jnp.float32),
            pltpu.VMEM((col_tiles * RMAX, col_tiles * tile), jnp.float32),
        ],
        compiler_params=pltpu.CompilerParams(vmem_limit_bytes=12 * MIB),
        cost_estimate=pl.CostEstimate(flops=2 * total * tile * tile, bytes_accessed=16 * total * tile, transcendentals=0),
        name="update_factors",
    )(dinv, pivots.reshape(1, tile), rank_rows, rank_cols, admissible, *[in_hbm(array) for array in (*xw, *vz)])


def halves_of(array):
    high = array.astype(jnp.bfloat16)
    return high, (array - high.astype(jnp.float32)).astype(jnp.bfloat16)


def finish_kernel(count, tile, row_map, front, left, right, *rest):
    own, out, held, kept, in_sem, out_sem, own_sem = rest[count - 1 :]
    pieces = (kept, *rest[: count - 1])
    me = group_index()
    col_tiles, rows, _ = kept.shape
    per_tile = tile // rows
    groups = count // per_tile

    def target(g):
        return row_map[0, lax.div(me ^ (g * per_tile), per_tile)]

    def at(g):
        return pl.ds(pl.multiple_of(target(g) * tile, tile), tile)

    def fetch(g):
        return pltpu.make_async_copy(front.at[at(g), :], held.at[g], in_sem.at[g])

    def store(g):
        return pltpu.make_async_copy(held.at[g], out.at[at(g), :], out_sem.at[g])

    fetch_own = pltpu.make_async_copy(own, kept, own_sem)
    for g in reversed(range(groups)):
        fetch(g).start()
    fetch_own.start()
    for g in reversed(range(groups)):
        mine = pl.ds(target(g), RMAX, stride=left.shape[1] // RMAX)
        a, b = halves_of(jnp.concatenate([left[n, mine, :] for n in range(left.shape[0])], axis=1))
        c, d = halves_of(jnp.concatenate([right[n, mine, :] for n in range(right.shape[0])], axis=1))
        update = lax.dot_general(
            jnp.concatenate([a, a, b, b], axis=0),
            jnp.concatenate([c, d, c, d], axis=0),
            (((0,), (0,)), ((), ())),
            preferred_element_type=jnp.float32,
        )
        fetch(g).wait()
        held[g] = held[g] - update
        for p in range(per_tile):
            m = g * per_tile + p
            if m == 0:
                fetch_own.wait()
            low = pl.ds(pl.multiple_of(lax.rem(me ^ m, per_tile) * rows, rows), rows)
            for j in range(col_tiles):
                span = pl.ds(j * tile, tile)
                held[g, low, span] = held[g, low, span] + pieces[m][j]
        store(g).start()
    for g in range(groups):
        store(g).wait()


def finish(front, left, right, pieces, row_map, tile):
    row_tiles = front.shape[0] // tile
    inner = pl.BlockSpec(memory_space=pltpu.VMEM)
    outer = pl.BlockSpec(memory_space=pltpu.HBM)
    return pl.pallas_call(
        functools.partial(finish_kernel, len(pieces), tile),
        out_shape=pltpu.HBM(front.shape, front.dtype),
        in_specs=[pl.BlockSpec(memory_space=pltpu.SMEM), outer] + [inner] * (1 + len(pieces)) + [outer],
        out_specs=outer,
        scratch_shapes=[
            pltpu.VMEM((row_tiles, tile, front.shape[1]), front.dtype),
            pltpu.VMEM(pieces[0].shape, front.dtype),
            pltpu.SemaphoreType.DMA((row_tiles,)),
            pltpu.SemaphoreType.DMA((row_tiles,)),
            pltpu.SemaphoreType.DMA,
        ],
        compiler_params=pltpu.CompilerParams(vmem_limit_bytes=16 * MIB),
        cost_estimate=pl.CostEstimate(flops=2 * front.size * 256, bytes_accessed=3 * front.size * 4, transcendentals=0),
        name="finish",
    )(
        in_hbm(row_map), in_hbm(front), in_vmem(left), in_vmem(right), *[in_vmem(piece) for piece in pieces[1:]], in_hbm(pieces[0])
    )


class Sender:
    def __init__(self):
        self.arrived = []

    def send(self, array, axes, m):
        spot = len(self.arrived) - WINDOW
        if spot >= 0:
            array, self.arrived[spot] = lax.optimization_barrier((array, self.arrived[spot]))
        size = int(np.prod([lax.axis_size(axis) for axis in axes]))
        self.arrived.append(lax.ppermute(array, axes, [(d, d ^ m) for d in range(size)]))
        return len(self.arrived) - 1


def on_device(
    front,
    child,
    row_map,
    col_map,
    x_fac,
    w_fac,
    v_fac,
    z_fac,
    dinv,
    pivots,
    rank_rows,
    rank_cols,
    admissible,
):
    tile = dinv.shape[0]
    row_tiles = front.shape[0] // tile
    col_tiles = front.shape[1] // tile
    devices = lax.axis_size("col") * lax.axis_size("leaf")

    sender = Sender()
    mine = jnp.pad(x_fac, ((0, row_tiles), (0, 0))) + jnp.pad(w_fac, ((row_tiles, 0), (0, 0)))
    mine, child = lax.optimization_barrier((mine, child))
    line = [sender.send(mine, GROUP, m) for m in range(NEAR, devices, NEAR)]
    pieces = place(child, col_map, tile, devices)
    pieces, v_fac, z_fac, rank_rows, rank_cols, admissible = lax.optimization_barrier(
        (pieces, v_fac, z_fac, rank_rows, rank_cols, admissible)
    )

    pieces = list(pieces)
    half = devices // 2
    crossing = list(reversed(range(half, devices)))
    middle = list(range(NEAR, half))
    local = [middle[-1], 3, middle[-2], *middle[:-2], 2, 1]
    spots, xw, vz = {}, [], []

    def send(kind, m):
        if kind == "child":
            spots[m] = sender.send(pieces[m], GROUP, m)
        elif kind == "xw":
            xw.append(sender.send(line, GROUP, m))
        else:
            vz.append(sender.send(both, ("row",), m))

    other = [("xw", 3)] + [("vz", m) for m in range(1, lax.axis_size("row"))] + [("child", m) for m in local]
    last = len(other) - 4
    gaps = len(crossing) - 3
    send("child", crossing[0])
    line = jnp.stack([mine] + [sender.arrived[i] for i in line])
    both = jnp.concatenate([v_fac, z_fac], axis=0)
    order = [("xw", 1), ("xw", 2), ("child", crossing[1]), ("child", crossing[2])]
    for n, m in enumerate(crossing[3:]):
        order += other[n * last // gaps : (n + 1) * last // gaps] + [("child", m)]
    for kind, m in order + other[last:]:
        if (kind, m) == ("child", local[2]):
            given = [line] + [sender.arrived[i] for i in xw], [both] + [sender.arrived[i] for i in vz]
            left, right = factors(dinv, pivots, rank_rows, rank_cols, admissible, *given)
            left, right, pieces[m] = lax.optimization_barrier((left, right, pieces[m]))
        send(kind, m)
    got = [pieces[0]] + [sender.arrived[spots[m]] for m in range(1, devices)]
    return finish(front, left, right, got, row_map, tile)


def solution(mesh):
    return jax.shard_map(
        on_device,
        mesh=mesh,
        in_specs=(
            P("row", GROUP),
            P(("row", "col", "leaf"), None),
            P("row", None),
            P(),
            P("row", GROUP),
            P("row", GROUP),
            P(GROUP, "row"),
            P(GROUP, "row"),
            P(),
            P(),
            P("row"),
            P(GROUP),
            P("row", GROUP),
        ),
        out_specs=P("row", GROUP),
        check_vma=False,
    )
```

```python
import functools

import jax
import jax.numpy as jnp
import numpy as np
from jax import lax
from jax.experimental import pallas as pl
from jax.experimental.pallas import tpu as pltpu
from jax.sharding import PartitionSpec as P

RMAX = 64
LANES = 128
NEAR = 4
WINDOW = 5
GROUP = ("col", "leaf")
HIGHEST = lax.Precision.HIGHEST
MIB = 1 << 20


def group_index():
    return lax.axis_index("col") * lax.axis_size("leaf") + lax.axis_index("leaf")


def in_hbm(array):
    return pltpu.with_memory_space_constraint(array, pltpu.HBM)


def place_kernel(tiles, tile, col_tiles, col_map, child, *rest):
    count = tiles // col_tiles
    pieces = rest[:count]
    inverse, held, in_sem, out_sem = rest[count:]
    me = group_index()

    def fetch(m, j):
        b = inverse[(me ^ m) * col_tiles + j]
        span = pl.ds(pl.multiple_of(b * tile, tile), tile)
        return pltpu.make_async_copy(child.at[:, span], held.at[m, j], in_sem.at[m, j])

    def store(m):
        return pltpu.make_async_copy(held.at[m], pieces[m], out_sem.at[m])

    for b in range(tiles):
        inverse[col_map[b]] = b
    for m in reversed(range(count)):
        for j in range(col_tiles):
            fetch(m, j).start()
    for m in reversed(range(count)):
        for j in range(col_tiles):
            fetch(m, j).wait()
        store(m).start()
    for m in reversed(range(count)):
        store(m).wait()


def in_vmem(array):
    return pltpu.with_memory_space_constraint(array, pltpu.VMEM)


def place(child, col_map, tile, devices):
    rows = child.shape[0]
    tiles = col_map.shape[0]
    col_tiles = tiles // devices
    return pl.pallas_call(
        functools.partial(place_kernel, tiles, tile, col_tiles),
        out_shape=[pltpu.HBM((col_tiles, rows, tile), child.dtype)] * devices,
        in_specs=[pl.BlockSpec(memory_space=pltpu.SMEM), pl.BlockSpec(memory_space=pltpu.HBM)],
        out_specs=[pl.BlockSpec(memory_space=pltpu.HBM)] * devices,
        scratch_shapes=[
            pltpu.SMEM((tiles,), jnp.int32),
            pltpu.VMEM((devices, col_tiles, rows, tile), child.dtype),
            pltpu.SemaphoreType.DMA((devices, col_tiles)),
            pltpu.SemaphoreType.DMA((devices,)),
        ],
        compiler_params=pltpu.CompilerParams(vmem_limit_bytes=8 * MIB),
        cost_estimate=pl.CostEstimate(flops=0, bytes_accessed=2 * child.size * 4, transcendentals=0),
        name="place_child",
    )(in_hbm(col_map), in_hbm(child))


def dot(a, b, contract=((1,), (0,))):
    return lax.dot_general(a, b, (contract, ((), ())), precision=HIGHEST, preferred_element_type=jnp.float32)


def log2(size):
    return size.bit_length() - 1


def factor_kernel(parts, halves, col_tiles, row_tiles, front, dinv, pivots, rank_rows, rank_cols, admissible, *rest):
    xw = rest[:parts]
    vz = rest[parts : parts + halves]
    left, right, staged, ws, vs, zs, sem = rest[parts + halves :]
    stage = pltpu.make_async_copy(front, staged, sem)
    stage.start()
    tile = dinv.shape[0]
    per = xw[0].shape[2] // tile
    chunk = vz[0].shape[1] // tile
    slots = xw[0].shape[0]
    rows = slots * row_tiles

    zs[...] = jnp.zeros_like(zs)
    for h in range(halves):
        for j in range(col_tiles):
            for p in range(chunk):
                at = pl.ds(j * RMAX + h * chunk + p, 1)
                span = pl.ds(p * tile, tile)
                vs[at, :] = vz[h][pl.ds(j, 1), span]
                zs[at, pl.ds(j * tile, tile)] = vz[h][pl.ds(col_tiles + j, 1), span]
    for q in range(per):
        for n in range(parts):
            at = pl.ds((q * parts + n) * rows, rows)
            span = pl.ds(q * tile, tile)
            mine = xw[n][:, :row_tiles, span].reshape(rows, tile)
            for g in range(tile // LANES):
                left[g, at, :] = mine[:, g * LANES : (g + 1) * LANES]
            ws[at, :] = xw[n][:, row_tiles:, span].reshape(rows, tile)

    hot = (lax.broadcasted_iota(jnp.int32, (tile, tile), 0) == pivots[...]).astype(jnp.float32)
    dv = dot(dot(hot, dinv[...]), vs[...], ((1,), (1,)))
    core = dot(ws[...], dv)

    row = lax.broadcasted_iota(jnp.int32, (row_tiles, col_tiles * RMAX), 0)
    lane = lax.broadcasted_iota(jnp.int32, (row_tiles, col_tiles * RMAX), 1)
    top_r, top_s = jnp.zeros_like(row), jnp.zeros_like(row)
    for i in range(row_tiles):
        for j in range(col_tiles):
            here = (row == i) & (lane >> log2(RMAX) == j)
            dense = admissible[i, j] == 0
            top_r = jnp.where(here, jnp.where(dense, RMAX, rank_rows[i]), top_r)
            top_s = jnp.where(here, jnp.where(dense, RMAX, rank_cols[j]), top_s)
    half = (lane & (RMAX - 1)) >> log2(chunk)
    s = ((lax.axis_index("row") ^ half) << log2(chunk)) + (lane & (chunk - 1))
    top_r = jnp.where(s < top_s, top_r, 0)
    top_r = jnp.broadcast_to(top_r[None], (RMAX,) + top_r.shape).reshape(core.shape)
    k = lax.broadcasted_iota(jnp.int32, core.shape, 0)
    source = ((k >> log2(row_tiles)) & (slots - 1)) * parts + ((k >> log2(rows)) & (parts - 1))
    r = (group_index() ^ source) * per + (k >> log2(rows * parts))
    product = dot(jnp.where(r < top_r, core, 0.0), zs[...])
    for g in range(right.shape[0]):
        right[g, :, :] = product[:, g * LANES : (g + 1) * LANES]
    stage.wait()


def factors(front, dinv, pivots, rank_rows, rank_cols, admissible, xw, vz):
    tile = dinv.shape[0]
    row_tiles, col_tiles = admissible.shape
    total = RMAX * row_tiles
    inner = pl.BlockSpec(memory_space=pltpu.VMEM)
    scalars = pl.BlockSpec(memory_space=pltpu.SMEM)
    return pl.pallas_call(
        functools.partial(factor_kernel, len(xw), len(vz), col_tiles, row_tiles),
        out_shape=[
            pltpu.VMEM((tile // LANES, total, LANES), jnp.float32),
            pltpu.VMEM((col_tiles * tile // LANES, total, LANES), jnp.float32),
            pltpu.VMEM(front.shape, front.dtype),
        ],
        in_specs=[pl.BlockSpec(memory_space=pltpu.HBM)] + [inner] * 2 + [scalars] * 3 + [inner] * (len(xw) + len(vz)),
        out_specs=[inner] * 3,
        scratch_shapes=[
            pltpu.VMEM((total, tile), jnp.float32),
            pltpu.VMEM((col_tiles * RMAX, tile), jnp.float32),
            pltpu.VMEM((col_tiles * RMAX, col_tiles * tile), jnp.float32),
            pltpu.SemaphoreType.DMA,
        ],
        compiler_params=pltpu.CompilerParams(vmem_limit_bytes=12 * MIB),
        cost_estimate=pl.CostEstimate(flops=2 * total * tile * tile, bytes_accessed=16 * total * tile, transcendentals=0),
        name="update_factors",
    )(in_hbm(front), dinv, pivots.reshape(1, tile), rank_rows, rank_cols, admissible, *[in_hbm(array) for array in (*xw, *vz)])


def halves_of(array):
    high = array.astype(jnp.bfloat16)
    return high, (array - high.astype(jnp.float32)).astype(jnp.bfloat16)


def finish_kernel(count, tile, row_map, front, left, right, *rest):
    own, out, held, kept, out_sem, own_sem = rest[count - 1 :]
    pieces = (kept, *rest[: count - 1])
    me = group_index()
    col_tiles, rows, _ = kept.shape
    per_tile = tile // rows
    groups = count // per_tile

    def target(g):
        return row_map[0, lax.div(me ^ (g * per_tile), per_tile)]

    def at(g):
        return pl.ds(pl.multiple_of(target(g) * tile, tile), tile)

    def store(g):
        return pltpu.make_async_copy(held.at[g], out.at[at(g), :], out_sem.at[g])

    fetch_own = pltpu.make_async_copy(own, kept, own_sem)
    fetch_own.start()
    for g in reversed(range(groups)):
        mine = pl.ds(target(g), RMAX, stride=left.shape[1] // RMAX)
        a, b = halves_of(jnp.concatenate([left[n, mine, :] for n in range(left.shape[0])], axis=1))
        c, d = halves_of(jnp.concatenate([right[n, mine, :] for n in range(right.shape[0])], axis=1))
        update = lax.dot_general(
            jnp.concatenate([a, a, b, b], axis=0),
            jnp.concatenate([c, d, c, d], axis=0),
            (((0,), (0,)), ((), ())),
            preferred_element_type=jnp.float32,
        )
        held[g] = front[at(g), :] - update
        for p in range(per_tile):
            m = g * per_tile + p
            if m == 0:
                fetch_own.wait()
            low = pl.ds(pl.multiple_of(lax.rem(me ^ m, per_tile) * rows, rows), rows)
            for j in range(col_tiles):
                span = pl.ds(j * tile, tile)
                held[g, low, span] = held[g, low, span] + pieces[m][j]
        store(g).start()
    for g in range(groups):
        store(g).wait()


def finish(front, left, right, pieces, row_map, tile):
    row_tiles = front.shape[0] // tile
    inner = pl.BlockSpec(memory_space=pltpu.VMEM)
    outer = pl.BlockSpec(memory_space=pltpu.HBM)
    return pl.pallas_call(
        functools.partial(finish_kernel, len(pieces), tile),
        out_shape=pltpu.HBM(front.shape, front.dtype),
        in_specs=[pl.BlockSpec(memory_space=pltpu.SMEM)] + [inner] * (2 + len(pieces)) + [outer],
        out_specs=outer,
        scratch_shapes=[
            pltpu.VMEM((row_tiles, tile, front.shape[1]), front.dtype),
            pltpu.VMEM(pieces[0].shape, front.dtype),
            pltpu.SemaphoreType.DMA((row_tiles,)),
            pltpu.SemaphoreType.DMA,
        ],
        compiler_params=pltpu.CompilerParams(vmem_limit_bytes=8 * MIB),
        cost_estimate=pl.CostEstimate(flops=2 * front.size * 256, bytes_accessed=3 * front.size * 4, transcendentals=0),
        name="finish",
    )(
        in_hbm(row_map), in_vmem(front), in_vmem(left), in_vmem(right), *[in_vmem(piece) for piece in pieces[1:]], in_hbm(pieces[0])
    )


class Sender:
    def __init__(self):
        self.arrived = []

    def send(self, array, axes, m):
        spot = len(self.arrived) - WINDOW
        if spot >= 0:
            array, self.arrived[spot] = lax.optimization_barrier((array, self.arrived[spot]))
        size = int(np.prod([lax.axis_size(axis) for axis in axes]))
        self.arrived.append(lax.ppermute(array, axes, [(d, d ^ m) for d in range(size)]))
        return len(self.arrived) - 1


def on_device(
    front,
    child,
    row_map,
    col_map,
    x_fac,
    w_fac,
    v_fac,
    z_fac,
    dinv,
    pivots,
    rank_rows,
    rank_cols,
    admissible,
):
    tile = dinv.shape[0]
    row_tiles = front.shape[0] // tile
    col_tiles = front.shape[1] // tile
    devices = lax.axis_size("col") * lax.axis_size("leaf")

    sender = Sender()
    mine = jnp.pad(x_fac, ((0, row_tiles), (0, 0))) + jnp.pad(w_fac, ((row_tiles, 0), (0, 0)))
    mine, child = lax.optimization_barrier((mine, child))
    line = [sender.send(mine, GROUP, m) for m in range(NEAR, devices, NEAR)]
    pieces = place(child, col_map, tile, devices)
    pieces, v_fac, z_fac, rank_rows, rank_cols, admissible = lax.optimization_barrier(
        (pieces, v_fac, z_fac, rank_rows, rank_cols, admissible)
    )

    pieces = list(pieces)
    half = devices // 2
    crossing = list(reversed(range(half, devices)))
    local = [m for pair in zip(reversed(range(NEAR, half)), [3, 2, 1] + [None] * half) for m in pair if m]
    between = [("xw", m) for m in range(1, NEAR)] + [("vz", m) for m in range(1, lax.axis_size("row"))]
    between += [("child", m) for m in local]
    gaps = len(crossing) - 2
    spots, xw, vz = {}, [], []
    for n, m in enumerate(crossing):
        for i, (kind, other) in enumerate(between):
            if n == 2 + i * gaps // len(between):
                if kind == "child":
                    if other == local[-3]:
                        given = [line] + [sender.arrived[i] for i in xw], [both] + [sender.arrived[i] for i in vz]
                        *ready, staged = factors(front, dinv, pivots, rank_rows, rank_cols, admissible, *given)
                        ready, staged, pieces[other] = lax.optimization_barrier((ready, staged, pieces[other]))
                    spots[other] = sender.send(pieces[other], GROUP, other)
                elif kind == "xw":
                    if not xw:
                        line = jnp.stack([mine] + [sender.arrived[i] for i in line])
                    xw.append(sender.send(line, GROUP, other))
                else:
                    if not vz:
                        both = jnp.concatenate([v_fac, z_fac], axis=0)
                    vz.append(sender.send(both, ("row",), other))
        spots[m] = sender.send(pieces[m], GROUP, m)
    got = [pieces[0]] + [sender.arrived[spots[m]] for m in range(1, devices)]
    return finish(staged, *ready, got, row_map, tile)


def solution(mesh):
    return jax.shard_map(
        on_device,
        mesh=mesh,
        in_specs=(
            P("row", GROUP),
            P(("row", "col", "leaf"), None),
            P("row", None),
            P(),
            P("row", GROUP),
            P("row", GROUP),
            P(GROUP, "row"),
            P(GROUP, "row"),
            P(),
            P(),
            P("row"),
            P(GROUP),
            P("row", GROUP),
        ),
        out_specs=P("row", GROUP),
        check_vma=False,
    )
```

```python
import functools

import jax
import jax.numpy as jnp
import numpy as np
from jax import lax
from jax.experimental import pallas as pl
from jax.experimental.pallas import tpu as pltpu
from jax.sharding import PartitionSpec as P

RMAX = 64
LANES = 128
NEAR = 4
WINDOW = 5
GROUP = ("col", "leaf")
HIGHEST = lax.Precision.HIGHEST
MIB = 1 << 20


def group_index():
    return lax.axis_index("col") * lax.axis_size("leaf") + lax.axis_index("leaf")


def in_hbm(array):
    return pltpu.with_memory_space_constraint(array, pltpu.HBM)


def place_kernel(tiles, tile, col_tiles, col_map, child, *rest):
    count = tiles // col_tiles
    pieces = rest[:count]
    inverse, held, in_sem, out_sem = rest[count:]
    me = group_index()

    def fetch(m, j):
        b = inverse[(me ^ m) * col_tiles + j]
        span = pl.ds(pl.multiple_of(b * tile, tile), tile)
        return pltpu.make_async_copy(child.at[:, span], held.at[m, j], in_sem.at[m, j])

    def store(m):
        return pltpu.make_async_copy(held.at[m], pieces[m], out_sem.at[m])

    for b in range(tiles):
        inverse[col_map[b]] = b
    for m in reversed(range(count)):
        for j in range(col_tiles):
            fetch(m, j).start()
    for m in reversed(range(count)):
        for j in range(col_tiles):
            fetch(m, j).wait()
        store(m).start()
    for m in reversed(range(count)):
        store(m).wait()


def in_vmem(array):
    return pltpu.with_memory_space_constraint(array, pltpu.VMEM)


def place(child, col_map, tile, devices):
    rows = child.shape[0]
    tiles = col_map.shape[0]
    col_tiles = tiles // devices
    return pl.pallas_call(
        functools.partial(place_kernel, tiles, tile, col_tiles),
        out_shape=[pltpu.HBM((col_tiles, rows, tile), child.dtype)] * devices,
        in_specs=[pl.BlockSpec(memory_space=pltpu.SMEM), pl.BlockSpec(memory_space=pltpu.HBM)],
        out_specs=[pl.BlockSpec(memory_space=pltpu.HBM)] * devices,
        scratch_shapes=[
            pltpu.SMEM((tiles,), jnp.int32),
            pltpu.VMEM((devices, col_tiles, rows, tile), child.dtype),
            pltpu.SemaphoreType.DMA((devices, col_tiles)),
            pltpu.SemaphoreType.DMA((devices,)),
        ],
        compiler_params=pltpu.CompilerParams(vmem_limit_bytes=8 * MIB),
        cost_estimate=pl.CostEstimate(flops=0, bytes_accessed=2 * child.size * 4, transcendentals=0),
        name="place_child",
    )(in_hbm(col_map), in_hbm(child))


def dot(a, b, contract=((1,), (0,))):
    return lax.dot_general(a, b, (contract, ((), ())), precision=HIGHEST, preferred_element_type=jnp.float32)


def log2(size):
    return size.bit_length() - 1


def factor_kernel(parts, halves, col_tiles, row_tiles, front, dinv, pivots, rank_rows, rank_cols, admissible, *rest):
    xw = rest[:parts]
    vz = rest[parts : parts + halves]
    left, right, staged, ws, vs, zs, sem = rest[parts + halves :]
    stage = pltpu.make_async_copy(front, staged, sem)
    stage.start()
    tile = dinv.shape[0]
    per = xw[0].shape[2] // tile
    chunk = vz[0].shape[1] // tile
    slots = xw[0].shape[0]
    rows = slots * row_tiles

    zs[...] = jnp.zeros_like(zs)
    for h in range(halves):
        for j in range(col_tiles):
            for p in range(chunk):
                at = pl.ds(j * RMAX + h * chunk + p, 1)
                span = pl.ds(p * tile, tile)
                vs[at, :] = vz[h][pl.ds(j, 1), span]
                zs[at, pl.ds(j * tile, tile)] = vz[h][pl.ds(col_tiles + j, 1), span]
    for q in range(per):
        for n in range(parts):
            at = pl.ds((q * parts + n) * rows, rows)
            span = pl.ds(q * tile, tile)
            mine = xw[n][:, :row_tiles, span].reshape(rows, tile)
            for g in range(tile // LANES):
                left[g, at, :] = mine[:, g * LANES : (g + 1) * LANES]
            ws[at, :] = xw[n][:, row_tiles:, span].reshape(rows, tile)

    hot = (lax.broadcasted_iota(jnp.int32, (tile, tile), 0) == pivots[...]).astype(jnp.float32)
    dv = dot(dot(hot, dinv[...]), vs[...], ((1,), (1,)))
    core = dot(ws[...], dv)

    row = lax.broadcasted_iota(jnp.int32, (row_tiles, col_tiles * RMAX), 0)
    lane = lax.broadcasted_iota(jnp.int32, (row_tiles, col_tiles * RMAX), 1)
    top_r, top_s = jnp.zeros_like(row), jnp.zeros_like(row)
    for i in range(row_tiles):
        for j in range(col_tiles):
            here = (row == i) & (lane >> log2(RMAX) == j)
            dense = admissible[i, j] == 0
            top_r = jnp.where(here, jnp.where(dense, RMAX, rank_rows[i]), top_r)
            top_s = jnp.where(here, jnp.where(dense, RMAX, rank_cols[j]), top_s)
    half = (lane & (RMAX - 1)) >> log2(chunk)
    s = ((lax.axis_index("row") ^ half) << log2(chunk)) + (lane & (chunk - 1))
    top_r = jnp.where(s < top_s, top_r, 0)
    top_r = jnp.broadcast_to(top_r[None], (RMAX,) + top_r.shape).reshape(core.shape)
    k = lax.broadcasted_iota(jnp.int32, core.shape, 0)
    source = ((k >> log2(row_tiles)) & (slots - 1)) * parts + ((k >> log2(rows)) & (parts - 1))
    r = (group_index() ^ source) * per + (k >> log2(rows * parts))
    product = dot(jnp.where(r < top_r, core, 0.0), zs[...])
    for g in range(right.shape[0]):
        right[g, :, :] = product[:, g * LANES : (g + 1) * LANES]
    stage.wait()


def factors(front, dinv, pivots, rank_rows, rank_cols, admissible, xw, vz):
    tile = dinv.shape[0]
    row_tiles, col_tiles = admissible.shape
    total = RMAX * row_tiles
    inner = pl.BlockSpec(memory_space=pltpu.VMEM)
    scalars = pl.BlockSpec(memory_space=pltpu.SMEM)
    return pl.pallas_call(
        functools.partial(factor_kernel, len(xw), len(vz), col_tiles, row_tiles),
        out_shape=[
            pltpu.VMEM((tile // LANES, total, LANES), jnp.float32),
            pltpu.VMEM((col_tiles * tile // LANES, total, LANES), jnp.float32),
            pltpu.VMEM(front.shape, front.dtype),
        ],
        in_specs=[pl.BlockSpec(memory_space=pltpu.HBM)] + [inner] * 2 + [scalars] * 3 + [inner] * (len(xw) + len(vz)),
        out_specs=[inner] * 3,
        scratch_shapes=[
            pltpu.VMEM((total, tile), jnp.float32),
            pltpu.VMEM((col_tiles * RMAX, tile), jnp.float32),
            pltpu.VMEM((col_tiles * RMAX, col_tiles * tile), jnp.float32),
            pltpu.SemaphoreType.DMA,
        ],
        compiler_params=pltpu.CompilerParams(vmem_limit_bytes=12 * MIB),
        cost_estimate=pl.CostEstimate(flops=2 * total * tile * tile, bytes_accessed=16 * total * tile, transcendentals=0),
        name="update_factors",
    )(in_hbm(front), dinv, pivots.reshape(1, tile), rank_rows, rank_cols, admissible, *[in_hbm(array) for array in (*xw, *vz)])


def halves_of(array):
    high = array.astype(jnp.bfloat16)
    return high, (array - high.astype(jnp.float32)).astype(jnp.bfloat16)


def finish_kernel(count, tile, row_map, front, left, right, *rest):
    own, out, held, kept, out_sem, own_sem = rest[count - 1 :]
    pieces = (kept, *rest[: count - 1])
    me = group_index()
    col_tiles, rows, _ = kept.shape
    per_tile = tile // rows
    groups = count // per_tile

    def target(g):
        return row_map[0, lax.div(me ^ (g * per_tile), per_tile)]

    def at(g):
        return pl.ds(pl.multiple_of(target(g) * tile, tile), tile)

    def store(g):
        return pltpu.make_async_copy(held.at[g], out.at[at(g), :], out_sem.at[g])

    fetch_own = pltpu.make_async_copy(own, kept, own_sem)
    fetch_own.start()
    for g in reversed(range(groups)):
        mine = pl.ds(target(g), RMAX, stride=left.shape[1] // RMAX)
        a, b = halves_of(jnp.concatenate([left[n, mine, :] for n in range(left.shape[0])], axis=1))
        c, d = halves_of(jnp.concatenate([right[n, mine, :] for n in range(right.shape[0])], axis=1))
        update = lax.dot_general(
            jnp.concatenate([a, a, b, b], axis=0),
            jnp.concatenate([c, d, c, d], axis=0),
            (((0,), (0,)), ((), ())),
            preferred_element_type=jnp.float32,
        )
        held[g] = front[at(g), :] - update
        for p in range(per_tile):
            m = g * per_tile + p
            if m == 0:
                fetch_own.wait()
            low = pl.ds(pl.multiple_of(lax.rem(me ^ m, per_tile) * rows, rows), rows)
            for j in range(col_tiles):
                span = pl.ds(j * tile, tile)
                held[g, low, span] = held[g, low, span] + pieces[m][j]
        store(g).start()
    for g in range(groups):
        store(g).wait()


def finish(front, left, right, pieces, row_map, tile):
    row_tiles = front.shape[0] // tile
    inner = pl.BlockSpec(memory_space=pltpu.VMEM)
    outer = pl.BlockSpec(memory_space=pltpu.HBM)
    return pl.pallas_call(
        functools.partial(finish_kernel, len(pieces), tile),
        out_shape=pltpu.HBM(front.shape, front.dtype),
        in_specs=[pl.BlockSpec(memory_space=pltpu.SMEM)] + [inner] * (2 + len(pieces)) + [outer],
        out_specs=outer,
        scratch_shapes=[
            pltpu.VMEM((row_tiles, tile, front.shape[1]), front.dtype),
            pltpu.VMEM(pieces[0].shape, front.dtype),
            pltpu.SemaphoreType.DMA((row_tiles,)),
            pltpu.SemaphoreType.DMA,
        ],
        compiler_params=pltpu.CompilerParams(vmem_limit_bytes=8 * MIB),
        cost_estimate=pl.CostEstimate(flops=2 * front.size * 256, bytes_accessed=3 * front.size * 4, transcendentals=0),
        name="finish",
    )(
        in_hbm(row_map), in_vmem(front), in_vmem(left), in_vmem(right), *[in_vmem(piece) for piece in pieces[1:]], in_hbm(pieces[0])
    )


class Sender:
    def __init__(self):
        self.arrived = []

    def send(self, array, axes, m):
        spot = len(self.arrived) - WINDOW
        if spot >= 0:
            array, self.arrived[spot] = lax.optimization_barrier((array, self.arrived[spot]))
        size = int(np.prod([lax.axis_size(axis) for axis in axes]))
        self.arrived.append(lax.ppermute(array, axes, [(d, d ^ m) for d in range(size)]))
        return len(self.arrived) - 1


def on_device(
    front,
    child,
    row_map,
    col_map,
    x_fac,
    w_fac,
    v_fac,
    z_fac,
    dinv,
    pivots,
    rank_rows,
    rank_cols,
    admissible,
):
    tile = dinv.shape[0]
    row_tiles = front.shape[0] // tile
    col_tiles = front.shape[1] // tile
    devices = lax.axis_size("col") * lax.axis_size("leaf")

    sender = Sender()
    mine = jnp.pad(x_fac, ((0, row_tiles), (0, 0))) + jnp.pad(w_fac, ((row_tiles, 0), (0, 0)))
    mine, child = lax.optimization_barrier((mine, child))
    line = [sender.send(mine, GROUP, m) for m in range(NEAR, devices, NEAR)]
    pieces = place(child, col_map, tile, devices)
    pieces, v_fac, z_fac, rank_rows, rank_cols, admissible = lax.optimization_barrier(
        (pieces, v_fac, z_fac, rank_rows, rank_cols, admissible)
    )

    pieces = list(pieces)
    half = devices // 2
    crossing = list(reversed(range(half, devices)))
    local = [m for pair in zip(reversed(range(NEAR, half)), [3, 2, 1] + [None] * half) for m in pair if m]
    between = [("xw", m) for m in range(1, NEAR)] + [("vz", m) for m in range(1, lax.axis_size("row"))]
    between += [("child", m) for m in local]
    gaps = len(crossing) - 2
    turn = [2 + i * gaps // len(between) for i in range(len(between))]
    order = []
    for n, m in enumerate(crossing[:-2]):
        order += [item for i, item in enumerate(between[:-4]) if turn[i] == n] + [("child", m)]
    order += [item for i, item in enumerate(between[:-4]) if turn[i] >= len(crossing) - 2]
    order += [("child", m) for m in (crossing[-2], local[-3], local[-4], crossing[-1], local[-1], local[-2])]
    spots, xw, vz = {}, [], []
    for kind, m in order:
        if kind == "xw":
            if not xw:
                line = jnp.stack([mine] + [sender.arrived[i] for i in line])
            xw.append(sender.send(line, GROUP, m))
        elif kind == "vz":
            if not vz:
                both = jnp.concatenate([v_fac, z_fac], axis=0)
            vz.append(sender.send(both, ("row",), m))
        else:
            if m == local[-3]:
                given = [line] + [sender.arrived[i] for i in xw], [both] + [sender.arrived[i] for i in vz]
                *ready, staged = factors(front, dinv, pivots, rank_rows, rank_cols, admissible, *given)
                ready, staged, pieces[m] = lax.optimization_barrier((ready, staged, pieces[m]))
            spots[m] = sender.send(pieces[m], GROUP, m)
    got = [pieces[0]] + [sender.arrived[spots[m]] for m in range(1, devices)]
    return finish(staged, *ready, got, row_map, tile)


def solution(mesh):
    return jax.shard_map(
        on_device,
        mesh=mesh,
        in_specs=(
            P("row", GROUP),
            P(("row", "col", "leaf"), None),
            P("row", None),
            P(),
            P("row", GROUP),
            P("row", GROUP),
            P(GROUP, "row"),
            P(GROUP, "row"),
            P(),
            P(),
            P("row"),
            P(GROUP),
            P("row", GROUP),
        ),
        out_specs=P("row", GROUP),
        check_vma=False,
    )
```

```python
import functools

import jax
import jax.numpy as jnp
import numpy as np
from jax import lax
from jax.experimental import pallas as pl
from jax.experimental.pallas import tpu as pltpu
from jax.sharding import PartitionSpec as P

RMAX = 64
LANES = 128
NEAR = 4
WINDOW = 5
GROUP = ("col", "leaf")
HIGHEST = lax.Precision.HIGHEST
MIB = 1 << 20


def group_index():
    return lax.axis_index("col") * lax.axis_size("leaf") + lax.axis_index("leaf")


def in_hbm(array):
    return pltpu.with_memory_space_constraint(array, pltpu.HBM)


def place_kernel(members, tiles, tile, col_tiles, col_map, child, *rest):
    pieces = rest[: len(members)]
    inverse, held, in_sem, out_sem = rest[len(members) :]
    me = group_index()

    def fetch(n, j):
        b = inverse[(me ^ members[n]) * col_tiles + j]
        span = pl.ds(pl.multiple_of(b * tile, tile), tile)
        return pltpu.make_async_copy(child.at[:, span], held.at[n, j], in_sem.at[n, j])

    def store(n):
        return pltpu.make_async_copy(held.at[n], pieces[n], out_sem.at[n])

    for b in range(tiles):
        inverse[col_map[b]] = b
    for n in range(len(members)):
        for j in range(col_tiles):
            fetch(n, j).start()
    for n in range(len(members)):
        for j in range(col_tiles):
            fetch(n, j).wait()
        store(n).start()
    for n in range(len(members)):
        store(n).wait()


def in_vmem(array):
    return pltpu.with_memory_space_constraint(array, pltpu.VMEM)


def place(child, col_map, tile, devices, members):
    rows = child.shape[0]
    tiles = col_map.shape[0]
    col_tiles = tiles // devices
    count = len(members)
    pieces = pl.pallas_call(
        functools.partial(place_kernel, members, tiles, tile, col_tiles),
        out_shape=[pltpu.HBM((col_tiles, rows, tile), child.dtype)] * count,
        in_specs=[pl.BlockSpec(memory_space=pltpu.SMEM), pl.BlockSpec(memory_space=pltpu.HBM)],
        out_specs=[pl.BlockSpec(memory_space=pltpu.HBM)] * count,
        scratch_shapes=[
            pltpu.SMEM((tiles,), jnp.int32),
            pltpu.VMEM((count, col_tiles, rows, tile), child.dtype),
            pltpu.SemaphoreType.DMA((count, col_tiles)),
            pltpu.SemaphoreType.DMA((count,)),
        ],
        compiler_params=pltpu.CompilerParams(vmem_limit_bytes=8 * MIB),
        cost_estimate=pl.CostEstimate(flops=0, bytes_accessed=8 * count * col_tiles * rows * tile, transcendentals=0),
        name="place_child",
    )(in_hbm(col_map), in_hbm(child))
    return dict(zip(members, pieces))


def dot(a, b, contract=((1,), (0,))):
    return lax.dot_general(a, b, (contract, ((), ())), precision=HIGHEST, preferred_element_type=jnp.float32)


def log2(size):
    return size.bit_length() - 1


def factor_kernel(parts, halves, col_tiles, row_tiles, front, dinv, pivots, rank_rows, rank_cols, admissible, *rest):
    xw = rest[:parts]
    vz = rest[parts : parts + halves]
    left, right, staged, ws, vs, zs, sem = rest[parts + halves :]
    stage = pltpu.make_async_copy(front, staged, sem)
    stage.start()
    tile = dinv.shape[0]
    per = xw[0].shape[2] // tile
    chunk = vz[0].shape[1] // tile
    slots = xw[0].shape[0]
    rows = slots * row_tiles

    zs[...] = jnp.zeros_like(zs)
    for h in range(halves):
        for j in range(col_tiles):
            for p in range(chunk):
                at = pl.ds(j * RMAX + h * chunk + p, 1)
                span = pl.ds(p * tile, tile)
                vs[at, :] = vz[h][pl.ds(j, 1), span]
                zs[at, pl.ds(j * tile, tile)] = vz[h][pl.ds(col_tiles + j, 1), span]
    for q in range(per):
        for n in range(parts):
            at = pl.ds((q * parts + n) * rows, rows)
            span = pl.ds(q * tile, tile)
            mine = xw[n][:, :row_tiles, span].reshape(rows, tile)
            for g in range(tile // LANES):
                left[g, at, :] = mine[:, g * LANES : (g + 1) * LANES]
            ws[at, :] = xw[n][:, row_tiles:, span].reshape(rows, tile)

    hot = (lax.broadcasted_iota(jnp.int32, (tile, tile), 0) == pivots[...]).astype(jnp.float32)
    dv = dot(dot(hot, dinv[...]), vs[...], ((1,), (1,)))
    core = dot(ws[...], dv)

    row = lax.broadcasted_iota(jnp.int32, (row_tiles, col_tiles * RMAX), 0)
    lane = lax.broadcasted_iota(jnp.int32, (row_tiles, col_tiles * RMAX), 1)
    top_r, top_s = jnp.zeros_like(row), jnp.zeros_like(row)
    for i in range(row_tiles):
        for j in range(col_tiles):
            here = (row == i) & (lane >> log2(RMAX) == j)
            dense = admissible[i, j] == 0
            top_r = jnp.where(here, jnp.where(dense, RMAX, rank_rows[i]), top_r)
            top_s = jnp.where(here, jnp.where(dense, RMAX, rank_cols[j]), top_s)
    half = (lane & (RMAX - 1)) >> log2(chunk)
    s = ((lax.axis_index("row") ^ half) << log2(chunk)) + (lane & (chunk - 1))
    top_r = jnp.where(s < top_s, top_r, 0)
    top_r = jnp.broadcast_to(top_r[None], (RMAX,) + top_r.shape).reshape(core.shape)
    k = lax.broadcasted_iota(jnp.int32, core.shape, 0)
    source = ((k >> log2(row_tiles)) & (slots - 1)) * parts + ((k >> log2(rows)) & (parts - 1))
    r = (group_index() ^ source) * per + (k >> log2(rows * parts))
    product = dot(jnp.where(r < top_r, core, 0.0), zs[...])
    for g in range(right.shape[0]):
        right[g, :, :] = product[:, g * LANES : (g + 1) * LANES]
    stage.wait()


def factors(front, dinv, pivots, rank_rows, rank_cols, admissible, xw, vz):
    tile = dinv.shape[0]
    row_tiles, col_tiles = admissible.shape
    total = RMAX * row_tiles
    inner = pl.BlockSpec(memory_space=pltpu.VMEM)
    scalars = pl.BlockSpec(memory_space=pltpu.SMEM)
    return pl.pallas_call(
        functools.partial(factor_kernel, len(xw), len(vz), col_tiles, row_tiles),
        out_shape=[
            pltpu.VMEM((tile // LANES, total, LANES), jnp.float32),
            pltpu.VMEM((col_tiles * tile // LANES, total, LANES), jnp.float32),
            pltpu.VMEM(front.shape, front.dtype),
        ],
        in_specs=[pl.BlockSpec(memory_space=pltpu.HBM)] + [inner] * 2 + [scalars] * 3 + [inner] * (len(xw) + len(vz)),
        out_specs=[inner] * 3,
        scratch_shapes=[
            pltpu.VMEM((total, tile), jnp.float32),
            pltpu.VMEM((col_tiles * RMAX, tile), jnp.float32),
            pltpu.VMEM((col_tiles * RMAX, col_tiles * tile), jnp.float32),
            pltpu.SemaphoreType.DMA,
        ],
        compiler_params=pltpu.CompilerParams(vmem_limit_bytes=12 * MIB),
        cost_estimate=pl.CostEstimate(flops=2 * total * tile * tile, bytes_accessed=16 * total * tile, transcendentals=0),
        name="update_factors",
    )(in_hbm(front), dinv, pivots.reshape(1, tile), rank_rows, rank_cols, admissible, *[in_hbm(array) for array in (*xw, *vz)])


def halves_of(array):
    high = array.astype(jnp.bfloat16)
    return high, (array - high.astype(jnp.float32)).astype(jnp.bfloat16)


def finish_kernel(count, tile, row_map, front, left, right, *rest):
    own, out, held, kept, out_sem, own_sem = rest[count - 1 :]
    pieces = (kept, *rest[: count - 1])
    me = group_index()
    col_tiles, rows, _ = kept.shape
    per_tile = tile // rows
    groups = count // per_tile

    def target(g):
        return row_map[0, lax.div(me ^ (g * per_tile), per_tile)]

    def at(g):
        return pl.ds(pl.multiple_of(target(g) * tile, tile), tile)

    def store(g):
        return pltpu.make_async_copy(held.at[g], out.at[at(g), :], out_sem.at[g])

    fetch_own = pltpu.make_async_copy(own, kept, own_sem)
    fetch_own.start()
    for g in reversed(range(groups)):
        mine = pl.ds(target(g), RMAX, stride=left.shape[1] // RMAX)
        a, b = halves_of(jnp.concatenate([left[n, mine, :] for n in range(left.shape[0])], axis=1))
        c, d = halves_of(jnp.concatenate([right[n, mine, :] for n in range(right.shape[0])], axis=1))
        update = lax.dot_general(
            jnp.concatenate([a, a, b, b], axis=0),
            jnp.concatenate([c, d, c, d], axis=0),
            (((0,), (0,)), ((), ())),
            preferred_element_type=jnp.float32,
        )
        held[g] = front[at(g), :] - update
        for p in range(per_tile):
            m = g * per_tile + p
            if m == 0:
                fetch_own.wait()
            low = pl.ds(pl.multiple_of(lax.rem(me ^ m, per_tile) * rows, rows), rows)
            for j in range(col_tiles):
                span = pl.ds(j * tile, tile)
                held[g, low, span] = held[g, low, span] + pieces[m][j]
        store(g).start()
    for g in range(groups):
        store(g).wait()


def finish(front, left, right, pieces, row_map, tile):
    row_tiles = front.shape[0] // tile
    inner = pl.BlockSpec(memory_space=pltpu.VMEM)
    outer = pl.BlockSpec(memory_space=pltpu.HBM)
    return pl.pallas_call(
        functools.partial(finish_kernel, len(pieces), tile),
        out_shape=pltpu.HBM(front.shape, front.dtype),
        in_specs=[pl.BlockSpec(memory_space=pltpu.SMEM)] + [inner] * (2 + len(pieces)) + [outer],
        out_specs=outer,
        scratch_shapes=[
            pltpu.VMEM((row_tiles, tile, front.shape[1]), front.dtype),
            pltpu.VMEM(pieces[0].shape, front.dtype),
            pltpu.SemaphoreType.DMA((row_tiles,)),
            pltpu.SemaphoreType.DMA,
        ],
        compiler_params=pltpu.CompilerParams(vmem_limit_bytes=8 * MIB),
        cost_estimate=pl.CostEstimate(flops=2 * front.size * 256, bytes_accessed=3 * front.size * 4, transcendentals=0),
        name="finish",
    )(
        in_hbm(row_map), in_vmem(front), in_vmem(left), in_vmem(right), *[in_vmem(piece) for piece in pieces[1:]], in_hbm(pieces[0])
    )


class Sender:
    def __init__(self):
        self.arrived = []

    def send(self, array, axes, m):
        spot = len(self.arrived) - WINDOW
        if spot >= 0:
            array, self.arrived[spot] = lax.optimization_barrier((array, self.arrived[spot]))
        size = int(np.prod([lax.axis_size(axis) for axis in axes]))
        self.arrived.append(lax.ppermute(array, axes, [(d, d ^ m) for d in range(size)]))
        return len(self.arrived) - 1


def on_device(
    front,
    child,
    row_map,
    col_map,
    x_fac,
    w_fac,
    v_fac,
    z_fac,
    dinv,
    pivots,
    rank_rows,
    rank_cols,
    admissible,
):
    tile = dinv.shape[0]
    row_tiles = front.shape[0] // tile
    col_tiles = front.shape[1] // tile
    devices = lax.axis_size("col") * lax.axis_size("leaf")

    sender = Sender()
    mine = jnp.pad(x_fac, ((0, row_tiles), (0, 0))) + jnp.pad(w_fac, ((row_tiles, 0), (0, 0)))
    mine, child = lax.optimization_barrier((mine, child))
    line = [sender.send(mine, GROUP, m) for m in range(NEAR, devices, NEAR)]
    early = [devices - 1, devices - 2, devices - 3]
    pieces = place(child, col_map, tile, devices, early)
    pieces, child, v_fac, z_fac = lax.optimization_barrier((pieces, child, v_fac, z_fac))
    pieces.update(place(child, col_map, tile, devices, list(reversed(range(devices - 3)))))
    half = devices // 2
    crossing = list(reversed(range(half, devices)))
    local = [m for pair in zip(reversed(range(NEAR, half)), [3, 2, 1] + [None] * half) for m in pair if m]
    between = [("xw", m) for m in range(1, NEAR)] + [("vz", m) for m in range(1, lax.axis_size("row"))]
    between += [("child", m) for m in local]
    gaps = len(crossing) - 2
    spots, xw, vz = {}, [], []
    for n, m in enumerate(crossing):
        for i, (kind, other) in enumerate(between):
            if n == 2 + i * gaps // len(between):
                if kind == "child":
                    if other == local[-3]:
                        given = [line] + [sender.arrived[i] for i in xw], [both] + [sender.arrived[i] for i in vz]
                        *ready, staged = factors(front, dinv, pivots, rank_rows, rank_cols, admissible, *given)
                        ready, staged, pieces[other] = lax.optimization_barrier((ready, staged, pieces[other]))
                    spots[other] = sender.send(pieces[other], GROUP, other)
                elif kind == "xw":
                    if not xw:
                        line = jnp.stack([mine] + [sender.arrived[i] for i in line])
                    xw.append(sender.send(line, GROUP, other))
                else:
                    if not vz:
                        both = jnp.concatenate([v_fac, z_fac], axis=0)
                    vz.append(sender.send(both, ("row",), other))
        spots[m] = sender.send(pieces[m], GROUP, m)
    got = [pieces[0]] + [sender.arrived[spots[m]] for m in range(1, devices)]
    return finish(staged, *ready, got, row_map, tile)


def solution(mesh):
    return jax.shard_map(
        on_device,
        mesh=mesh,
        in_specs=(
            P("row", GROUP),
            P(("row", "col", "leaf"), None),
            P("row", None),
            P(),
            P("row", GROUP),
            P("row", GROUP),
            P(GROUP, "row"),
            P(GROUP, "row"),
            P(),
            P(),
            P("row"),
            P(GROUP),
            P("row", GROUP),
        ),
        out_specs=P("row", GROUP),
        check_vma=False,
    )
```

```python
import functools

import jax
import jax.numpy as jnp
import numpy as np
from jax import lax
from jax.experimental import pallas as pl
from jax.experimental.pallas import tpu as pltpu
from jax.sharding import PartitionSpec as P

RMAX = 64
LANES = 128
NEAR = 4
WINDOW = 5
GROUP = ("col", "leaf")
HIGHEST = lax.Precision.HIGHEST
MIB = 1 << 20


def group_index():
    return lax.axis_index("col") * lax.axis_size("leaf") + lax.axis_index("leaf")


def in_hbm(array):
    return pltpu.with_memory_space_constraint(array, pltpu.HBM)


def place_kernel(members, tiles, tile, col_tiles, col_map, child, *rest):
    pieces = rest[: len(members)]
    inverse, held, in_sem, out_sem = rest[len(members) :]
    me = group_index()

    def fetch(n, j):
        b = inverse[(me ^ members[n]) * col_tiles + j]
        span = pl.ds(pl.multiple_of(b * tile, tile), tile)
        return pltpu.make_async_copy(child.at[:, span], held.at[n, j], in_sem.at[n, j])

    def store(n):
        return pltpu.make_async_copy(held.at[n], pieces[n], out_sem.at[n])

    for b in range(tiles):
        inverse[col_map[b]] = b
    for n in range(len(members)):
        for j in range(col_tiles):
            fetch(n, j).start()
    for n in range(len(members)):
        for j in range(col_tiles):
            fetch(n, j).wait()
        store(n).start()
    for n in range(len(members)):
        store(n).wait()


def in_vmem(array):
    return pltpu.with_memory_space_constraint(array, pltpu.VMEM)


def place(child, col_map, tile, devices, members):
    rows = child.shape[0]
    tiles = col_map.shape[0]
    col_tiles = tiles // devices
    count = len(members)
    pieces = pl.pallas_call(
        functools.partial(place_kernel, members, tiles, tile, col_tiles),
        out_shape=[pltpu.HBM((col_tiles, rows, tile), child.dtype)] * count,
        in_specs=[pl.BlockSpec(memory_space=pltpu.SMEM), pl.BlockSpec(memory_space=pltpu.HBM)],
        out_specs=[pl.BlockSpec(memory_space=pltpu.HBM)] * count,
        scratch_shapes=[
            pltpu.SMEM((tiles,), jnp.int32),
            pltpu.VMEM((count, col_tiles, rows, tile), child.dtype),
            pltpu.SemaphoreType.DMA((count, col_tiles)),
            pltpu.SemaphoreType.DMA((count,)),
        ],
        compiler_params=pltpu.CompilerParams(vmem_limit_bytes=8 * MIB),
        cost_estimate=pl.CostEstimate(flops=0, bytes_accessed=8 * count * col_tiles * rows * tile, transcendentals=0),
        name="place_child",
    )(in_hbm(col_map), in_hbm(child))
    return dict(zip(members, pieces))


def dot(a, b, contract=((1,), (0,))):
    return lax.dot_general(a, b, (contract, ((), ())), precision=HIGHEST, preferred_element_type=jnp.float32)


def log2(size):
    return size.bit_length() - 1


def factor_kernel(parts, halves, col_tiles, row_tiles, front, dinv, pivots, rank_rows, rank_cols, admissible, *rest):
    xw = rest[:parts]
    vz = rest[parts : parts + halves]
    left, right, staged, ws, vs, zs, sem = rest[parts + halves :]
    stage = pltpu.make_async_copy(front, staged, sem)
    stage.start()
    tile = dinv.shape[0]
    per = xw[0].shape[2] // tile
    chunk = vz[0].shape[1] // tile
    slots = xw[0].shape[0]
    rows = slots * row_tiles

    zs[...] = jnp.zeros_like(zs)
    for h in range(halves):
        for j in range(col_tiles):
            for p in range(chunk):
                at = pl.ds(j * RMAX + h * chunk + p, 1)
                span = pl.ds(p * tile, tile)
                vs[at, :] = vz[h][pl.ds(j, 1), span]
                zs[at, pl.ds(j * tile, tile)] = vz[h][pl.ds(col_tiles + j, 1), span]
    for q in range(per):
        for n in range(parts):
            at = pl.ds((q * parts + n) * rows, rows)
            span = pl.ds(q * tile, tile)
            mine = xw[n][:, :row_tiles, span].reshape(rows, tile)
            for g in range(tile // LANES):
                left[g, at, :] = mine[:, g * LANES : (g + 1) * LANES]
            ws[at, :] = xw[n][:, row_tiles:, span].reshape(rows, tile)

    hot = (lax.broadcasted_iota(jnp.int32, (tile, tile), 0) == pivots[...]).astype(jnp.float32)
    dv = dot(dot(hot, dinv[...]), vs[...], ((1,), (1,)))
    core = dot(ws[...], dv)

    row = lax.broadcasted_iota(jnp.int32, (row_tiles, col_tiles * RMAX), 0)
    lane = lax.broadcasted_iota(jnp.int32, (row_tiles, col_tiles * RMAX), 1)
    top_r, top_s = jnp.zeros_like(row), jnp.zeros_like(row)
    for i in range(row_tiles):
        for j in range(col_tiles):
            here = (row == i) & (lane >> log2(RMAX) == j)
            dense = admissible[i, j] == 0
            top_r = jnp.where(here, jnp.where(dense, RMAX, rank_rows[i]), top_r)
            top_s = jnp.where(here, jnp.where(dense, RMAX, rank_cols[j]), top_s)
    half = (lane & (RMAX - 1)) >> log2(chunk)
    s = ((lax.axis_index("row") ^ half) << log2(chunk)) + (lane & (chunk - 1))
    top_r = jnp.where(s < top_s, top_r, 0)
    top_r = jnp.broadcast_to(top_r[None], (RMAX,) + top_r.shape).reshape(core.shape)
    k = lax.broadcasted_iota(jnp.int32, core.shape, 0)
    source = ((k >> log2(row_tiles)) & (slots - 1)) * parts + ((k >> log2(rows)) & (parts - 1))
    r = (group_index() ^ source) * per + (k >> log2(rows * parts))
    product = dot(jnp.where(r < top_r, core, 0.0), zs[...])
    for g in range(right.shape[0]):
        right[g, :, :] = product[:, g * LANES : (g + 1) * LANES]
    stage.wait()


def factors(front, dinv, pivots, rank_rows, rank_cols, admissible, xw, vz):
    tile = dinv.shape[0]
    row_tiles, col_tiles = admissible.shape
    total = RMAX * row_tiles
    inner = pl.BlockSpec(memory_space=pltpu.VMEM)
    scalars = pl.BlockSpec(memory_space=pltpu.SMEM)
    return pl.pallas_call(
        functools.partial(factor_kernel, len(xw), len(vz), col_tiles, row_tiles),
        out_shape=[
            pltpu.VMEM((tile // LANES, total, LANES), jnp.float32),
            pltpu.VMEM((col_tiles * tile // LANES, total, LANES), jnp.float32),
            pltpu.VMEM(front.shape, front.dtype),
        ],
        in_specs=[pl.BlockSpec(memory_space=pltpu.HBM)] + [inner] * 2 + [scalars] * 3 + [inner] * (len(xw) + len(vz)),
        out_specs=[inner] * 3,
        scratch_shapes=[
            pltpu.VMEM((total, tile), jnp.float32),
            pltpu.VMEM((col_tiles * RMAX, tile), jnp.float32),
            pltpu.VMEM((col_tiles * RMAX, col_tiles * tile), jnp.float32),
            pltpu.SemaphoreType.DMA,
        ],
        compiler_params=pltpu.CompilerParams(vmem_limit_bytes=12 * MIB),
        cost_estimate=pl.CostEstimate(flops=2 * total * tile * tile, bytes_accessed=16 * total * tile, transcendentals=0),
        name="update_factors",
    )(in_hbm(front), dinv, pivots.reshape(1, tile), rank_rows, rank_cols, admissible, *[in_hbm(array) for array in (*xw, *vz)])


def halves_of(array):
    high = array.astype(jnp.bfloat16)
    return high, (array - high.astype(jnp.float32)).astype(jnp.bfloat16)


def finish_kernel(count, tile, row_map, front, left, right, *rest):
    own, out, held, kept, out_sem, own_sem = rest[count - 1 :]
    pieces = (kept, *rest[: count - 1])
    me = group_index()
    col_tiles, rows, _ = kept.shape
    per_tile = tile // rows
    groups = count // per_tile

    def target(g):
        return row_map[0, lax.div(me ^ (g * per_tile), per_tile)]

    def at(g):
        return pl.ds(pl.multiple_of(target(g) * tile, tile), tile)

    def store(g):
        return pltpu.make_async_copy(held.at[g], out.at[at(g), :], out_sem.at[g])

    fetch_own = pltpu.make_async_copy(own, kept, own_sem)
    fetch_own.start()
    for g in reversed(range(groups)):
        mine = pl.ds(target(g), RMAX, stride=left.shape[1] // RMAX)
        a, b = halves_of(jnp.concatenate([left[n, mine, :] for n in range(left.shape[0])], axis=1))
        c, d = halves_of(jnp.concatenate([right[n, mine, :] for n in range(right.shape[0])], axis=1))
        update = lax.dot_general(
            jnp.concatenate([a, a, b, b], axis=0),
            jnp.concatenate([c, d, c, d], axis=0),
            (((0,), (0,)), ((), ())),
            preferred_element_type=jnp.float32,
        )
        held[g] = front[at(g), :] - update
        for p in range(per_tile):
            m = g * per_tile + p
            if m == 0:
                fetch_own.wait()
            low = pl.ds(pl.multiple_of(lax.rem(me ^ m, per_tile) * rows, rows), rows)
            for j in range(col_tiles):
                span = pl.ds(j * tile, tile)
                held[g, low, span] = held[g, low, span] + pieces[m][j]
        store(g).start()
    for g in range(groups):
        store(g).wait()


def finish(front, left, right, pieces, row_map, tile):
    row_tiles = front.shape[0] // tile
    inner = pl.BlockSpec(memory_space=pltpu.VMEM)
    outer = pl.BlockSpec(memory_space=pltpu.HBM)
    return pl.pallas_call(
        functools.partial(finish_kernel, len(pieces), tile),
        out_shape=pltpu.HBM(front.shape, front.dtype),
        in_specs=[pl.BlockSpec(memory_space=pltpu.SMEM)] + [inner] * (2 + len(pieces)) + [outer],
        out_specs=outer,
        scratch_shapes=[
            pltpu.VMEM((row_tiles, tile, front.shape[1]), front.dtype),
            pltpu.VMEM(pieces[0].shape, front.dtype),
            pltpu.SemaphoreType.DMA((row_tiles,)),
            pltpu.SemaphoreType.DMA,
        ],
        compiler_params=pltpu.CompilerParams(vmem_limit_bytes=8 * MIB),
        cost_estimate=pl.CostEstimate(flops=2 * front.size * 256, bytes_accessed=3 * front.size * 4, transcendentals=0),
        name="finish",
    )(
        in_hbm(row_map), in_vmem(front), in_vmem(left), in_vmem(right), *[in_vmem(piece) for piece in pieces[1:]], in_hbm(pieces[0])
    )


class Sender:
    def __init__(self):
        self.arrived = []

    def send(self, array, axes, m):
        spot = len(self.arrived) - WINDOW
        if spot >= 0:
            array, self.arrived[spot] = lax.optimization_barrier((array, self.arrived[spot]))
        size = int(np.prod([lax.axis_size(axis) for axis in axes]))
        self.arrived.append(lax.ppermute(array, axes, [(d, d ^ m) for d in range(size)]))
        return len(self.arrived) - 1


def on_device(
    front,
    child,
    row_map,
    col_map,
    x_fac,
    w_fac,
    v_fac,
    z_fac,
    dinv,
    pivots,
    rank_rows,
    rank_cols,
    admissible,
):
    tile = dinv.shape[0]
    row_tiles = front.shape[0] // tile
    col_tiles = front.shape[1] // tile
    devices = lax.axis_size("col") * lax.axis_size("leaf")

    sender = Sender()
    mine = jnp.pad(x_fac, ((0, row_tiles), (0, 0))) + jnp.pad(w_fac, ((row_tiles, 0), (0, 0)))
    mine, child = lax.optimization_barrier((mine, child))
    line = [sender.send(mine, GROUP, m) for m in range(NEAR, devices, NEAR)]
    early = [devices - 1, devices - 2]
    pieces = place(child, col_map, tile, devices, early)
    pieces, child, v_fac, z_fac = lax.optimization_barrier((pieces, child, v_fac, z_fac))
    pieces.update(place(child, col_map, tile, devices, list(reversed(range(devices - 2)))))
    half = devices // 2
    crossing = list(reversed(range(half, devices)))
    local = [m for pair in zip(reversed(range(NEAR, half)), [3, 2, 1] + [None] * half) for m in pair if m]
    between = [("xw", m) for m in range(1, NEAR)] + [("vz", m) for m in range(1, lax.axis_size("row"))]
    between += [("child", m) for m in local]
    gaps = len(crossing) - 2
    spots, xw, vz = {}, [], []
    for n, m in enumerate(crossing):
        for i, (kind, other) in enumerate(between):
            if n == 2 + i * gaps // len(between):
                if kind == "child":
                    if other == local[-3]:
                        given = [line] + [sender.arrived[i] for i in xw], [both] + [sender.arrived[i] for i in vz]
                        *ready, staged = factors(front, dinv, pivots, rank_rows, rank_cols, admissible, *given)
                        ready, staged, pieces[other] = lax.optimization_barrier((ready, staged, pieces[other]))
                    spots[other] = sender.send(pieces[other], GROUP, other)
                elif kind == "xw":
                    if not xw:
                        line = jnp.stack([mine] + [sender.arrived[i] for i in line])
                    xw.append(sender.send(line, GROUP, other))
                else:
                    if not vz:
                        both = jnp.concatenate([v_fac, z_fac], axis=0)
                    vz.append(sender.send(both, ("row",), other))
        spots[m] = sender.send(pieces[m], GROUP, m)
    got = [pieces[0]] + [sender.arrived[spots[m]] for m in range(1, devices)]
    return finish(staged, *ready, got, row_map, tile)


def solution(mesh):
    return jax.shard_map(
        on_device,
        mesh=mesh,
        in_specs=(
            P("row", GROUP),
            P(("row", "col", "leaf"), None),
            P("row", None),
            P(),
            P("row", GROUP),
            P("row", GROUP),
            P(GROUP, "row"),
            P(GROUP, "row"),
            P(),
            P(),
            P("row"),
            P(GROUP),
            P("row", GROUP),
        ),
        out_specs=P("row", GROUP),
        check_vma=False,
    )
```
